32 devices in a mesh: groups: 2 (over x), long: 16 (over z, y, core).
Axes of the slice: x: 2, y: 2, z: 4, core: 2. Of those that a mesh axis runs over, the one named last changes fastest.
Arguments:
- displacement: float32 [4, 2, 128, 16, 256], P('groups', None, 'long'), parts along dimension 0, may hold values from -6 to 6
- velocity: float32 [4, 2, 128, 16, 256], P('groups', None, 'long'), parts along dimension 0, may hold values from -4 to 4
- damage: float32 [4, 128, 16, 256], P('groups', 'long'), parts along dimension 0, may hold values from 0 to 0.6
- material: int32 [4, 128, 16, 256], P('groups', 'long'), parts along dimension 0, may hold values from 0 to 3
- damage_table: float32 [2, 4], replicated, may hold values from 0.1 to 2
- fault_rows: int32 [4, 128, 16], P('groups', 'long'), parts along dimension 0, may hold values from 0 to 3
- kernel: float32 [16, 64, 2, 2], P(None, 'long'), may hold values from -1.5 to 1.5
- history: float32 [30, 64, 2, 2, 16], P('groups', 'long'), parts along dimension 0, may hold values from -6 to 6
Outputs:
- displacement_out: float32 [4, 2, 128, 16, 256], P('groups', None, 'long'), parts along dimension 0
- velocity_out: float32 [4, 2, 128, 16, 256], P('groups', None, 'long'), parts along dimension 0
- damage_out: float32 [4, 128, 16, 256], P('groups', 'long'), parts along dimension 0
- history_out: float32 [30, 64, 2, 2, 16], P('groups', 'long'), parts along dimension 0
The draws below stay inside these ranges and needn't reach their ends.
There are 2 independent parts, one for each index of `groups`. The reference program is written for one: setup_inputs(seed, part) draws one part's arguments, and reference() takes and returns one part's arrays. A program takes and returns all parts, laid end to end along the dimension named above; an argument that names none is the same for every part. Nothing has to cross between parts.
Inputs may be any that keep to these rules, and one draw needn't show every extreme that they name: `fault_rows`: row of the fault face, counted from the fault.
All inputs are finite; a program needn't handle non-finite values.
Results may differ from the reference program's by a relative error of at most 0.00011.
Values sent between devices are 32-bit elements; how exact they have to be, the bound alone decides.
No kernel may reach another device: no remote copies, remote signals or barrier semaphores. Data moves between devices by JAX's collectives and lax.ppermute only.
A program may use at most 64 MiB of HBM per device.

```python
import math
import jax
import jax.numpy as jnp
from jax import lax

NY = 256
NZ = 16
COMP = 2
LAGS = 16
STEPS = 2
NCLASS = 4
FACE_ROWS = 4
NX = 128
K = 64


def touch_ends(drawn, own_key, smallest, high):
    shape = drawn.shape
    place = [jax.random.randint(jax.random.fold_in(own_key, axis), (), 0, shape[axis]) for axis in range(len(shape))]
    drawn = drawn.at[tuple(place)].set(smallest)
    longest = shape.index(max(shape))
    place[longest] = (place[longest] + 1) % shape[longest]
    return drawn.at[tuple(place)].set(high)


def levels(rng, dims, split, least, top_value):
    loudness = 1.0
    for dim, shards_of in split:
        steps = jax.random.uniform(jax.random.fold_in(jax.random.fold_in(rng, 6), dim), (shards_of,), jnp.float32, least / len(split), top_value / len(split))
        loudness = loudness * jnp.repeat(jnp.exp(steps), dims[dim] // shards_of).reshape((-1,) + (1,) * (len(dims) - 1 - dim))
    return loudness


def bell_draw(stream_key, dims, deviation, bound, pieces=(), kind=jnp.bfloat16):
    values = deviation * jax.random.normal(stream_key, dims, jnp.float32)
    if pieces:
        values = values * levels(stream_key, dims, pieces, -0.22, 0.18)
    return jnp.clip(values, -bound, bound).astype(kind)


def setup_inputs(seed: int = 0, part: int = 0) -> dict:
    key_of = jax.random.split(jax.random.key(seed), 9)
    own_keys = jax.random.split(jax.random.fold_in(key_of[8], part), 9)
    return {
        "displacement": bell_draw(own_keys[0], (COMP, 2, NX, NZ, NY), 1.0, 6.0, ((2, 16),), jnp.float32),
        "velocity": bell_draw(own_keys[1], (COMP, 2, NX, NZ, NY), 0.5, 4.0, ((2, 16),), jnp.float32),
        "damage": jnp.clip(0.6 * jax.random.uniform(own_keys[2], (2, NX, NZ, NY), jnp.float32) ** levels(own_keys[2], (2, NX, NZ, NY), ((1, 16),), -0.2, 0.2), 0.0, 0.6),
        "material": touch_ends(jax.random.randint(own_keys[3], (2, NX, NZ, NY), 0, NCLASS), jax.random.fold_in(own_keys[3], 1), 0, NCLASS - 1).astype(jnp.int32),
        "damage_table": jnp.clip(jnp.exp(jax.random.uniform(key_of[4], (2, NCLASS), jnp.float32, math.log(0.1), math.log(2.0))), 0.1, 2.0),
        "fault_rows": touch_ends(jax.random.randint(own_keys[5], (2, NX, NZ), 0, FACE_ROWS), jax.random.fold_in(own_keys[5], 1), 0, FACE_ROWS - 1).astype(jnp.int32),
        "kernel": bell_draw(key_of[6], (LAGS, K, 2, COMP), LAGS ** -0.5, 1.5, ((1, 16),), jnp.float32),
        "history": bell_draw(own_keys[7], (LAGS - 1, K, 2, COMP, NZ), 1.0, 6.0, ((1, 16),), jnp.float32),
    }


time_step = 0.5


def class_lookup(material, table_row):
    result = jnp.zeros(material.shape, table_row.dtype)
    for level in range(table_row.shape[0]):
        result = result + jnp.where(material == level, table_row[level], jnp.zeros((), table_row.dtype))
    return result


def wrap_length(values_in, axis):
    count = values_in.shape[axis]
    last_one = lax.slice_in_dim(values_in, count - 1, count, axis=axis)
    first_one = lax.slice_in_dim(values_in, 0, 1, axis=axis)
    return jnp.concatenate([last_one, values_in, first_one], axis)


def neighbour(values_in, axis, higher):
    selector = [slice(None)] * values_in.ndim
    for dimension in range(values_in.ndim - 3, values_in.ndim):
        selector[dimension] = slice(1, -1)
    selector[axis] = slice(2, None) if higher else slice(0, -2)
    return values_in[tuple(selector)]


def local_terms(padded_u, padded_c):
    outer_u = jnp.pad(padded_u, ((0, 0), (0, 0), (0, 0), (1, 1), (1, 1)))
    outer_c = jnp.pad(padded_c, ((0, 0), (0, 0), (1, 1), (1, 1)), mode="edge")
    centre_u = outer_u[:, :, 1:-1, 1:-1, 1:-1]
    centre_c = outer_c[:, 1:-1, 1:-1, 1:-1]
    forces = jnp.zeros_like(centre_u)
    energy = jnp.zeros_like(centre_c)
    for offset in range(3):
        above_u = neighbour(outer_u, 2 + offset, True)
        below_u = neighbour(outer_u, 2 + offset, False)
        above_c = neighbour(outer_c, 1 + offset, True)
        below_c = neighbour(outer_c, 1 + offset, False)
        forces = forces + (0.5 * (centre_c + above_c))[None] * (above_u - centre_u)
        forces = forces + (0.5 * (centre_c + below_c))[None] * (below_u - centre_u)
        gradient = 0.5 * (above_u - below_u)
        energy = energy + jnp.sum(gradient * gradient, axis=0)
    return forces, energy


def convolve(kernel, stacked):
    kernel_real = kernel[:, :, 0, :, None]
    kernel_imag = kernel[:, :, 1, :, None]
    spec_real = stacked[:, :, 0]
    spec_imag = stacked[:, :, 1]
    out_real = jnp.sum(kernel_real * spec_real - kernel_imag * spec_imag, axis=0)
    out_imag = jnp.sum(kernel_real * spec_imag + kernel_imag * spec_real, axis=0)
    return out_real, out_imag


def reference(displacement, velocity, damage, material, damage_table, fault_rows, kernel, history):
    rates = class_lookup(material, damage_table[0])
    limits = class_lookup(material, damage_table[1])
    heights = lax.broadcasted_iota(jnp.int32, damage.shape, 3)
    on_fault = (heights == fault_rows[..., None]).astype(displacement.dtype)
    signs = jnp.array([1.0, -1.0], displacement.dtype)[:, None, None, None]
    lagged = [history[level] for level in range(LAGS - 1)]
    for number in range(STEPS):
        stiffness = 1.0 - damage
        forces, energy = local_terms(wrap_length(displacement, 2), wrap_length(stiffness, 1))
        face = jnp.sum(displacement * on_fault[None], axis=4)
        slip = face[:, 1] - face[:, 0]
        spectrum = jnp.fft.rfft(slip, axis=1, norm="ortho")[:, :K]
        current = jnp.transpose(jnp.stack([jnp.real(spectrum), jnp.imag(spectrum)], 0), (2, 0, 1, 3))
        stacked = jnp.stack([current] + lagged, 0)
        traction_real, traction_imag = convolve(kernel, stacked)
        complete = lax.complex(traction_real, traction_imag)
        complete = jnp.concatenate([complete, jnp.zeros_like(complete[:1])], 0)
        traction = jnp.transpose(jnp.fft.irfft(complete, n=NX, axis=0, norm="ortho"), (1, 0, 2))
        pushes = traction[:, None, :, :, None] * signs[None] * on_fault[None]
        velocity = velocity + time_step * (forces + pushes)
        displacement = displacement + time_step * velocity
        damage = 1.0 - (1.0 - damage) * jnp.exp(-rates * jax.nn.softplus(energy - limits))
        lagged = [current] + lagged[:-1]
    return displacement, velocity, damage, jnp.stack(lagged, 0)
```

```python
import functools
import math

import jax
import jax.numpy as jnp
import numpy as np
from jax import lax
from jax.experimental import pallas as pl
from jax.experimental.pallas import tpu as pltpu
from jax.sharding import PartitionSpec as P

DT = 0.5
EXACT = lax.Precision.HIGHEST
LANES = 128
GROUP = 8
OWNED = GROUP // 2
HALO_PLANES = 18


def table_of(length):
    lane = np.arange(length)
    wave = (lane // GROUP) * OWNED + lane % OWNED
    imag = (lane % GROUP) // OWNED
    phase = (np.arange(length)[:, None] * wave[None]) % length * (2.0 * np.pi / length)
    table = np.where(imag[None] == 1, -np.sin(phase), np.cos(phase)) / math.sqrt(length)
    return table.astype(np.float32)


def iota(shape, axis):
    return lax.broadcasted_iota(jnp.int32, shape, axis)


def up_z(a, fill):
    n = a.shape[0]
    return jnp.where(iota(a.shape, 0) == n - 1, fill, pltpu.roll(a, n - 1, 0))


def down_z(a, fill):
    return jnp.where(iota(a.shape, 0) == 0, fill, pltpu.roll(a, 1, 0))


def up_r(a, fill):
    n = a.shape[1]
    return jnp.where(iota(a.shape, 1) == n - 1, fill, pltpu.roll(a, n - 1, 1))


def down_r(a, fill):
    return jnp.where(iota(a.shape, 1) == 0, fill, pltpu.roll(a, 1, 1))


def fault_columns(rows_ref):
    rows = rows_ref[...].astype(jnp.float32).reshape(2 * GROUP, -1)
    nz = rows.shape[1]
    eye = (iota((nz, nz), 0) == iota((nz, nz), 1)).astype(jnp.float32)
    return lax.dot_general(eye, rows, (((1,), (1,)), ((), ())), preferred_element_type=jnp.float32)


def on_fault_plane(columns, s, x):
    nz = columns.shape[0]
    column = columns[:, s * GROUP + x : s * GROUP + x + 1]
    return jnp.broadcast_to(column, (nz, LANES)) == iota((nz, LANES), 1).astype(jnp.float32)


def pack_kernel(u_ref, v_ref, d_ref, rows_ref, kern_ref, hist_ref, out_ref):
    nz = u_ref.shape[3]
    lane = iota((nz, LANES), 1)
    columns = fault_columns(rows_ref)
    out = jnp.zeros((nz, LANES), jnp.float32)
    zero = jnp.zeros((nz, LANES), jnp.float32)
    for x in range(GROUP):
        slip = [zero, zero]
        ahead = [zero, zero]
        for s in range(2):
            fault = on_fault_plane(columns, s, x)
            c0 = 1.0 - d_ref[s, x]
            bars = []
            if x > 0:
                bars.append((x - 1, 0.5 * (c0 + (1.0 - d_ref[s, x - 1]))))
            if x < GROUP - 1:
                bars.append((x + 1, 0.5 * (c0 + (1.0 - d_ref[s, x + 1]))))
            bar_zu = 0.5 * (c0 + up_z(c0, c0))
            bar_zd = 0.5 * (c0 + down_z(c0, c0))
            bar_ru = 0.5 * (c0 + up_r(c0, c0))
            bar_rd = 0.5 * (c0 + down_r(c0, c0))
            for c in range(2):
                u0 = u_ref[c, s, x]
                force = bar_zu * (up_z(u0, 0.0) - u0) + bar_zd * (down_z(u0, 0.0) - u0)
                force += bar_ru * (up_r(u0, 0.0) - u0) + bar_rd * (down_r(u0, 0.0) - u0)
                for other, bar in bars:
                    force += bar * (u_ref[c, s, other] - u0)
                later = u0 + DT * (v_ref[c, s, x] + DT * force)
                sign = 1.0 if s == 1 else -1.0
                slip[c] += jnp.where(fault, sign * u0, 0.0)
                ahead[c] += jnp.where(fault, sign * later, 0.0)
            if x in (0, GROUP - 1):
                side = 0 if x == 0 else 1
                for c in range(2):
                    at = side * 16 + s * 8 + c * 4
                    here = (lane >= at) & (lane < at + 4)
                    for which, plane in ((0, u_ref[c, s, x]), (32, c0), (64, fault.astype(jnp.float32))):
                        spot = (lane >= which + at) & (lane < which + at + 4)
                        moved = plane if which + at == 0 else pltpu.roll(plane, which + at, 1)
                        out = jnp.where(spot, moved, out)
        for c in range(2):
            out = jnp.where(lane == 96 + c * GROUP + x, jnp.sum(slip[c], 1, keepdims=True), out)
            out = jnp.where(lane == 112 + c * GROUP + x, jnp.sum(ahead[c], 1, keepdims=True), out)
    out_ref[0:nz, :] = out

    kern = kern_ref[...]
    count = kern.shape[0]
    real_row = (iota(kern.shape, 0) // 2) % 2 == 0
    from_next = pltpu.roll(kern, count - 2, 0)
    a_rows = jnp.where(real_row, kern, pltpu.roll(kern, 2, 0))
    b_rows = jnp.where(real_row, -from_next, kern)
    b_source = jnp.where(real_row, from_next, -kern)
    parts = []
    lags = hist_ref.shape[0] + 1
    for skip in (1, 2):
        straight = jnp.zeros((count, nz), jnp.float32)
        crossed = jnp.zeros((count, nz), jnp.float32)
        for l in range(skip, lags):
            straight += a_rows[:, l : l + 1] * hist_ref[l - skip]
            crossed += b_source[:, l : l + 1] * hist_ref[l - skip]
        real_here = (iota((count, nz), 0) // 2) % 2 == 0
        swapped = jnp.where(real_here, pltpu.roll(crossed, count - 2, 0), pltpu.roll(crossed, 2, 0))
        parts.append(straight + swapped)
    for l in (0, 1):
        parts.append(jnp.broadcast_to(a_rows[:, l : l + 1], (count, nz)))
        parts.append(jnp.broadcast_to(b_rows[:, l : l + 1], (count, nz)))
    stacked = jnp.concatenate(parts, 0)
    total = stacked.shape[0]
    row = iota((total, LANES), 0)
    target = (row // 16) * 16 + (row % 2) * GROUP + ((row // 2) % 2) * OWNED + (row // 4) % OWNED
    place = (target == iota((total, LANES), 1)).astype(jnp.float32)
    out_ref[nz : 2 * nz, :] = lax.dot_general(
        stacked, place, (((0,), (0,)), ((), ())), precision=EXACT, preferred_element_type=jnp.float32
    )


def swap_parts(a):
    n = a.shape[1]
    return jnp.where(
        iota(a.shape, 1) % GROUP < OWNED, pltpu.roll(a, n - OWNED, 1), pltpu.roll(a, OWNED, 1)
    )


def spectral(n, pos, gathered, table_ref, near_ref, spread_ref, hist_out_ref):
    nz = gathered.shape[1] // 2
    length = n * GROUP
    lane = iota((nz, LANES), 1)
    for t in range(length // LANES):
        acc = [jnp.zeros((nz, LANES), jnp.float32) for _ in range(16)]
        for dd in range(LANES // GROUP):
            d = t * (LANES // GROUP) + dd
            first = gathered[d, 0:nz]
            second = gathered[d, nz : 2 * nz]
            spot = (lane >= dd * GROUP) & (lane < (dd + 1) * GROUP)
            for g in range(16):
                source, at = (first, 12 + g) if g < 4 else (second, g - 4)
                turn = ((dd - at) * GROUP) % LANES
                moved = source if turn == 0 else pltpu.roll(source, turn, 1)
                acc[g] = jnp.where(spot, moved, acc[g])
            following = gathered[(d + 1) % n, 0:nz]
            before = gathered[(d - 1) % n, 0:nz]
            strip_sign = jnp.where(lane < 8, -1.0, 1.0) * (DT * DT)
            own_right = pltpu.roll(first, LANES - 16, 1)
            bar = 0.5 * pltpu.roll(own_right + following, LANES - 32, 1)
            right = bar * (following - own_right) * pltpu.roll(own_right, LANES - 64, 1) * strip_sign
            prev_right = pltpu.roll(before, LANES - 16, 1)
            bar = 0.5 * pltpu.roll(prev_right + first, LANES - 32, 1)
            left = bar * (prev_right - first) * pltpu.roll(first, LANES - 64, 1) * strip_sign
            for c in range(2):
                mine = (lane < 16) & ((lane // 4) % 2 == c)
                for x, flux in ((0, left), (GROUP - 1, right)):
                    column = jnp.sum(jnp.where(mine, flux, 0.0), 1, keepdims=True)
                    acc[2 + c] = jnp.where(lane == dd * GROUP + x, acc[2 + c] + column, acc[2 + c])
        for g in range(16):
            spread_ref[g * nz : (g + 1) * nz, t * LANES : (t + 1) * LANES] = acc[g]
    both = 2 * nz
    spectra = jnp.dot(
        spread_ref[0 : 2 * both, :], table_ref[...], precision=EXACT, preferred_element_type=jnp.float32
    )
    first_now = spectra[0:both]
    hist1 = spread_ref[2 * both : 3 * both, :]
    hist2 = spread_ref[3 * both : 4 * both, :]
    k0r = spread_ref[4 * both : 5 * both, :]
    k0i = spread_ref[5 * both : 6 * both, :]
    k1r = spread_ref[6 * both : 7 * both, :]
    k1i = spread_ref[7 * both : 8 * both, :]
    swapped = swap_parts(first_now)
    traction1 = hist1 + k0r * first_now + k0i * swapped
    wide = iota((both, length), 1)
    kept = jnp.where(wide == OWNED, 0.0, traction1)
    second_now = spectra[both : 2 * both] - (2.0 * DT * DT) * kept
    traction2 = hist2 + k1r * first_now + k1i * swapped + k0r * second_now + k0i * swap_parts(second_now)
    weight = jnp.where((wide // GROUP == 0) & (wide % OWNED == 0), 1.0, 2.0)
    weighted = jnp.concatenate([weight * traction1, weight * traction2], 0)
    for i, owner in enumerate((lax.rem(pos + n - 1, n), pos, lax.rem(pos + 1, n))):
        near_ref[i * GROUP : (i + 1) * GROUP, :] = table_ref[
            pl.ds(pl.multiple_of(owner * GROUP, GROUP), GROUP), :
        ]
    tractions = lax.dot_general(
        weighted, near_ref[...], (((1,), (1,)), ((), ())), precision=EXACT, preferred_element_type=jnp.float32
    )
    rows = 2 * GROUP
    row = iota((rows, length), 0)
    target = pos * GROUP + ((row // 2) % 2) * OWNED + row // 4
    for step, now in ((1, first_now), (0, second_now)):
        total = jnp.zeros((rows, nz), jnp.float32)
        for c in range(2):
            pick = ((target == iota((rows, length), 1)) & (row % 2 == c)).astype(jnp.float32)
            total += lax.dot_general(
                pick, now[c * nz : (c + 1) * nz], (((1,), (1,)), ((), ())),
                precision=EXACT, preferred_element_type=jnp.float32,
            )
        hist_out_ref[step] = total
    return tractions


def stencil(u, c):
    (cm, c0, cp), quarter = c, None
    bars = (
        (0.5 * (c0 + cp), 0.5 * (c0 + cm)),
        (0.5 * (c0 + up_z(c0, c0)), 0.5 * (c0 + down_z(c0, c0))),
        (0.5 * (c0 + up_r(c0, c0)), 0.5 * (c0 + down_r(c0, c0))),
    )
    forces = []
    for um, u0, up in u:
        pairs = (
            (up - u0, u0 - um),
            (up_z(u0, 0.0) - u0, u0 - down_z(u0, 0.0)),
            (up_r(u0, 0.0) - u0, u0 - down_r(u0, 0.0)),
        )
        force = None
        for (above, below), (bar_up, bar_down) in zip(pairs, bars):
            term = bar_up * above - bar_down * below
            force = term if force is None else force + term
            gradient = above + below
            quarter = gradient * gradient if quarter is None else quarter + gradient * gradient
        forces.append(force)
    return forces, 0.25 * quarter


def decay(classes, table_ref, energy):
    rate = jnp.full(classes.shape, table_ref[0, 0])
    limit = jnp.full(classes.shape, table_ref[1, 0])
    for level in range(1, table_ref.shape[1]):
        here = classes == level
        rate = jnp.where(here, table_ref[0, level], rate)
        limit = jnp.where(here, table_ref[1, level], limit)
    over = energy - limit
    soft = jnp.maximum(over, 0.0) + jnp.log(1.0 + jnp.exp(-jnp.abs(over)))
    return jnp.exp(-rate * soft)


def steps_kernel(
    n, u_ref, v_ref, d_ref, mat_ref, tab_ref, rows_ref, left_ref, right_ref, gathered, hist_ref, table_ref,
    u_out, v_out, d_out, hist_out,
    ue, ve, de, mat, halo_mat, u1, c1, uo, vo, do, spread, near, push_t, fault_p, in_sem, out_sem,
):
    pos = lax.axis_index("long")
    nz = u_ref.shape[2]
    copies = []

    def copy(src, dst):
        i = len(copies)
        copies.append(pltpu.make_async_copy(src, dst, in_sem.at[i]))
        copies[-1].start()

    copy(u_ref, ue.at[:, pl.ds(2, GROUP)])
    copy(v_ref, ve.at[:, pl.ds(1, GROUP)])
    copy(d_ref, de.at[:, pl.ds(2, GROUP)])
    copy(mat_ref, mat)
    for halo, side in ((left_ref, 0), (right_ref, 1)):
        for k in range(2):
            at = k + side * (GROUP + 2)
            copy(halo.at[pl.ds(4 * k, 4)], ue.at[:, at])
            copy(halo.at[pl.ds(8 + 2 * k, 2)], de.at[:, at])
        copy(halo.at[pl.ds(12, 4)], ve.at[:, side * (GROUP + 1)])
        copy(halo.at[pl.ds(16, 2)], halo_mat.at[side])

    hist_out[2:] = hist_ref[: hist_ref.shape[0] - 2]
    tractions = spectral(n, pos, gathered, table_ref, near, spread, hist_out)
    for step in range(2):
        for c in range(2):
            at = (step * 2 + c) * nz
            for x in range(GROUP + 2):
                push_t[step * 2 + c, x] = jnp.broadcast_to(
                    tractions[at : at + nz, GROUP - 1 + x : GROUP + x], (nz, LANES)
                )
    columns = fault_columns(rows_ref)
    lane = iota((nz, LANES), 1)
    for s in range(2):
        for x in range(GROUP):
            fault_p[s, 1 + x] = on_fault_plane(columns, s, x).astype(jnp.float32)
        for x, owner, at in ((0, lax.rem(pos + n - 1, n), 80), (GROUP + 1, lax.rem(pos + 1, n), 64)):
            moved = pltpu.roll(gathered[owner, 0:nz], LANES - (at + s * 8), 1)
            fault_p[s, x] = jnp.where(lane < 4, moved, 0.0)
    for one in copies:
        one.wait()

    def first_step(x, classes_of):
        for s in range(2):
            c = [1.0 - de[s, x + k] for k in range(3)]
            u = [[ue[comp * 2 + s, x + k] for k in range(3)] for comp in range(2)]
            forces, energy = stencil(u, c)
            c1[s, x] = c[1] * decay(classes_of(s), tab_ref, energy)
            for comp in range(2):
                v_new = ve[comp * 2 + s, x] + DT * forces[comp]
                ve[comp * 2 + s, x] = v_new
                u1[comp * 2 + s, x] = u[comp][1] + DT * v_new
                push = (DT if s == 0 else -DT) * push_t[comp, x] * fault_p[s, x]
                ve[comp * 2 + s, x, :, 0:LANES] += push
                u1[comp * 2 + s, x, :, 0:LANES] += DT * push

    first_step(0, lambda s: halo_mat[0, s].astype(jnp.int32))
    first_step(GROUP + 1, lambda s: halo_mat[1, s].astype(jnp.int32))

    @pl.loop(0, GROUP)
    def _(x):
        first_step(x + 1, lambda s: mat[s, x])

    def outs(x):
        return (
            pltpu.make_async_copy(uo.at[:, x], u_out.at[:, x], out_sem.at[0, x]),
            pltpu.make_async_copy(vo.at[:, x], v_out.at[:, x], out_sem.at[1, x]),
            pltpu.make_async_copy(do.at[:, x], d_out.at[:, x], out_sem.at[2, x]),
        )

    @pl.loop(0, GROUP)
    def _(x):
        for s in range(2):
            c = [c1[s, x + k] for k in range(3)]
            u = [[u1[comp * 2 + s, x + k] for k in range(3)] for comp in range(2)]
            forces, energy = stencil(u, c)
            do[s, x] = 1.0 - c[1] * decay(mat[s, x], tab_ref, energy)
            for comp in range(2):
                v_new = ve[comp * 2 + s, x + 1] + DT * forces[comp]
                vo[comp * 2 + s, x] = v_new
                uo[comp * 2 + s, x] = u[comp][1] + DT * v_new
                push = (DT if s == 0 else -DT) * push_t[2 + comp, x + 1] * fault_p[s, x + 1]
                vo[comp * 2 + s, x, :, 0:LANES] += push
                uo[comp * 2 + s, x, :, 0:LANES] += DT * push
        for one in outs(x):
            one.start()

    @pl.loop(0, GROUP)
    def _(x):
        for one in outs(x):
            one.wait()


def per_device(n, displacement, velocity, damage, material, damage_table, fault_rows, kernel, history):
    comps, strips, cells, nz, ny = displacement.shape
    assert cells == GROUP and comps == 2 and strips == 2
    lags = kernel.shape[0]
    f32 = jnp.float32
    u = displacement.reshape(4, cells, nz, ny)
    v = velocity.reshape(4, cells, nz, ny)

    def send(first, second, inner):
        return jnp.concatenate(
            [u[:, first], u[:, second], damage[:, first], damage[:, second], v[:, inner],
             material[:, inner].astype(f32)], 0)

    ring = [(i, (i + 1) % n) for i in range(n)]
    left = lax.ppermute(send(cells - 2, cells - 1, cells - 1), "long", ring)
    right = lax.ppermute(send(0, 1, 0), "long", [(b, a) for a, b in ring])

    kern = jnp.transpose(kernel, (1, 2, 3, 0)).reshape(2 * GROUP, lags)
    hist = history.reshape(lags - 1, 2 * GROUP, nz)
    whole = pl.BlockSpec(memory_space=pltpu.VMEM)
    hbm = pl.BlockSpec(memory_space=pl.ANY)
    smem = pl.BlockSpec(memory_space=pltpu.SMEM)
    tile = lambda *lead: pl.BlockSpec((*lead, nz, LANES), lambda i: (0,) * (len(lead) + 2))
    full = lambda a: pl.BlockSpec(a.shape, lambda i: (0,) * a.ndim)
    block = pl.pallas_call(
        pack_kernel,
        grid=(1,),
        out_shape=jax.ShapeDtypeStruct((2 * nz, LANES), f32),
        in_specs=[tile(2, 2, cells), tile(2, 2, cells), tile(2, cells), full(fault_rows), full(kern), full(hist)],
        out_specs=pl.BlockSpec((2 * nz, LANES), lambda i: (0, 0)),
        compiler_params=pltpu.CompilerParams(vmem_limit_bytes=32 * 1024 * 1024),
    )(displacement, velocity, damage, fault_rows, kern, hist)

    gathered = lax.all_to_all(jnp.broadcast_to(block[None], (n, *block.shape)), "long", 0, 0)

    table = jnp.asarray(table_of(n * cells))
    scratch = lambda *lead: pltpu.VMEM((*lead, nz, ny), f32)
    u_new, v_new, d_new, hist_new = pl.pallas_call(
        functools.partial(steps_kernel, n),
        out_shape=(
            jax.ShapeDtypeStruct(u.shape, f32),
            jax.ShapeDtypeStruct(v.shape, f32),
            jax.ShapeDtypeStruct(damage.shape, f32),
            jax.ShapeDtypeStruct(hist.shape, f32),
        ),
        in_specs=[hbm, hbm, hbm, hbm, smem, whole, hbm, hbm, whole, whole, whole],
        out_specs=[hbm, hbm, hbm, whole],
        scratch_shapes=[
            scratch(4, cells + 4), scratch(4, cells + 2), scratch(2, cells + 4),
            pltpu.VMEM((2, cells, nz, ny), jnp.int32), scratch(2, 2),
            scratch(4, cells + 2), scratch(2, cells + 2),
            scratch(4, cells), scratch(4, cells), scratch(2, cells),
            pltpu.VMEM((16 * nz, n * cells), f32), pltpu.VMEM((3 * cells, n * cells), f32),
            pltpu.VMEM((4, cells + 2, nz, LANES), f32), pltpu.VMEM((2, cells + 2, nz, LANES), f32),
            pltpu.SemaphoreType.DMA((16,)), pltpu.SemaphoreType.DMA((3, cells)),
        ],
        compiler_params=pltpu.CompilerParams(vmem_limit_bytes=48 * 1024 * 1024),
    )(u, v, damage, material, damage_table, fault_rows, left, right, gathered, hist, table)
    return (
        u_new.reshape(displacement.shape),
        v_new.reshape(velocity.shape),
        d_new,
        hist_new.reshape(history.shape),
    )


def solution(mesh):
    placed = (
        P("groups", None, "long", None, None),
        P("groups", None, "long", None, None),
        P("groups", "long", None, None),
        P("groups", "long", None, None),
        P(),
        P("groups", "long", None),
        P(None, "long", None, None),
        P("groups", "long", None, None, None),
    )
    return jax.shard_map(
        functools.partial(per_device, mesh.shape["long"]),
        mesh=mesh,
        in_specs=placed,
        out_specs=(placed[0], placed[1], placed[2], placed[7]),
        check_vma=False,
    )
```

```python
import functools
import math

import jax
import jax.numpy as jnp
import numpy as np
from jax import lax
from jax.experimental import pallas as pl
from jax.experimental.pallas import tpu as pltpu
from jax.sharding import PartitionSpec as P

DT = 0.5
EXACT = lax.Precision.HIGHEST
LANES = 128
GROUP = 8
OWNED = GROUP // 2
HALO_PLANES = 18
SLOTS = GROUP + 2


def table_of(length):
    lane = np.arange(length)
    wave = (lane // GROUP) * OWNED + lane % OWNED
    imag = (lane % GROUP) // OWNED
    phase = (np.arange(length)[:, None] * wave[None]) % length * (2.0 * np.pi / length)
    table = np.where(imag[None] == 1, -np.sin(phase), np.cos(phase)) / math.sqrt(length)
    return table.astype(np.float32)


def iota(shape, axis):
    return lax.broadcasted_iota(jnp.int32, shape, axis)


def up_z(a, fill):
    n = a.shape[0]
    return jnp.where(iota(a.shape, 0) == n - 1, fill, pltpu.roll(a, n - 1, 0))


def down_z(a, fill):
    return jnp.where(iota(a.shape, 0) == 0, fill, pltpu.roll(a, 1, 0))


def up_r(a, fill):
    n = a.shape[1]
    return jnp.where(iota(a.shape, 1) == n - 1, fill, pltpu.roll(a, n - 1, 1))


def down_r(a, fill):
    return jnp.where(iota(a.shape, 1) == 0, fill, pltpu.roll(a, 1, 1))


def fault_columns(rows_ref):
    rows = rows_ref[...].astype(jnp.float32).reshape(2 * GROUP, -1)
    nz = rows.shape[1]
    eye = (iota((nz, nz), 0) == iota((nz, nz), 1)).astype(jnp.float32)
    return lax.dot_general(eye, rows, (((1,), (1,)), ((), ())), preferred_element_type=jnp.float32)


def on_fault_plane(columns, s, x):
    nz = columns.shape[0]
    column = columns[:, s * GROUP + x : s * GROUP + x + 1]
    return jnp.broadcast_to(column, (nz, LANES)) == iota((nz, LANES), 1).astype(jnp.float32)


class Copies:
    def __init__(self, sems):
        self.sems, self.made = sems, []

    def start(self, src, dst):
        one = pltpu.make_async_copy(src, dst, self.sems.at[len(self.made)])
        one.start()
        self.made.append(one)
        return one

    def wait(self):
        for one in self.made:
            one.wait()


def pack_kernel(
    n, u_hbm, v_hbm, d_hbm, mat_hbm, rows_hbm, kern_hbm, hist_hbm,
    out_ref, even_ref, odd_ref,
    ut, vt, dt, rows_ref, kern_ref, hist_ref, mat_ref, sems, halo_sems,
):
    nz = u_hbm.shape[2]
    loads, halos = Copies(sems), Copies(halo_sems)
    near = pl.ds(0, LANES)
    loads.start(u_hbm.at[:, :, :, near], ut)
    loads.start(d_hbm.at[:, :, :, near], dt)
    loads.start(rows_hbm, rows_ref)
    loads.start(v_hbm.at[:, :, :, near], vt)
    loads.start(kern_hbm, kern_ref)
    loads.start(hist_hbm, hist_ref)
    parity = lax.rem(lax.axis_index("long"), 2)
    for i, (ref, right) in enumerate(((even_ref, 1 - parity), (odd_ref, parity))):
        low, inner = right * (GROUP - 2), right * (GROUP - 1)
        for k in range(2):
            halos.start(u_hbm.at[:, low + k], ref.at[pl.ds(4 * k, 4)])
            halos.start(d_hbm.at[:, low + k], ref.at[pl.ds(8 + 2 * k, 2)])
        halos.start(v_hbm.at[:, inner], ref.at[pl.ds(12, 4)])
        halos.start(mat_hbm.at[:, inner], mat_ref.at[i])
    loads.wait()

    lane = iota((nz, LANES), 1)
    columns = fault_columns(rows_ref)
    out = jnp.zeros((nz, LANES), jnp.float32)
    edges = jnp.zeros((nz, LANES), jnp.float32)
    zero = jnp.zeros((nz, LANES), jnp.float32)
    for x in range(GROUP):
        slip = [zero, zero]
        ahead = [zero, zero]
        for s in range(2):
            fault = on_fault_plane(columns, s, x)
            c0 = 1.0 - dt[s, x]
            bars = []
            if x > 0:
                bars.append((x - 1, 0.5 * (c0 + (1.0 - dt[s, x - 1]))))
            if x < GROUP - 1:
                bars.append((x + 1, 0.5 * (c0 + (1.0 - dt[s, x + 1]))))
            bar_zu = 0.5 * (c0 + up_z(c0, c0))
            bar_zd = 0.5 * (c0 + down_z(c0, c0))
            bar_ru = 0.5 * (c0 + up_r(c0, c0))
            bar_rd = 0.5 * (c0 + down_r(c0, c0))
            for c in range(2):
                u0 = ut[c * 2 + s, x]
                force = bar_zu * (up_z(u0, 0.0) - u0) + bar_zd * (down_z(u0, 0.0) - u0)
                force += bar_ru * (up_r(u0, 0.0) - u0) + bar_rd * (down_r(u0, 0.0) - u0)
                for other, bar in bars:
                    force += bar * (ut[c * 2 + s, other] - u0)
                later = u0 + DT * (vt[c * 2 + s, x] + DT * force)
                sign = 1.0 if s == 1 else -1.0
                slip[c] += jnp.where(fault, sign * u0, 0.0)
                ahead[c] += jnp.where(fault, sign * later, 0.0)
            if x in (0, GROUP - 1):
                side = 0 if x == 0 else 1
                for c in range(2):
                    at = side * 16 + s * 8 + c * 4
                    for which, plane in ((0, ut[c * 2 + s, x]), (32, c0), (64, fault.astype(jnp.float32))):
                        spot = (lane >= which + at) & (lane < which + at + 4)
                        moved = plane if which + at == 0 else pltpu.roll(plane, which + at, 1)
                        edges = jnp.where(spot, moved, edges)
        for c in range(2):
            out = jnp.where(lane == c * GROUP + x, jnp.sum(slip[c], 1, keepdims=True), out)
            out = jnp.where(lane == 16 + c * GROUP + x, jnp.sum(ahead[c], 1, keepdims=True), out)

    kern = kern_ref[...]
    count = kern.shape[0]
    real_row = (iota(kern.shape, 0) // 2) % 2 == 0
    from_next = pltpu.roll(kern, count - 2, 0)
    a_rows = jnp.where(real_row, kern, pltpu.roll(kern, 2, 0))
    b_rows = jnp.where(real_row, -from_next, kern)
    b_source = jnp.where(real_row, from_next, -kern)
    parts = []
    lags = hist_ref.shape[0] + 1
    for skip in (1, 2):
        straight = jnp.zeros((count, nz), jnp.float32)
        crossed = jnp.zeros((count, nz), jnp.float32)
        for l in range(skip, lags):
            straight += a_rows[:, l : l + 1] * hist_ref[l - skip]
            crossed += b_source[:, l : l + 1] * hist_ref[l - skip]
        real_here = (iota((count, nz), 0) // 2) % 2 == 0
        swapped = jnp.where(real_here, pltpu.roll(crossed, count - 2, 0), pltpu.roll(crossed, 2, 0))
        parts.append(straight + swapped)
    for l in (0, 1):
        parts.append(jnp.broadcast_to(a_rows[:, l : l + 1], (count, nz)))
        parts.append(jnp.broadcast_to(b_rows[:, l : l + 1], (count, nz)))
    stacked = jnp.concatenate(parts, 0)
    total = stacked.shape[0]
    row = iota((total, LANES), 0)
    target = 32 + (row // 16) * 16 + (row % 2) * GROUP + ((row // 2) % 2) * OWNED + (row // 4) % OWNED
    place = (target == iota((total, LANES), 1)).astype(jnp.float32)
    out += lax.dot_general(
        stacked, place, (((0,), (0,)), ((), ())), precision=EXACT, preferred_element_type=jnp.float32
    )
    for d in range(n):
        out_ref[d, 0:nz, :] = out
        out_ref[d, nz : 2 * nz, :] = edges
    halos.wait()
    for i, ref in enumerate((even_ref, odd_ref)):
        ref[16:18] = mat_ref[i].astype(jnp.float32)


def stencil(u, c):
    (cm, c0, cp), quarter = c, None
    bars = (
        (0.5 * (c0 + cp), 0.5 * (c0 + cm)),
        (0.5 * (c0 + up_z(c0, c0)), 0.5 * (c0 + down_z(c0, c0))),
        (0.5 * (c0 + up_r(c0, c0)), 0.5 * (c0 + down_r(c0, c0))),
    )
    forces = []
    for um, u0, up in u:
        pairs = (
            (up - u0, u0 - um),
            (up_z(u0, 0.0) - u0, u0 - down_z(u0, 0.0)),
            (up_r(u0, 0.0) - u0, u0 - down_r(u0, 0.0)),
        )
        force = None
        for (above, below), (bar_up, bar_down) in zip(pairs, bars):
            term = bar_up * above - bar_down * below
            force = term if force is None else force + term
            gradient = above + below
            quarter = gradient * gradient if quarter is None else quarter + gradient * gradient
        forces.append(force)
    return forces, 0.25 * quarter


def classed(classes, table_ref):
    rate = jnp.full(classes.shape, table_ref[0, 0])
    limit = jnp.full(classes.shape, table_ref[1, 0])
    for level in range(1, table_ref.shape[1]):
        here = classes == level
        rate = jnp.where(here, table_ref[0, level], rate)
        limit = jnp.where(here, table_ref[1, level], limit)
    return rate, limit


def decay(rate, limit, energy):
    over = energy - limit
    soft = jnp.maximum(over, 0.0) + jnp.log(1.0 + jnp.exp(-jnp.abs(over)))
    return jnp.exp(-rate * soft)


PK_U, PK_C, PK_V, PK_RATE, PK_LIMIT, PK_FAULT, PK_COUNT = 0, 4, 6, 10, 12, 14, 16


def local_kernel(
    n, u_hbm, v_hbm, d_hbm, mat_hbm, tab_hbm, rows_hbm, even_hbm, odd_hbm, hist_hbm, table_hbm,
    u_out, v_out, d_out, hist_out, ut, vt, dt, packed, near, table_out,
    ue, ve, de, mat, halo_mat, tab_ref, rows_ref, u1, c1, uo, vo, do, in_sem, out_sem, misc_sem,
):
    pos = lax.axis_index("long")
    parity = lax.rem(pos, 2)
    nz = u_hbm.shape[2]
    loads, misc = Copies(in_sem), Copies(misc_sem)
    loads.start(u_hbm, ue.at[:, pl.ds(2, GROUP)])
    loads.start(v_hbm, ve.at[:, pl.ds(1, GROUP)])
    loads.start(d_hbm, de.at[:, pl.ds(2, GROUP)])
    loads.start(mat_hbm, mat)
    loads.start(tab_hbm, tab_ref)
    loads.start(rows_hbm, rows_ref)
    for halo, right in ((even_hbm, 1 - parity), (odd_hbm, parity)):
        for k in range(2):
            at = k + right * (GROUP + 2)
            loads.start(halo.at[pl.ds(4 * k, 4)], ue.at[:, at])
            loads.start(halo.at[pl.ds(8 + 2 * k, 2)], de.at[:, at])
        loads.start(halo.at[pl.ds(12, 4)], ve.at[:, right * (GROUP + 1)])
        loads.start(halo.at[pl.ds(16, 2)], halo_mat.at[right])
    kept = hist_hbm.shape[0] - 2
    table_copy = misc.start(table_hbm, table_out)
    misc.start(hist_hbm.at[pl.ds(0, kept)], hist_out.at[pl.ds(2, kept)])
    loads.wait()

    lane = iota((nz, LANES), 1)
    columns = fault_columns(rows_ref)

    def put(plane, slot, value):
        spot = (lane >= slot * GROUP) & (lane < (slot + 1) * GROUP)
        shift = slot * GROUP
        packed[plane] = jnp.where(spot, pltpu.roll(value, shift, 1), packed[plane])

    def first_step(x, classes_of):
        for s in range(2):
            c = [1.0 - de[s, x + k] for k in range(3)]
            u = [[ue[comp * 2 + s, x + k] for k in range(3)] for comp in range(2)]
            forces, energy = stencil(u, c)
            rate, limit = classed(classes_of(s), tab_ref)
            c_new = c[1] * decay(rate, limit, energy)
            c1[s, x] = c_new
            put(PK_C + s, x, c_new[:, :LANES])
            put(PK_RATE + s, x, rate[:, :LANES])
            put(PK_LIMIT + s, x, limit[:, :LANES])
            for comp in range(2):
                i = comp * 2 + s
                v_new = ve[i, x] + DT * forces[comp]
                u_new = u[comp][1] + DT * v_new
                ve[i, x] = v_new
                u1[i, x] = u_new
                put(PK_V + i, x, v_new[:, :LANES])
                put(PK_U + i, x, u_new[:, :LANES])

    packed[...] = jnp.zeros(packed.shape, jnp.float32)
    first_step(0, lambda s: halo_mat[0, s].astype(jnp.int32))
    first_step(GROUP + 1, lambda s: halo_mat[1, s].astype(jnp.int32))

    @pl.loop(0, GROUP)
    def _(x):
        first_step(x + 1, lambda s: mat[s, x])

    far = pl.ds(LANES, uo.shape[3] - LANES)

    def outs(x):
        return (
            pltpu.make_async_copy(uo.at[:, x, :, far], u_out.at[:, x, :, far], out_sem.at[0, x]),
            pltpu.make_async_copy(vo.at[:, x, :, far], v_out.at[:, x, :, far], out_sem.at[1, x]),
            pltpu.make_async_copy(do.at[:, x, :, far], d_out.at[:, x, :, far], out_sem.at[2, x]),
        )

    @pl.loop(0, GROUP)
    def _(x):
        for s in range(2):
            c = [c1[s, x + k] for k in range(3)]
            u = [[u1[comp * 2 + s, x + k] for k in range(3)] for comp in range(2)]
            forces, energy = stencil(u, c)
            rate, limit = classed(mat[s, x], tab_ref)
            d_new = 1.0 - c[1] * decay(rate, limit, energy)
            do[s, x] = d_new
            dt[s, x] = d_new[:, :LANES]
            for comp in range(2):
                i = comp * 2 + s
                v_new = ve[i, x + 1] + DT * forces[comp]
                u_new = u[comp][1] + DT * v_new
                vo[i, x] = v_new
                uo[i, x] = u_new
                vt[i, x] = v_new[:, :LANES]
                ut[i, x] = u_new[:, :LANES]
        for one in outs(x):
            one.start()

    spread = iota((columns.shape[1], LANES), 0)
    wide = iota((columns.shape[1], LANES), 1)
    for s in range(2):
        pick = (spread == s * GROUP + wide // GROUP - 1) & (wide >= GROUP) & (wide < (GROUP + 1) * GROUP)
        rows = jnp.dot(columns, pick.astype(jnp.float32), preferred_element_type=jnp.float32)
        inside = (lane >= GROUP) & (lane < (GROUP + 1) * GROUP)
        hit = inside & (rows == (lane % GROUP).astype(jnp.float32))
        packed[PK_FAULT + s] = hit.astype(jnp.float32)
    table_copy.wait()
    length = table_out.shape[0]
    near[...] = jnp.zeros(near.shape, jnp.float32)
    for slot in range(SLOTS):
        x = lax.rem(pos * GROUP + (length - 1 + slot), length)
        near[slot * GROUP : (slot + 1) * GROUP, :] = jnp.broadcast_to(
            table_out[pl.ds(x, 1), :], (GROUP, length)
        )
    for one in misc.made[1:]:
        one.wait()

    @pl.loop(0, GROUP)
    def _(x):
        for one in outs(x):
            one.wait()


def regroup(blocks):
    lane = iota(blocks[0].shape, 1) // GROUP
    for bit in (1, 2, 4, 8):
        low = (lane & bit) == 0
        new = list(blocks)
        for i in range(16):
            if i & bit == 0:
                a, b = blocks[i], blocks[i | bit]
                new[i] = jnp.where(low, a, pltpu.roll(b, bit * GROUP, 1))
                new[i | bit] = jnp.where(low, pltpu.roll(a, LANES - bit * GROUP, 1), b)
        blocks = new
    return blocks


def swap_parts(a):
    n = a.shape[1]
    return jnp.where(
        iota(a.shape, 1) % GROUP < OWNED, pltpu.roll(a, n - OWNED, 1), pltpu.roll(a, OWNED, 1)
    )


def final_kernel(
    n, gathered, u_in, v_in, d_in, hist_in, ut, vt, dt, packed, near, table,
    u_out, v_out, d_out, hist_out,
    spread, edge, uo, vo, do, hist_ref, sems,
):
    pos = lax.axis_index("long")
    nz = gathered.shape[1] // 2
    length = n * GROUP
    lane = iota((nz, LANES), 1)
    for t in range(length // LANES):
        at = slice(t * LANES, (t + 1) * LANES)
        for half, ref in ((0, spread), (1, edge)):
            blocks = [gathered[t * 16 + d, half * nz : (half + 1) * nz] for d in range(16)]
            for g, block in enumerate(regroup(blocks)[: ref.shape[0] // nz]):
                ref[g * nz : (g + 1) * nz, at] = block

    def edges(which, side, s):
        g = which * 4 + side * 2 + s
        return edge[g * nz : (g + 1) * nz, :]

    full = iota((nz, length), 1)
    adds = []
    for s in range(2):
        next_u = pltpu.roll(edges(0, 0, s), length - GROUP, 1)
        next_c = pltpu.roll(edges(1, 0, s), length - GROUP, 1)
        flux = (0.5 * (edges(1, 1, s) + next_c)) * (next_u - edges(0, 1, s))
        flux = (DT * DT if s == 1 else -DT * DT) * flux
        adds.append((edges(2, 1, s) * flux, edges(2, 0, s) * pltpu.roll(-flux, GROUP, 1)))
    for side, x in ((0, GROUP - 1), (1, 0)):
        total = adds[0][side] + adds[1][side]
        total += pltpu.roll(total, length - 1, 1)
        total += pltpu.roll(total, length - 2, 1)
        for c in range(2):
            moved = pltpu.roll(total, (x - c * 4) % length, 1)
            spread[(2 + c) * nz : (3 + c) * nz, :] += jnp.where(full % GROUP == x, moved, 0.0)

    both = 2 * nz
    spectra = jnp.dot(
        spread[0 : 2 * both, :], table[...], precision=EXACT, preferred_element_type=jnp.float32
    )
    first_now = spectra[0:both]
    hist1, hist2, k0r, k0i, k1r, k1i = (spread[i * both : (i + 1) * both, :] for i in range(2, 8))
    swapped = swap_parts(first_now)
    traction1 = hist1 + k0r * first_now + k0i * swapped
    wide = iota((both, length), 1)
    kept = jnp.where(wide == OWNED, 0.0, traction1)
    second_now = spectra[both : 2 * both] - (2.0 * DT * DT) * kept
    traction2 = hist2 + k1r * first_now + k1i * swapped + k0r * second_now + k0i * swap_parts(second_now)
    weight = jnp.where((wide // GROUP == 0) & (wide % OWNED == 0), 1.0, 2.0)
    weighted = jnp.concatenate([weight * traction1, weight * traction2], 0)
    tractions = lax.dot_general(
        weighted, near[...], (((1,), (1,)), ((), ())), precision=EXACT, preferred_element_type=jnp.float32
    )

    u_now, v_now, c_now, faults = [], [], [], []
    for s in range(2):
        before = pltpu.roll(gathered[lax.rem(pos + n - 1, n), nz : 2 * nz], LANES - (80 + s * 8), 1)
        after = pltpu.roll(
            gathered[lax.rem(pos + 1, n), nz : 2 * nz], (GROUP + 1) * GROUP + LANES - (64 + s * 8), 1
        )
        last = (GROUP + 1) * GROUP
        fault = jnp.where(lane < 4, before, packed[PK_FAULT + s])
        fault = jnp.where((lane >= last) & (lane < last + 4), after, fault)
        faults.append(fault if s == 0 else -fault)
        c_now.append(packed[PK_C + s])
    for i in range(4):
        c, s = i // 2, i % 2
        push = DT * tractions[c * nz : (c + 1) * nz] * faults[s]
        v_now.append(packed[PK_V + i] + push)
        u_now.append(packed[PK_U + i] + DT * push)

    low_row = lane % GROUP == 0

    def around(a, fill):
        return (
            pltpu.roll(a, LANES - GROUP, 1), pltpu.roll(a, GROUP, 1),
            up_z(a, fill), down_z(a, fill),
            pltpu.roll(a, LANES - 1, 1), jnp.where(low_row, fill, pltpu.roll(a, 1, 1)),
        )

    results = {}
    for s in range(2):
        c0 = c_now[s]
        bars = [0.5 * (c0 + one) for one in around(c0, c0)]
        quarter = jnp.zeros((nz, LANES), jnp.float32)
        for c in range(2):
            i = c * 2 + s
            u0 = u_now[i]
            steps = [one - u0 for one in around(u0, 0.0)]
            force = bars[0] * steps[0]
            for bar, step in zip(bars[1:], steps[1:]):
                force += bar * step
            for k in range(3):
                gradient = steps[2 * k] - steps[2 * k + 1]
                quarter += gradient * gradient
            at = (2 + c) * nz
            v_new = v_now[i] + DT * (force + tractions[at : at + nz] * faults[s])
            results["v", i] = v_new
            results["u", i] = u0 + DT * v_new
        results["d", s] = 1.0 - c0 * decay(packed[PK_RATE + s], packed[PK_LIMIT + s], 0.25 * quarter)

    out = Copies(sems)
    first = pl.ds(0, LANES)
    changed = lane < 5
    for name, count, old, ref, dst in (
        ("u", 4, ut, uo, u_out), ("v", 4, vt, vo, v_out), ("d", 2, dt, do, d_out)
    ):
        for i in range(count):
            for x in range(GROUP):
                moved = pltpu.roll(results[name, i], LANES - (x + 1) * GROUP, 1)
                ref[i, x] = jnp.where(changed, moved, old[i, x])
        out.start(ref, dst.at[:, :, :, first])

    rows = 2 * GROUP
    row = iota((rows, length), 0)
    target = pos * GROUP + ((row // 2) % 2) * OWNED + row // 4
    for step, now in ((1, first_now), (0, second_now)):
        total = jnp.zeros((rows, nz), jnp.float32)
        for c in range(2):
            pick = ((target == iota((rows, length), 1)) & (row % 2 == c)).astype(jnp.float32)
            total += lax.dot_general(
                pick, now[c * nz : (c + 1) * nz], (((1,), (1,)), ((), ())),
                precision=EXACT, preferred_element_type=jnp.float32,
            )
        hist_ref[step] = total
    out.start(hist_ref, hist_out.at[pl.ds(0, 2)])
    out.wait()


def per_device(n, displacement, velocity, damage, material, damage_table, fault_rows, kernel, history):
    comps, strips, cells, nz, ny = displacement.shape
    assert cells == GROUP and comps == 2 and strips == 2
    lags = kernel.shape[0]
    length = n * cells
    f32 = jnp.float32
    u = displacement.reshape(4, cells, nz, ny)
    v = velocity.reshape(4, cells, nz, ny)
    kern = jnp.transpose(kernel, (1, 2, 3, 0)).reshape(2 * GROUP, lags)
    hist = history.reshape(lags - 1, 2 * GROUP, nz)
    table = jnp.asarray(table_of(length))

    vmem = pl.BlockSpec(memory_space=pltpu.VMEM)
    hbm = pl.BlockSpec(memory_space=pltpu.HBM)
    either = pl.BlockSpec(memory_space=pl.ANY)
    shaped = lambda *shape: jax.ShapeDtypeStruct(shape, f32)
    scratch = lambda *lead: pltpu.VMEM((*lead, nz, ny), f32)
    near_rows = lambda *lead: pltpu.VMEM((*lead, nz, LANES), f32)
    params = pltpu.CompilerParams(vmem_limit_bytes=40 * 1024 * 1024)

    block, even, odd = pl.pallas_call(
        functools.partial(pack_kernel, n),
        out_shape=(shaped(n, 2 * nz, LANES), shaped(HALO_PLANES, nz, ny), shaped(HALO_PLANES, nz, ny)),
        in_specs=[hbm] * 7,
        out_specs=[vmem] * 3,
        scratch_shapes=[
            near_rows(4, cells), near_rows(4, cells), near_rows(2, cells),
            pltpu.VMEM(fault_rows.shape, jnp.int32), pltpu.VMEM(kern.shape, f32), pltpu.VMEM(hist.shape, f32),
            pltpu.VMEM((2, 2, nz, ny), jnp.int32),
            pltpu.SemaphoreType.DMA((6,)), pltpu.SemaphoreType.DMA((12,)),
        ],
        compiler_params=params,
    )(u, v, damage, material, fault_rows, kern, hist)

    pairs = [(i, i ^ 1) for i in range(n)]
    even = lax.ppermute(even, "long", pairs)
    odd = lax.ppermute(odd, "long", [((a + 1) % n, (b + 1) % n) for a, b in pairs])
    gathered = lax.all_to_all(block, "long", 0, 0)

    u_far, v_far, d_far, hist_far, ut, vt, dt, packed, near, table = pl.pallas_call(
        functools.partial(local_kernel, n),
        out_shape=(
            shaped(*u.shape), shaped(*v.shape), shaped(*damage.shape), shaped(*hist.shape),
            shaped(4, cells, nz, LANES), shaped(4, cells, nz, LANES), shaped(2, cells, nz, LANES),
            shaped(PK_COUNT, nz, LANES), shaped(LANES, length), shaped(length, length),
        ),
        in_specs=[hbm] * 6 + [either] * 2 + [hbm] * 2,
        out_specs=[hbm] * 4 + [vmem] * 6,
        scratch_shapes=[
            scratch(4, cells + 4), scratch(4, cells + 2), scratch(2, cells + 4),
            pltpu.VMEM((2, cells, nz, ny), jnp.int32), scratch(2, 2),
            pltpu.SMEM(damage_table.shape, f32), pltpu.VMEM(fault_rows.shape, jnp.int32),
            scratch(4, cells + 2), scratch(2, cells + 2),
            scratch(4, cells), scratch(4, cells), scratch(2, cells),
            pltpu.SemaphoreType.DMA((18,)), pltpu.SemaphoreType.DMA((3, cells)), pltpu.SemaphoreType.DMA((2,)),
        ],
        compiler_params=params,
        cost_estimate=pl.CostEstimate(flops=20_000_000, bytes_accessed=6_000_000, transcendentals=400_000),
    )(u, v, damage, material, damage_table, fault_rows, even, odd, hist, table)

    u_new, v_new, d_new, hist_new = pl.pallas_call(
        functools.partial(final_kernel, n),
        out_shape=(shaped(*u.shape), shaped(*v.shape), shaped(*damage.shape), shaped(*hist.shape)),
        in_specs=[vmem] + [hbm] * 4 + [vmem] * 6,
        out_specs=[hbm] * 4,
        input_output_aliases={1: 0, 2: 1, 3: 2, 4: 3},
        scratch_shapes=[
            pltpu.VMEM((16 * nz, length), f32), pltpu.VMEM((12 * nz, length), f32),
            near_rows(4, cells), near_rows(4, cells), near_rows(2, cells),
            pltpu.VMEM((2, 2 * GROUP, nz), f32), pltpu.SemaphoreType.DMA((4,)),
        ],
        compiler_params=params,
    )(gathered, u_far, v_far, d_far, hist_far, ut, vt, dt, packed, near, table)
    return (
        u_new.reshape(displacement.shape),
        v_new.reshape(velocity.shape),
        d_new,
        hist_new.reshape(history.shape),
    )


def solution(mesh):
    placed = (
        P("groups", None, "long", None, None),
        P("groups", None, "long", None, None),
        P("groups", "long", None, None),
        P("groups", "long", None, None),
        P(),
        P("groups", "long", None),
        P(None, "long", None, None),
        P("groups", "long", None, None, None),
    )
    return jax.shard_map(
        functools.partial(per_device, mesh.shape["long"]),
        mesh=mesh,
        in_specs=placed,
        out_specs=(placed[0], placed[1], placed[2], placed[7]),
        check_vma=False,
    )
```

```python
import functools
import math

import jax
import jax.numpy as jnp
import numpy as np
from jax import lax
from jax.experimental import pallas as pl
from jax.experimental.pallas import tpu as pltpu
from jax.sharding import PartitionSpec as P

DT = 0.5
EXACT = lax.Precision.HIGHEST
LANES = 128
GROUP = 8
OWNED = GROUP // 2
HALO_PLANES = 18
SLOTS = GROUP + 2


def table_of(length):
    lane = np.arange(length)
    wave = (lane // GROUP) * OWNED + lane % OWNED
    imag = (lane % GROUP) // OWNED
    phase = (np.arange(length)[:, None] * wave[None]) % length * (2.0 * np.pi / length)
    table = np.where(imag[None] == 1, -np.sin(phase), np.cos(phase)) / math.sqrt(length)
    return table.astype(np.float32)


def iota(shape, axis):
    return lax.broadcasted_iota(jnp.int32, shape, axis)


def up_z(a, fill):
    n = a.shape[0]
    return jnp.where(iota(a.shape, 0) == n - 1, fill, pltpu.roll(a, n - 1, 0))


def down_z(a, fill):
    return jnp.where(iota(a.shape, 0) == 0, fill, pltpu.roll(a, 1, 0))


def up_r(a, fill):
    n = a.shape[1]
    return jnp.where(iota(a.shape, 1) == n - 1, fill, pltpu.roll(a, n - 1, 1))


def down_r(a, fill):
    return jnp.where(iota(a.shape, 1) == 0, fill, pltpu.roll(a, 1, 1))


def fault_columns(rows_ref):
    rows = rows_ref[...].astype(jnp.float32).reshape(2 * GROUP, -1)
    nz = rows.shape[1]
    eye = (iota((nz, nz), 0) == iota((nz, nz), 1)).astype(jnp.float32)
    return lax.dot_general(eye, rows, (((1,), (1,)), ((), ())), preferred_element_type=jnp.float32)


def on_fault_plane(columns, s, x):
    nz = columns.shape[0]
    column = columns[:, s * GROUP + x : s * GROUP + x + 1]
    return jnp.broadcast_to(column, (nz, LANES)) == iota((nz, LANES), 1).astype(jnp.float32)


def k_row(lag, comp, form):
    return comp * 4 + form * 2 + lag


class Copies:
    def __init__(self, sems):
        self.sems, self.made = sems, []

    def start(self, src, dst):
        one = pltpu.make_async_copy(src, dst, self.sems.at[len(self.made)])
        one.start()
        self.made.append(one)
        return one

    def wait(self):
        for one in self.made:
            one.wait()


def pack_kernel(
    u_hbm, v_hbm, d_hbm, mat_hbm, rows_hbm, kern_hbm, hist_hbm,
    out_ref, even_ref, odd_ref,
    ut, vt, dt, rows_ref, kern_ref, hist_ref, mat_ref, sems, halo_sems,
):
    nz = u_hbm.shape[2]
    loads, halos = Copies(sems), Copies(halo_sems)
    near = pl.ds(0, LANES)
    loads.start(u_hbm.at[:, :, :, near], ut)
    loads.start(d_hbm.at[:, :, :, near], dt)
    loads.start(rows_hbm, rows_ref)
    loads.start(v_hbm.at[:, :, :, near], vt)
    loads.start(kern_hbm, kern_ref)
    loads.start(hist_hbm, hist_ref)
    parity = lax.rem(lax.axis_index("long"), 2)
    for i, (ref, right) in enumerate(((even_ref, 1 - parity), (odd_ref, parity))):
        low, inner = right * (GROUP - 2), right * (GROUP - 1)
        for k in range(2):
            halos.start(u_hbm.at[:, low + k], ref.at[pl.ds(4 * k, 4)])
            halos.start(d_hbm.at[:, low + k], ref.at[pl.ds(8 + 2 * k, 2)])
        halos.start(v_hbm.at[:, inner], ref.at[pl.ds(12, 4)])
        halos.start(mat_hbm.at[:, inner], mat_ref.at[i])
    loads.wait()

    lane = iota((nz, LANES), 1)
    columns = fault_columns(rows_ref)
    out = jnp.zeros((nz, LANES), jnp.float32)
    zero = jnp.zeros((nz, LANES), jnp.float32)
    for x in range(GROUP):
        slip = [zero, zero]
        ahead = [zero, zero]
        for s in range(2):
            fault = on_fault_plane(columns, s, x)
            c0 = 1.0 - dt[s, x]
            bars = []
            if x > 0:
                bars.append((x - 1, 0.5 * (c0 + (1.0 - dt[s, x - 1]))))
            if x < GROUP - 1:
                bars.append((x + 1, 0.5 * (c0 + (1.0 - dt[s, x + 1]))))
            bar_zu = 0.5 * (c0 + up_z(c0, c0))
            bar_zd = 0.5 * (c0 + down_z(c0, c0))
            bar_ru = 0.5 * (c0 + up_r(c0, c0))
            bar_rd = 0.5 * (c0 + down_r(c0, c0))
            for c in range(2):
                u0 = ut[c * 2 + s, x]
                force = bar_zu * (up_z(u0, 0.0) - u0) + bar_zd * (down_z(u0, 0.0) - u0)
                force += bar_ru * (up_r(u0, 0.0) - u0) + bar_rd * (down_r(u0, 0.0) - u0)
                for other, bar in bars:
                    force += bar * (ut[c * 2 + s, other] - u0)
                later = u0 + DT * (vt[c * 2 + s, x] + DT * force)
                sign = 1.0 if s == 1 else -1.0
                slip[c] += jnp.where(fault, sign * u0, 0.0)
                ahead[c] += jnp.where(fault, sign * later, 0.0)
            if x in (0, GROUP - 1):
                side = 0 if x == 0 else 1
                moves = [(64 + side * 16 + s * 8 + c * 4, ut[c * 2 + s, x]) for c in range(2)]
                moves.append((96 + side * 8 + s * 4, c0))
                for at, plane in moves:
                    out = jnp.where((lane >= at) & (lane < at + 4), pltpu.roll(plane, at, 1), out)
                column = columns[:, s * GROUP + x : s * GROUP + x + 1]
                out = jnp.where(lane == 112 + side * 2 + s, column, out)
        for c in range(2):
            out = jnp.where(lane == c * GROUP + x, jnp.sum(slip[c], 1, keepdims=True), out)
            out = jnp.where(lane == 16 + c * GROUP + x, jnp.sum(ahead[c], 1, keepdims=True), out)

    kern = kern_ref[...]
    count = kern.shape[0]
    real_row = (iota(kern.shape, 0) // 2) % 2 == 0
    from_next = pltpu.roll(kern, count - 2, 0)
    a_rows = jnp.where(real_row, kern, pltpu.roll(kern, 2, 0))
    b_rows = jnp.where(real_row, -from_next, kern)
    b_source = jnp.where(real_row, from_next, -kern)
    parts = []
    lags = hist_ref.shape[0] + 1
    for skip in (1, 2):
        straight = jnp.zeros((count, nz), jnp.float32)
        crossed = jnp.zeros((count, nz), jnp.float32)
        for l in range(skip, lags):
            straight += a_rows[:, l : l + 1] * hist_ref[l - skip]
            crossed += b_source[:, l : l + 1] * hist_ref[l - skip]
        real_here = (iota((count, nz), 0) // 2) % 2 == 0
        swapped = jnp.where(real_here, pltpu.roll(crossed, count - 2, 0), pltpu.roll(crossed, 2, 0))
        parts.append(straight + swapped)
    square = (count, nz)
    coefficients = jnp.zeros(square, jnp.float32)
    for c in range(2):
        for form, rows in enumerate((a_rows, b_rows)):
            for l in (0, 1):
                here = (iota(square, 0) % 2 == c) & (iota(square, 1) == k_row(l, c, form))
                coefficients = jnp.where(here, rows[:, l : l + 1], coefficients)
    parts.append(coefficients)
    stacked = jnp.concatenate(parts, 0)
    total = stacked.shape[0]
    row = iota((total, LANES), 0)
    start = jnp.where(row < 32, 32 + (row // 16) * 16 + (row % 2) * GROUP, LANES - GROUP)
    target = start + ((row // 2) % 2) * OWNED + (row // 4) % OWNED
    place = (target == iota((total, LANES), 1)).astype(jnp.float32)
    out += lax.dot_general(
        stacked, place, (((0,), (0,)), ((), ())), precision=EXACT, preferred_element_type=jnp.float32
    )
    for d in range(out_ref.shape[0]):
        out_ref[d] = out
    halos.wait()
    for i, ref in enumerate((even_ref, odd_ref)):
        ref[16:18] = mat_ref[i].astype(jnp.float32)


def stencil(u, c):
    (cm, c0, cp), quarter = c, None
    bars = (
        (0.5 * (c0 + cp), 0.5 * (c0 + cm)),
        (0.5 * (c0 + up_z(c0, c0)), 0.5 * (c0 + down_z(c0, c0))),
        (0.5 * (c0 + up_r(c0, c0)), 0.5 * (c0 + down_r(c0, c0))),
    )
    forces = []
    for um, u0, up in u:
        pairs = (
            (up - u0, u0 - um),
            (up_z(u0, 0.0) - u0, u0 - down_z(u0, 0.0)),
            (up_r(u0, 0.0) - u0, u0 - down_r(u0, 0.0)),
        )
        force = None
        for (above, below), (bar_up, bar_down) in zip(pairs, bars):
            term = bar_up * above - bar_down * below
            force = term if force is None else force + term
            gradient = above + below
            quarter = gradient * gradient if quarter is None else quarter + gradient * gradient
        forces.append(force)
    return forces, 0.25 * quarter


def classed(classes, table_ref):
    rate = jnp.full(classes.shape, table_ref[0, 0])
    limit = jnp.full(classes.shape, table_ref[1, 0])
    for level in range(1, table_ref.shape[1]):
        here = classes == level
        rate = jnp.where(here, table_ref[0, level], rate)
        limit = jnp.where(here, table_ref[1, level], limit)
    return rate, limit


def decay(rate, limit, energy):
    over = energy - limit
    soft = jnp.maximum(over, 0.0) + jnp.log(1.0 + jnp.exp(-jnp.abs(over)))
    return jnp.exp(-rate * soft)


PK_U, PK_C, PK_V, PK_RATE, PK_LIMIT, PK_FAULT, PK_COUNT = 0, 4, 6, 10, 12, 14, 16


def local_kernel(
    n, u_hbm, v_hbm, d_hbm, mat_hbm, tab_hbm, rows_hbm, even_hbm, odd_hbm, hist_hbm, table_hbm,
    u_out, v_out, d_out, hist_out, ut, vt, dt, packed, near, table_out,
    ue, ve, de, mat, halo_mat, tab_ref, rows_ref, u1, c1, uo, vo, do, in_sem, out_sem, misc_sem,
):
    pos = lax.axis_index("long")
    parity = lax.rem(pos, 2)
    nz = u_hbm.shape[2]
    loads, misc = Copies(in_sem), Copies(misc_sem)
    loads.start(u_hbm, ue.at[:, pl.ds(2, GROUP)])
    loads.start(v_hbm, ve.at[:, pl.ds(1, GROUP)])
    loads.start(d_hbm, de.at[:, pl.ds(2, GROUP)])
    loads.start(mat_hbm, mat)
    loads.start(tab_hbm, tab_ref)
    loads.start(rows_hbm, rows_ref)
    for halo, right in ((even_hbm, 1 - parity), (odd_hbm, parity)):
        for k in range(2):
            at = k + right * (GROUP + 2)
            loads.start(halo.at[pl.ds(4 * k, 4)], ue.at[:, at])
            loads.start(halo.at[pl.ds(8 + 2 * k, 2)], de.at[:, at])
        loads.start(halo.at[pl.ds(12, 4)], ve.at[:, right * (GROUP + 1)])
        loads.start(halo.at[pl.ds(16, 2)], halo_mat.at[right])
    kept = hist_hbm.shape[0] - 2
    table_copy = misc.start(table_hbm, table_out)
    misc.start(hist_hbm.at[pl.ds(0, kept)], hist_out.at[pl.ds(2, kept)])
    loads.wait()

    lane = iota((nz, LANES), 1)
    columns = fault_columns(rows_ref)

    def put(plane, slot, value):
        spot = (lane >= slot * GROUP) & (lane < (slot + 1) * GROUP)
        shift = slot * GROUP
        packed[plane] = jnp.where(spot, pltpu.roll(value, shift, 1), packed[plane])

    def first_step(x, classes_of):
        for s in range(2):
            c = [1.0 - de[s, x + k] for k in range(3)]
            u = [[ue[comp * 2 + s, x + k] for k in range(3)] for comp in range(2)]
            forces, energy = stencil(u, c)
            rate, limit = classed(classes_of(s), tab_ref)
            c_new = c[1] * decay(rate, limit, energy)
            c1[s, x] = c_new
            put(PK_C + s, x, c_new[:, :LANES])
            put(PK_RATE + s, x, rate[:, :LANES])
            put(PK_LIMIT + s, x, limit[:, :LANES])
            for comp in range(2):
                i = comp * 2 + s
                v_new = ve[i, x] + DT * forces[comp]
                u_new = u[comp][1] + DT * v_new
                ve[i, x] = v_new
                u1[i, x] = u_new
                put(PK_V + i, x, v_new[:, :LANES])
                put(PK_U + i, x, u_new[:, :LANES])

    packed[...] = jnp.zeros(packed.shape, jnp.float32)
    first_step(0, lambda s: halo_mat[0, s].astype(jnp.int32))
    first_step(GROUP + 1, lambda s: halo_mat[1, s].astype(jnp.int32))

    @pl.loop(0, GROUP)
    def _(x):
        first_step(x + 1, lambda s: mat[s, x])

    far = pl.ds(LANES, uo.shape[3] - LANES)

    def outs(x):
        return (
            pltpu.make_async_copy(uo.at[:, x, :, far], u_out.at[:, x, :, far], out_sem.at[0, x]),
            pltpu.make_async_copy(vo.at[:, x, :, far], v_out.at[:, x, :, far], out_sem.at[1, x]),
            pltpu.make_async_copy(do.at[:, x, :, far], d_out.at[:, x, :, far], out_sem.at[2, x]),
        )

    @pl.loop(0, GROUP)
    def _(x):
        for s in range(2):
            c = [c1[s, x + k] for k in range(3)]
            u = [[u1[comp * 2 + s, x + k] for k in range(3)] for comp in range(2)]
            forces, energy = stencil(u, c)
            rate, limit = classed(mat[s, x], tab_ref)
            d_new = 1.0 - c[1] * decay(rate, limit, energy)
            do[s, x] = d_new
            dt[s, x] = d_new[:, :LANES]
            for comp in range(2):
                i = comp * 2 + s
                v_new = ve[i, x + 1] + DT * forces[comp]
                u_new = u[comp][1] + DT * v_new
                vo[i, x] = v_new
                uo[i, x] = u_new
                vt[i, x] = v_new[:, :LANES]
                ut[i, x] = u_new[:, :LANES]
        for one in outs(x):
            one.start()

    spread = iota((columns.shape[1], LANES), 0)
    wide = iota((columns.shape[1], LANES), 1)
    for s in range(2):
        pick = (spread == s * GROUP + wide // GROUP - 1) & (wide >= GROUP) & (wide < (GROUP + 1) * GROUP)
        rows = jnp.dot(columns, pick.astype(jnp.float32), preferred_element_type=jnp.float32)
        inside = (lane >= GROUP) & (lane < (GROUP + 1) * GROUP)
        hit = inside & (rows == (lane % GROUP).astype(jnp.float32))
        packed[PK_FAULT + s] = hit.astype(jnp.float32)
    table_copy.wait()
    length = table_out.shape[0]
    near[...] = jnp.zeros(near.shape, jnp.float32)
    for slot in range(SLOTS):
        x = lax.rem(pos * GROUP + (length - 1 + slot), length)
        near[slot * GROUP : (slot + 1) * GROUP, :] = jnp.broadcast_to(
            table_out[pl.ds(x, 1), :], (GROUP, length)
        )
    for one in misc.made[1:]:
        one.wait()

    @pl.loop(0, GROUP)
    def _(x):
        for one in outs(x):
            one.wait()


def regroup(blocks):
    lane = iota(blocks[0].shape, 1) // GROUP
    for bit in (1, 2, 4, 8):
        low = (lane & bit) == 0
        new = list(blocks)
        for i in range(16):
            if i & bit == 0:
                a, b = blocks[i], blocks[i | bit]
                new[i] = jnp.where(low, a, pltpu.roll(b, bit * GROUP, 1))
                new[i | bit] = jnp.where(low, pltpu.roll(a, LANES - bit * GROUP, 1), b)
        blocks = new
    return blocks


def swap_parts(a):
    n = a.shape[1]
    return jnp.where(
        iota(a.shape, 1) % GROUP < OWNED, pltpu.roll(a, n - OWNED, 1), pltpu.roll(a, OWNED, 1)
    )


def final_kernel(
    n, gathered, u_in, v_in, d_in, hist_in, ut, vt, dt, packed, near, table,
    u_out, v_out, d_out, hist_out,
    spread, uo, vo, do, hist_ref, sems,
):
    pos = lax.axis_index("long")
    nz = gathered.shape[1]
    length = n * GROUP
    lane = iota((nz, LANES), 1)

    def block_of(device):
        return gathered[device]

    for t in range(length // LANES):
        at = slice(t * LANES, (t + 1) * LANES)
        for g, block in enumerate(regroup([block_of(t * 16 + d) for d in range(16)])):
            spread[g * nz : (g + 1) * nz, at] = block

    def group(g):
        return spread[g * nz : (g + 1) * nz, :]

    full = iota((nz, length), 1)

    def stiff(side, s):
        plane = group(12 + side)
        first_half = full % GROUP < 4
        if s == 0:
            return jnp.where(first_half, plane, pltpu.roll(plane, 4, 1))
        return jnp.where(first_half, pltpu.roll(plane, length - 4, 1), plane)

    def on_edge(side, s):
        j = side * 2 + s
        row = pltpu.roll(group(14), length - j, 1) if j else group(14)
        row = jnp.where(full % GROUP == 0, row, 0.0)
        for step in (1, 2, 4):
            row += pltpu.roll(row, step, 1)
        return row == (full % 4).astype(jnp.float32)

    adds = []
    for s in range(2):
        next_u = pltpu.roll(group(8 + s), length - GROUP, 1)
        next_c = pltpu.roll(stiff(0, s), length - GROUP, 1)
        flux = (0.5 * (stiff(1, s) + next_c)) * (next_u - group(10 + s))
        flux = (DT * DT if s == 1 else -DT * DT) * flux
        adds.append((
            jnp.where(on_edge(1, s), flux, 0.0), jnp.where(on_edge(0, s), pltpu.roll(-flux, GROUP, 1), 0.0)
        ))
    for side, x in ((0, GROUP - 1), (1, 0)):
        total = adds[0][side] + adds[1][side]
        total += pltpu.roll(total, length - 1, 1)
        total += pltpu.roll(total, length - 2, 1)
        for c in range(2):
            moved = pltpu.roll(total, (x - c * 4) % length, 1)
            spread[(2 + c) * nz : (3 + c) * nz, :] += jnp.where(full % GROUP == x, moved, 0.0)

    both = 2 * nz
    spectra = jnp.dot(
        spread[0 : 2 * both, :], table[...], precision=EXACT, preferred_element_type=jnp.float32
    )
    first_now = spectra[0:both]
    hist1, hist2 = (spread[i * both : (i + 1) * both, :] for i in (2, 3))

    def factor(lag, form):
        rows = [15 * nz + k_row(lag, c, form) for c in range(2)]
        return jnp.concatenate(
            [jnp.broadcast_to(spread[row : row + 1, :], (nz, length)) for row in rows], 0
        )

    k0r, k0i, k1r, k1i = factor(0, 0), factor(0, 1), factor(1, 0), factor(1, 1)
    swapped = swap_parts(first_now)
    traction1 = hist1 + k0r * first_now + k0i * swapped
    wide = iota((both, length), 1)
    kept = jnp.where(wide == OWNED, 0.0, traction1)
    second_now = spectra[both : 2 * both] - (2.0 * DT * DT) * kept
    traction2 = hist2 + k1r * first_now + k1i * swapped + k0r * second_now + k0i * swap_parts(second_now)
    weight = jnp.where((wide // GROUP == 0) & (wide % OWNED == 0), 1.0, 2.0)
    weighted = jnp.concatenate([weight * traction1, weight * traction2], 0)
    tractions = lax.dot_general(
        weighted, near[...], (((1,), (1,)), ((), ())), precision=EXACT, preferred_element_type=jnp.float32
    )

    u_now, v_now, c_now, faults = [], [], [], []
    for s in range(2):
        before = block_of(lax.rem(pos + n - 1, n))[:, 114 + s : 115 + s]
        after = block_of(lax.rem(pos + 1, n))[:, 112 + s : 113 + s]
        row = (lane % GROUP).astype(jnp.float32)
        fault = packed[PK_FAULT + s]
        fault = jnp.where(lane // GROUP == 0, (row == before).astype(jnp.float32), fault)
        fault = jnp.where(lane // GROUP == GROUP + 1, (row == after).astype(jnp.float32), fault)
        faults.append(fault if s == 0 else -fault)
        c_now.append(packed[PK_C + s])
    for i in range(4):
        c, s = i // 2, i % 2
        push = DT * tractions[c * nz : (c + 1) * nz] * faults[s]
        v_now.append(packed[PK_V + i] + push)
        u_now.append(packed[PK_U + i] + DT * push)

    low_row = lane % GROUP == 0

    def around(a, fill):
        return (
            pltpu.roll(a, LANES - GROUP, 1), pltpu.roll(a, GROUP, 1),
            up_z(a, fill), down_z(a, fill),
            pltpu.roll(a, LANES - 1, 1), jnp.where(low_row, fill, pltpu.roll(a, 1, 1)),
        )

    results = {}
    for s in range(2):
        c0 = c_now[s]
        bars = [0.5 * (c0 + one) for one in around(c0, c0)]
        quarter = jnp.zeros((nz, LANES), jnp.float32)
        for c in range(2):
            i = c * 2 + s
            u0 = u_now[i]
            steps = [one - u0 for one in around(u0, 0.0)]
            force = bars[0] * steps[0]
            for bar, step in zip(bars[1:], steps[1:]):
                force += bar * step
            for k in range(3):
                gradient = steps[2 * k] - steps[2 * k + 1]
                quarter += gradient * gradient
            at = (2 + c) * nz
            v_new = v_now[i] + DT * (force + tractions[at : at + nz] * faults[s])
            results["v", i] = v_new
            results["u", i] = u0 + DT * v_new
        results["d", s] = 1.0 - c0 * decay(packed[PK_RATE + s], packed[PK_LIMIT + s], 0.25 * quarter)

    out = Copies(sems)
    first = pl.ds(0, LANES)
    changed = lane < 5
    for name, count, old, ref, dst in (
        ("u", 4, ut, uo, u_out), ("v", 4, vt, vo, v_out), ("d", 2, dt, do, d_out)
    ):
        for i in range(count):
            for x in range(GROUP):
                moved = pltpu.roll(results[name, i], LANES - (x + 1) * GROUP, 1)
                ref[i, x] = jnp.where(changed, moved, old[i, x])
        out.start(ref, dst.at[:, :, :, first])

    rows = 2 * GROUP
    row = iota((rows, length), 0)
    target = pos * GROUP + ((row // 2) % 2) * OWNED + row // 4
    for step, now in ((1, first_now), (0, second_now)):
        total = jnp.zeros((rows, nz), jnp.float32)
        for c in range(2):
            pick = ((target == iota((rows, length), 1)) & (row % 2 == c)).astype(jnp.float32)
            total += lax.dot_general(
                pick, now[c * nz : (c + 1) * nz], (((1,), (1,)), ((), ())),
                precision=EXACT, preferred_element_type=jnp.float32,
            )
        hist_ref[step] = total
    out.start(hist_ref, hist_out.at[pl.ds(0, 2)])
    out.wait()


def per_device(n, displacement, velocity, damage, material, damage_table, fault_rows, kernel, history):
    comps, strips, cells, nz, ny = displacement.shape
    assert cells == GROUP and comps == 2 and strips == 2
    lags = kernel.shape[0]
    length = n * cells
    f32 = jnp.float32
    u = displacement.reshape(4, cells, nz, ny)
    v = velocity.reshape(4, cells, nz, ny)
    kern = jnp.transpose(kernel, (1, 2, 3, 0)).reshape(2 * GROUP, lags)
    hist = history.reshape(lags - 1, 2 * GROUP, nz)
    table = jnp.asarray(table_of(length))

    vmem = pl.BlockSpec(memory_space=pltpu.VMEM)
    hbm = pl.BlockSpec(memory_space=pltpu.HBM)
    either = pl.BlockSpec(memory_space=pl.ANY)
    shaped = lambda *shape: jax.ShapeDtypeStruct(shape, f32)
    scratch = lambda *lead: pltpu.VMEM((*lead, nz, ny), f32)
    near_rows = lambda *lead: pltpu.VMEM((*lead, nz, LANES), f32)
    params = pltpu.CompilerParams(vmem_limit_bytes=40 * 1024 * 1024)

    u, v, d_in, m_in, t_in, f_in, kern, hist, table = (
        pltpu.with_memory_space_constraint(a, pltpu.HBM)
        for a in (u, v, damage, material, damage_table, fault_rows, kern, hist, table)
    )
    block, even, odd = pl.pallas_call(
        pack_kernel,
        out_shape=(shaped(n, nz, LANES), shaped(HALO_PLANES, nz, ny), shaped(HALO_PLANES, nz, ny)),
        in_specs=[hbm] * 7,
        out_specs=[vmem] * 3,
        scratch_shapes=[
            near_rows(4, cells), near_rows(4, cells), near_rows(2, cells),
            pltpu.VMEM(fault_rows.shape, jnp.int32), pltpu.VMEM(kern.shape, f32), pltpu.VMEM(hist.shape, f32),
            pltpu.VMEM((2, 2, nz, ny), jnp.int32),
            pltpu.SemaphoreType.DMA((6,)), pltpu.SemaphoreType.DMA((12,)),
        ],
        compiler_params=params,
    )(u, v, d_in, m_in, f_in, kern, hist)

    pairs = [(i, i ^ 1) for i in range(n)]
    even = lax.ppermute(even, "long", pairs)
    odd = lax.ppermute(odd, "long", [((a + 1) % n, (b + 1) % n) for a, b in pairs])
    gathered = lax.all_to_all(block, "long", 0, 0)

    u_far, v_far, d_far, hist_far, ut, vt, dt, packed, near, table = pl.pallas_call(
        functools.partial(local_kernel, n),
        out_shape=(
            shaped(*u.shape), shaped(*v.shape), shaped(*damage.shape), shaped(*hist.shape),
            shaped(4, cells, nz, LANES), shaped(4, cells, nz, LANES), shaped(2, cells, nz, LANES),
            shaped(PK_COUNT, nz, LANES), shaped(LANES, length), shaped(length, length),
        ),
        in_specs=[hbm] * 6 + [either] * 2 + [hbm] * 2,
        out_specs=[hbm] * 4 + [vmem] * 6,
        scratch_shapes=[
            scratch(4, cells + 4), scratch(4, cells + 2), scratch(2, cells + 4),
            pltpu.VMEM((2, cells, nz, ny), jnp.int32), scratch(2, 2),
            pltpu.SMEM(damage_table.shape, f32), pltpu.VMEM(fault_rows.shape, jnp.int32),
            scratch(4, cells + 2), scratch(2, cells + 2),
            scratch(4, cells), scratch(4, cells), scratch(2, cells),
            pltpu.SemaphoreType.DMA((18,)), pltpu.SemaphoreType.DMA((3, cells)), pltpu.SemaphoreType.DMA((2,)),
        ],
        compiler_params=params,
        cost_estimate=pl.CostEstimate(flops=20_000_000_000, bytes_accessed=600_000_000, transcendentals=400_000),
    )(u, v, d_in, m_in, t_in, f_in, even, odd, hist, table)

    u_new, v_new, d_new, hist_new = pl.pallas_call(
        functools.partial(final_kernel, n),
        out_shape=(shaped(*u.shape), shaped(*v.shape), shaped(*damage.shape), shaped(*hist.shape)),
        in_specs=[vmem] + [hbm] * 4 + [vmem] * 6,
        out_specs=[hbm] * 4,
        input_output_aliases={1: 0, 2: 1, 3: 2, 4: 3},
        scratch_shapes=[
            pltpu.VMEM((16 * nz, length), f32),
            near_rows(4, cells), near_rows(4, cells), near_rows(2, cells),
            pltpu.VMEM((2, 2 * GROUP, nz), f32), pltpu.SemaphoreType.DMA((4,)),
        ],
        compiler_params=params,
    )(gathered, u_far, v_far, d_far, hist_far, ut, vt, dt, packed, near, table)
    return (
        u_new.reshape(displacement.shape),
        v_new.reshape(velocity.shape),
        d_new,
        hist_new.reshape(history.shape),
    )


def solution(mesh):
    placed = (
        P("groups", None, "long", None, None),
        P("groups", None, "long", None, None),
        P("groups", "long", None, None),
        P("groups", "long", None, None),
        P(),
        P("groups", "long", None),
        P(None, "long", None, None),
        P("groups", "long", None, None, None),
    )
    return jax.shard_map(
        functools.partial(per_device, mesh.shape["long"]),
        mesh=mesh,
        in_specs=placed,
        out_specs=(placed[0], placed[1], placed[2], placed[7]),
        check_vma=False,
    )
```

```python
import functools
import math

import jax
import jax.numpy as jnp
import numpy as np
from jax import lax
from jax.experimental import pallas as pl
from jax.experimental.pallas import tpu as pltpu
from jax.sharding import PartitionSpec as P

DT = 0.5
EXACT = lax.Precision.HIGHEST
LANES = 128
GROUP = 8
OWNED = GROUP // 2
HALO_PLANES = 18
SLOTS = GROUP + 2


def table_of(length):
    lane = np.arange(length)
    wave = (lane // GROUP) * OWNED + lane % OWNED
    imag = (lane % GROUP) // OWNED
    phase = (np.arange(length)[:, None] * wave[None]) % length * (2.0 * np.pi / length)
    table = np.where(imag[None] == 1, -np.sin(phase), np.cos(phase)) / math.sqrt(length)
    return table.astype(np.float32)


def iota(shape, axis):
    return lax.broadcasted_iota(jnp.int32, shape, axis)


def up_z(a, fill):
    n = a.shape[0]
    return jnp.where(iota(a.shape, 0) == n - 1, fill, pltpu.roll(a, n - 1, 0))


def down_z(a, fill):
    return jnp.where(iota(a.shape, 0) == 0, fill, pltpu.roll(a, 1, 0))


def up_r(a, fill):
    n = a.shape[1]
    return jnp.where(iota(a.shape, 1) == n - 1, fill, pltpu.roll(a, n - 1, 1))


def down_r(a, fill):
    return jnp.where(iota(a.shape, 1) == 0, fill, pltpu.roll(a, 1, 1))


def fault_columns(rows_ref):
    rows = rows_ref[...].astype(jnp.float32).reshape(2 * GROUP, -1)
    nz = rows.shape[1]
    eye = (iota((nz, nz), 0) == iota((nz, nz), 1)).astype(jnp.float32)
    return lax.dot_general(eye, rows, (((1,), (1,)), ((), ())), preferred_element_type=jnp.float32)


def on_fault_plane(columns, s, x):
    nz = columns.shape[0]
    column = columns[:, s * GROUP + x : s * GROUP + x + 1]
    return jnp.broadcast_to(column, (nz, LANES)) == iota((nz, LANES), 1).astype(jnp.float32)


def k_row(lag, comp, form):
    return comp * 4 + form * 2 + lag


class Copies:
    def __init__(self, sems):
        self.sems, self.made = sems, []

    def start(self, src, dst):
        one = pltpu.make_async_copy(src, dst, self.sems.at[len(self.made)])
        one.start()
        self.made.append(one)
        return one

    def wait(self):
        for one in self.made:
            one.wait()


def halo_kernel(u_ref, v_ref, d_ref, mat_ref, even_ref, odd_ref):
    parity = lax.rem(lax.axis_index("long"), 2)
    for ref, right in ((even_ref, 1 - parity), (odd_ref, parity)):
        low, inner = right * (GROUP - 2), right * (GROUP - 1)
        for k in range(2):
            for i in range(4):
                ref[4 * k + i] = u_ref[i, low + k]
            for s in range(2):
                ref[8 + 2 * k + s] = d_ref[s, low + k]
        for i in range(4):
            ref[12 + i] = v_ref[i, inner]
        for s in range(2):
            ref[16 + s] = mat_ref[s, inner].astype(jnp.float32)


def pack_kernel(count, *refs):
    sources, held = refs[:count], refs[count : 2 * count]
    out_ref, sems = refs[2 * count :]
    loads = Copies(sems)
    ut, vt, dt, rows_ref, kern_ref, hist_ref = held[:6]
    half = GROUP // 2
    for first in (0, half):
        for src, dst in zip(sources[:3], held[:3]):
            loads.start(src.at[:, pl.ds(first, half)], dst.at[:, pl.ds(first, half)])
        if first == 0:
            for src, dst in zip(sources[3:6], held[3:6]):
                loads.start(src, dst)
    for src, dst in zip(sources[6:], held[6:]):
        loads.start(src, dst)
    for one in loads.made[:4]:
        one.wait()
    nz = ut.shape[2]
    near = slice(0, LANES)
    lane = iota((nz, LANES), 1)
    columns = fault_columns(rows_ref)
    out = jnp.zeros((nz, LANES), jnp.float32)
    zero = jnp.zeros((nz, LANES), jnp.float32)
    for x in range(GROUP):
        if x == half - 1:
            for one in loads.made[4:9]:
                one.wait()
        slip = [zero, zero]
        ahead = [zero, zero]
        for s in range(2):
            fault = on_fault_plane(columns, s, x)
            c0 = 1.0 - dt[s, x, :, near]
            bars = []
            if x > 0:
                bars.append((x - 1, 0.5 * (c0 + (1.0 - dt[s, x - 1, :, near]))))
            if x < GROUP - 1:
                bars.append((x + 1, 0.5 * (c0 + (1.0 - dt[s, x + 1, :, near]))))
            bar_zu = 0.5 * (c0 + up_z(c0, c0))
            bar_zd = 0.5 * (c0 + down_z(c0, c0))
            bar_ru = 0.5 * (c0 + up_r(c0, c0))
            bar_rd = 0.5 * (c0 + down_r(c0, c0))
            for c in range(2):
                u0 = ut[c * 2 + s, x, :, near]
                force = bar_zu * (up_z(u0, 0.0) - u0) + bar_zd * (down_z(u0, 0.0) - u0)
                force += bar_ru * (up_r(u0, 0.0) - u0) + bar_rd * (down_r(u0, 0.0) - u0)
                for other, bar in bars:
                    force += bar * (ut[c * 2 + s, other, :, near] - u0)
                later = u0 + DT * (vt[c * 2 + s, x, :, near] + DT * force)
                sign = 1.0 if s == 1 else -1.0
                slip[c] += jnp.where(fault, sign * u0, 0.0)
                ahead[c] += jnp.where(fault, sign * later, 0.0)
            if x in (0, GROUP - 1):
                side = 0 if x == 0 else 1
                moves = [(64 + side * 16 + s * 8 + c * 4, ut[c * 2 + s, x, :, near]) for c in range(2)]
                moves.append((96 + side * 8 + s * 4, c0))
                for at, plane in moves:
                    out = jnp.where((lane >= at) & (lane < at + 4), pltpu.roll(plane, at, 1), out)
                column = columns[:, s * GROUP + x : s * GROUP + x + 1]
                out = jnp.where(lane == 112 + side * 2 + s, column, out)
        for c in range(2):
            out = jnp.where(lane == c * GROUP + x, jnp.sum(slip[c], 1, keepdims=True), out)
            out = jnp.where(lane == 16 + c * GROUP + x, jnp.sum(ahead[c], 1, keepdims=True), out)

    kern = kern_ref[...]
    count = kern.shape[0]
    real_row = (iota(kern.shape, 0) // 2) % 2 == 0
    from_next = pltpu.roll(kern, count - 2, 0)
    a_rows = jnp.where(real_row, kern, pltpu.roll(kern, 2, 0))
    b_rows = jnp.where(real_row, -from_next, kern)
    b_source = jnp.where(real_row, from_next, -kern)
    parts = []
    lags = hist_ref.shape[0] + 1
    for skip in (1, 2):
        straight = jnp.zeros((count, nz), jnp.float32)
        crossed = jnp.zeros((count, nz), jnp.float32)
        for l in range(skip, lags):
            straight += a_rows[:, l : l + 1] * hist_ref[l - skip]
            crossed += b_source[:, l : l + 1] * hist_ref[l - skip]
        real_here = (iota((count, nz), 0) // 2) % 2 == 0
        swapped = jnp.where(real_here, pltpu.roll(crossed, count - 2, 0), pltpu.roll(crossed, 2, 0))
        parts.append(straight + swapped)
    square = (count, nz)
    coefficients = jnp.zeros(square, jnp.float32)
    for c in range(2):
        for form, rows in enumerate((a_rows, b_rows)):
            for l in (0, 1):
                here = (iota(square, 0) % 2 == c) & (iota(square, 1) == k_row(l, c, form))
                coefficients = jnp.where(here, rows[:, l : l + 1], coefficients)
    parts.append(coefficients)
    stacked = jnp.concatenate(parts, 0)
    total = stacked.shape[0]
    row = iota((total, LANES), 0)
    start = jnp.where(row < 32, 32 + (row // 16) * 16 + (row % 2) * GROUP, LANES - GROUP)
    target = start + ((row // 2) % 2) * OWNED + (row // 4) % OWNED
    place = (target == iota((total, LANES), 1)).astype(jnp.float32)
    out_ref[0] = out + lax.dot_general(
        stacked, place, (((0,), (0,)), ((), ())), precision=EXACT, preferred_element_type=jnp.float32
    )
    for one in loads.made[9:]:
        one.wait()


TILE = 8


class Plane:
    def __init__(self, tiles):
        self.tiles = tiles

    @classmethod
    def load(cls, ref, *index):
        nz, ny = ref.shape[-2:]
        return cls([
            [ref[(*index, slice(i, i + TILE), slice(j, j + LANES))] for j in range(0, ny, LANES)]
            for i in range(0, nz, TILE)
        ])

    def store(self, ref, *index):
        for i, line in enumerate(self.tiles):
            for j, tile in enumerate(line):
                ref[(*index, slice(i * TILE, (i + 1) * TILE), slice(j * LANES, (j + 1) * LANES))] = tile

    def map(self, function, *others):
        return Plane([
            [function(tile, *(other.tiles[i][j] for other in others)) for j, tile in enumerate(line)]
            for i, line in enumerate(self.tiles)
        ])

    def __add__(self, other):
        return self.map(lambda a, b: a + b, other)

    def __sub__(self, other):
        return self.map(lambda a, b: a - b, other)

    def __mul__(self, other):
        if isinstance(other, Plane):
            return self.map(lambda a, b: a * b, other)
        return self.map(lambda a: a * other)

    def moved(self, axis, step, zero):
        lines = self.tiles if axis == 1 else [list(line) for line in zip(*self.tiles)]
        size = LANES if axis == 1 else TILE
        shape = lines[0][0].shape
        end = iota(shape, axis) == (size - 1 if step == 1 else 0)
        result = []
        for line in lines:
            turned = [pltpu.roll(tile, size - 1 if step == 1 else 1, axis) for tile in line]
            new = []
            for k, tile in enumerate(line):
                inside = 0 <= k + step < len(line)
                new.append(jnp.where(end, turned[k + step] if inside else (0.0 if zero else tile), turned[k]))
            result.append(new)
        return Plane(result if axis == 1 else [list(line) for line in zip(*result)])


def stencil(u, c):
    cm, c0, cp = c
    around = [cp, cm] + [c0.moved(axis, step, False) for axis in (0, 1) for step in (1, -1)]
    bars = [c0 + one for one in around]
    forces, quarter = [], None
    for um, u0, up in u:
        near = [up, um] + [u0.moved(axis, step, True) for axis in (0, 1) for step in (1, -1)]
        force = None
        for bar, one in zip(bars, near):
            term = bar * (one - u0)
            force = term if force is None else force + term
        for k in range(0, 6, 2):
            gradient = near[k] - near[k + 1]
            quarter = gradient * gradient if quarter is None else quarter + gradient * gradient
        forces.append(force)
    return forces, quarter * 0.25


def classed(classes, table_ref):
    def entry(row, level):
        return jnp.broadcast_to(table_ref[row : row + 1, level : level + 1], classes.shape)

    rate, limit = entry(0, 0), entry(1, 0)
    for level in range(1, table_ref.shape[1]):
        here = classes == level
        rate = jnp.where(here, entry(0, level), rate)
        limit = jnp.where(here, entry(1, level), limit)
    return rate, limit


def decay(rate, limit, energy):
    over = energy - limit
    soft = jnp.maximum(over, 0.0) + jnp.log(1.0 + jnp.exp(-jnp.abs(over)))
    return jnp.exp(-rate * soft)


PK_U, PK_C, PK_V, PK_RATE, PK_LIMIT, PK_FAULT, PK_COUNT = 0, 4, 6, 10, 12, 14, 16


def strides(n):
    far = [(1 << i) | 1 for i in reversed(range(1, n.bit_length() - 1))]
    return far[-1:] + far[:-1] + [1]


def second_step(x, u1, c1, v1, rates, limits, uo, vo, do):
    for s in range(2):
        c = [Plane.load(c1, s, x + k) for k in range(3)]
        u = [[Plane.load(u1, comp * 2 + s, x + k) for k in range(3)] for comp in range(2)]
        forces, energy = stencil(u, c)
        left = Plane.load(rates, s, x).map(decay, Plane.load(limits, s, x), energy)
        c[1].map(lambda a, b: 1.0 - a * b, left).store(do, s, x)
        for comp in range(2):
            i = comp * 2 + s
            v_new = Plane.load(v1, i, x + 1) + forces[comp] * (0.5 * DT)
            v_new.store(vo, i, x)
            (u[comp][1] + v_new * DT).store(uo, i, x)


def inner_kernel(u_ref, v_ref, d_ref, mat, tab_ref, u1, c1, v1, rates, limits, uo, vo, do):
    def stiff(s, x):
        return Plane.load(d_ref, s, x).map(lambda a: 1.0 - a)

    def first_step(x):
        for s in range(2):
            c = [stiff(s, x + k) for k in (-1, 0, 1)]
            u = [[Plane.load(u_ref, comp * 2 + s, x + k) for k in (-1, 0, 1)] for comp in range(2)]
            finish_first(s, x, c, u, Plane.load(mat, s, x), v_ref, x, tab_ref, u1, c1, v1, rates, limits)

    @pl.loop(0, (GROUP - 2) // 2)
    def _(k):
        first_step(2 * k + 1)
        first_step(2 * k + 2)

    @pl.loop(0, (GROUP - 4) // 2)
    def _(k):
        second_step(2 * k + 2, u1, c1, v1, rates, limits, uo, vo, do)
        second_step(2 * k + 3, u1, c1, v1, rates, limits, uo, vo, do)


def finish_first(s, x, c, u, classes, v_now, v_at, tab_ref, u1, c1, v1, rates, limits):
    slot = x + 1
    forces, energy = stencil(u, c)
    both = classes.map(lambda a: classed(a, tab_ref))
    rate, limit = both.map(lambda a: a[0]), both.map(lambda a: a[1])
    (c[1] * rate.map(decay, limit, energy)).store(c1, s, slot)
    if not isinstance(x, int) or 0 <= x < GROUP:
        rate.store(rates, s, x)
        limit.store(limits, s, x)
    for comp in range(2):
        i = comp * 2 + s
        old = v_now[comp] if isinstance(v_now, list) else Plane.load(v_now, i, v_at)
        v_new = old + forces[comp] * (0.5 * DT)
        v_new.store(v1, i, slot)
        (u[comp][1] + v_new * DT).store(u1, i, slot)


def edge_kernel(
    u_ref, v_ref, d_ref, mat, tab_ref, rows_ref, table, even_ref, odd_ref, *refs,
):
    u1, c1, v1, rates, limits, uo, vo, do, packed, near = refs[8:]
    pos = lax.axis_index("long")
    nz = u_ref.shape[2]
    lane = iota((nz, LANES), 1)
    columns = fault_columns(rows_ref)
    even_pos = lax.rem(pos, 2) == 0

    def halo(side, plane):
        pick = even_pos == (side == 1)
        return Plane.load(even_ref, plane).map(lambda a, b: jnp.where(pick, a, b), Plane.load(odd_ref, plane))

    def beside(x):
        if 0 <= x < GROUP:
            return None
        return (0, x + 2) if x < 0 else (1, x - GROUP)

    def disp(i, x):
        at = beside(x)
        return Plane.load(u_ref, i, x) if at is None else halo(at[0], 4 * at[1] + i)

    def stiff(s, x):
        at = beside(x)
        plane = Plane.load(d_ref, s, x) if at is None else halo(at[0], 8 + 2 * at[1] + s)
        return plane.map(lambda a: 1.0 - a)

    for x in (-1, 0, GROUP - 1, GROUP):
        at = beside(x)
        for s in range(2):
            c = [stiff(s, x + k) for k in (-1, 0, 1)]
            u = [[disp(comp * 2 + s, x + k) for k in (-1, 0, 1)] for comp in range(2)]
            if at is None:
                classes, old = Plane.load(mat, s, x), v_ref
            else:
                classes = halo(at[0], 16 + s).map(lambda a: a.astype(jnp.int32))
                old = [halo(at[0], 12 + comp * 2 + s) for comp in range(2)]
            finish_first(s, x, c, u, classes, old, x, tab_ref, u1, c1, v1, rates, limits)
    for x in (0, 1, GROUP - 2, GROUP - 1):
        second_step(x, u1, c1, v1, rates, limits, uo, vo, do)

    def pack(plane, ref, i, first_slot):
        total = jnp.zeros((nz, LANES), jnp.float32)
        for k in range(ref.shape[1]):
            slot = first_slot + k
            value = pltpu.roll(ref[i, k, :, 0:LANES], slot * GROUP, 1) if slot else ref[i, k, :, 0:LANES]
            total = jnp.where(lane // GROUP == slot, value, total)
        packed[plane] = total

    for i in range(4):
        pack(PK_U + i, u1, i, 0)
        pack(PK_V + i, v1, i, 0)
    for s in range(2):
        pack(PK_C + s, c1, s, 0)
        pack(PK_RATE + s, rates, s, 1)
        pack(PK_LIMIT + s, limits, s, 1)

    spread = iota((columns.shape[1], LANES), 0)
    wide = iota((columns.shape[1], LANES), 1)
    for s in range(2):
        pick = (spread == s * GROUP + wide // GROUP - 1) & (wide >= GROUP) & (wide < (GROUP + 1) * GROUP)
        rows = jnp.dot(columns, pick.astype(jnp.float32), preferred_element_type=jnp.float32)
        inside = (lane >= GROUP) & (lane < (GROUP + 1) * GROUP)
        hit = inside & (rows == (lane % GROUP).astype(jnp.float32))
        packed[PK_FAULT + s] = hit.astype(jnp.float32)
    length = table.shape[0]
    near[...] = jnp.zeros(near.shape, jnp.float32)
    for slot in range(SLOTS):
        x = lax.rem(pos * GROUP + (length - 1 + slot), length)
        near[slot * GROUP : (slot + 1) * GROUP, :] = jnp.broadcast_to(table[pl.ds(x, 1), :], (GROUP, length))


def regroup(blocks):
    lane = iota(blocks[0].shape, 1) // GROUP
    for bit in (1, 2, 4, 8):
        low = (lane & bit) == 0
        new = list(blocks)
        for i in range(16):
            if i & bit == 0:
                a, b = blocks[i], blocks[i | bit]
                new[i] = jnp.where(low, a, pltpu.roll(b, bit * GROUP, 1))
                new[i | bit] = jnp.where(low, pltpu.roll(a, LANES - bit * GROUP, 1), b)
        blocks = new
    return blocks


def swap_parts(a):
    n = a.shape[1]
    return jnp.where(
        iota(a.shape, 1) % GROUP < OWNED, pltpu.roll(a, n - OWNED, 1), pltpu.roll(a, OWNED, 1)
    )


def final_kernel(
    n, gathered, uo, vo, do, packed, near, table, hist_ref,
    u_out, v_out, d_out, hist_out,
    spread, ut, vt, dt, hist_new, sems,
):
    out = Copies(sems)
    first, far = pl.ds(0, LANES), pl.ds(LANES, uo.shape[3] - LANES)
    for ref, dst in ((uo, u_out), (vo, v_out), (do, d_out)):
        out.start(ref.at[:, :, :, far], dst.at[:, :, :, far])
    kept = hist_ref.shape[0] - 2
    out.start(hist_ref.at[pl.ds(0, kept)], hist_out.at[pl.ds(2, kept)])
    pos = lax.axis_index("long")
    nz = gathered.shape[1]
    length = n * GROUP
    lane = iota((nz, LANES), 1)

    def block_of(device):
        apart = jnp.bitwise_xor(pos, device)
        at, core = 0, lax.rem(apart, 2)
        steps = strides(n)
        for i, stride in enumerate(steps[:-1]):
            bit = lax.rem(lax.div(apart, stride - 1), 2)
            at, core = at + bit * (1 << i), core + bit
        return gathered[at + lax.rem(core, 2) * (n // 2)]

    for t in range(length // LANES):
        at = slice(t * LANES, (t + 1) * LANES)
        for g, block in enumerate(regroup([block_of(jnp.int32(t * 16 + d)) for d in range(16)])):
            spread[g * nz : (g + 1) * nz, at] = block

    def group(g):
        return spread[g * nz : (g + 1) * nz, :]

    full = iota((nz, length), 1)

    def stiff(side, s):
        plane = group(12 + side)
        first_half = full % GROUP < 4
        if s == 0:
            return jnp.where(first_half, plane, pltpu.roll(plane, 4, 1))
        return jnp.where(first_half, pltpu.roll(plane, length - 4, 1), plane)

    def on_edge(side, s):
        j = side * 2 + s
        row = pltpu.roll(group(14), length - j, 1) if j else group(14)
        row = jnp.where(full % GROUP == 0, row, 0.0)
        for step in (1, 2, 4):
            row += pltpu.roll(row, step, 1)
        return row == (full % 4).astype(jnp.float32)

    adds = []
    for s in range(2):
        next_u = pltpu.roll(group(8 + s), length - GROUP, 1)
        next_c = pltpu.roll(stiff(0, s), length - GROUP, 1)
        flux = (0.5 * (stiff(1, s) + next_c)) * (next_u - group(10 + s))
        flux = (DT * DT if s == 1 else -DT * DT) * flux
        adds.append((
            jnp.where(on_edge(1, s), flux, 0.0), jnp.where(on_edge(0, s), pltpu.roll(-flux, GROUP, 1), 0.0)
        ))
    for side, x in ((0, GROUP - 1), (1, 0)):
        total = adds[0][side] + adds[1][side]
        total += pltpu.roll(total, length - 1, 1)
        total += pltpu.roll(total, length - 2, 1)
        for c in range(2):
            moved = pltpu.roll(total, (x - c * 4) % length, 1)
            spread[(2 + c) * nz : (3 + c) * nz, :] += jnp.where(full % GROUP == x, moved, 0.0)

    both = 2 * nz
    spectra = jnp.dot(
        spread[0 : 2 * both, :], table[...], precision=EXACT, preferred_element_type=jnp.float32
    )
    first_now = spectra[0:both]
    hist1, hist2 = (spread[i * both : (i + 1) * both, :] for i in (2, 3))

    def factor(lag, form):
        rows = [15 * nz + k_row(lag, c, form) for c in range(2)]
        return jnp.concatenate(
            [jnp.broadcast_to(spread[row : row + 1, :], (nz, length)) for row in rows], 0
        )

    k0r, k0i, k1r, k1i = factor(0, 0), factor(0, 1), factor(1, 0), factor(1, 1)
    swapped = swap_parts(first_now)
    traction1 = hist1 + k0r * first_now + k0i * swapped
    wide = iota((both, length), 1)
    kept = jnp.where(wide == OWNED, 0.0, traction1)
    second_now = spectra[both : 2 * both] - (2.0 * DT * DT) * kept
    traction2 = hist2 + k1r * first_now + k1i * swapped + k0r * second_now + k0i * swap_parts(second_now)
    weight = jnp.where((wide // GROUP == 0) & (wide % OWNED == 0), 1.0, 2.0)
    weighted = jnp.concatenate([weight * traction1, weight * traction2], 0)
    tractions = lax.dot_general(
        weighted, near[...], (((1,), (1,)), ((), ())), precision=EXACT, preferred_element_type=jnp.float32
    )

    u_now, v_now, c_now, faults = [], [], [], []
    for s in range(2):
        before = block_of(lax.rem(pos + n - 1, n))[:, 114 + s : 115 + s]
        after = block_of(lax.rem(pos + 1, n))[:, 112 + s : 113 + s]
        row = (lane % GROUP).astype(jnp.float32)
        fault = packed[PK_FAULT + s]
        fault = jnp.where(lane // GROUP == 0, (row == before).astype(jnp.float32), fault)
        fault = jnp.where(lane // GROUP == GROUP + 1, (row == after).astype(jnp.float32), fault)
        faults.append(fault if s == 0 else -fault)
        c_now.append(packed[PK_C + s])
    for i in range(4):
        c, s = i // 2, i % 2
        push = DT * tractions[c * nz : (c + 1) * nz] * faults[s]
        v_now.append(packed[PK_V + i] + push)
        u_now.append(packed[PK_U + i] + DT * push)

    low_row = lane % GROUP == 0

    def around(a, fill):
        return (
            pltpu.roll(a, LANES - GROUP, 1), pltpu.roll(a, GROUP, 1),
            up_z(a, fill), down_z(a, fill),
            pltpu.roll(a, LANES - 1, 1), jnp.where(low_row, fill, pltpu.roll(a, 1, 1)),
        )

    results = {}
    for s in range(2):
        c0 = c_now[s]
        bars = [0.5 * (c0 + one) for one in around(c0, c0)]
        quarter = jnp.zeros((nz, LANES), jnp.float32)
        for c in range(2):
            i = c * 2 + s
            u0 = u_now[i]
            steps = [one - u0 for one in around(u0, 0.0)]
            force = bars[0] * steps[0]
            for bar, step in zip(bars[1:], steps[1:]):
                force += bar * step
            for k in range(3):
                gradient = steps[2 * k] - steps[2 * k + 1]
                quarter += gradient * gradient
            at = (2 + c) * nz
            v_new = v_now[i] + DT * (force + tractions[at : at + nz] * faults[s])
            results["v", i] = v_new
            results["u", i] = u0 + DT * v_new
        results["d", s] = 1.0 - c0 * decay(packed[PK_RATE + s], packed[PK_LIMIT + s], 0.25 * quarter)

    changed = lane < 5
    for name, count, old, ref, dst in (
        ("u", 4, uo, ut, u_out), ("v", 4, vo, vt, v_out), ("d", 2, do, dt, d_out)
    ):
        for i in range(count):
            for x in range(GROUP):
                moved = pltpu.roll(results[name, i], LANES - (x + 1) * GROUP, 1)
                ref[i, x] = jnp.where(changed, moved, old[i, x, :, 0:LANES])
        out.start(ref, dst.at[:, :, :, first])

    rows = 2 * GROUP
    row = iota((rows, length), 0)
    target = pos * GROUP + ((row // 2) % 2) * OWNED + row // 4
    for step, now in ((1, first_now), (0, second_now)):
        total = jnp.zeros((rows, nz), jnp.float32)
        for c in range(2):
            pick = ((target == iota((rows, length), 1)) & (row % 2 == c)).astype(jnp.float32)
            total += lax.dot_general(
                pick, now[c * nz : (c + 1) * nz], (((1,), (1,)), ((), ())),
                precision=EXACT, preferred_element_type=jnp.float32,
            )
        hist_new[step] = total
    out.start(hist_new, hist_out.at[pl.ds(0, 2)])
    out.wait()


def per_device(n, displacement, velocity, damage, material, damage_table, fault_rows, kernel, history):
    comps, strips, cells, nz, ny = displacement.shape
    assert cells == GROUP and comps == 2 and strips == 2
    lags = kernel.shape[0]
    length = n * cells
    f32 = jnp.float32
    u = displacement.reshape(4, cells, nz, ny)
    v = velocity.reshape(4, cells, nz, ny)
    kern = jnp.transpose(kernel, (1, 2, 3, 0)).reshape(2 * GROUP, lags)
    hist = history.reshape(lags - 1, 2 * GROUP, nz)
    table = jnp.asarray(table_of(length))

    vmem = pl.BlockSpec(memory_space=pltpu.VMEM)
    hbm = pl.BlockSpec(memory_space=pltpu.HBM)
    shaped = lambda *shape: jax.ShapeDtypeStruct(shape, f32)
    scratch = lambda *lead: pltpu.VMEM((*lead, nz, ny), f32)
    near_rows = lambda *lead: pltpu.VMEM((*lead, nz, LANES), f32)
    params = pltpu.CompilerParams(vmem_limit_bytes=40 * 1024 * 1024)

    sources = [u, v, damage, fault_rows, kern, hist, material, damage_table, table]
    held = [pltpu.VMEM(a.shape, a.dtype) for a in sources]
    *held, block = pl.pallas_call(
        functools.partial(pack_kernel, len(sources)),
        out_shape=(*held, pltpu.VMEM((1, nz, LANES), f32)),
        in_specs=[hbm] * len(sources),
        out_specs=[vmem] * (len(sources) + 1),
        scratch_shapes=[pltpu.SemaphoreType.DMA((len(sources) + 3,))],
        compiler_params=params,
    )(*(pltpu.with_memory_space_constraint(a, pltpu.HBM) for a in sources))
    u, v, damage, fault_rows, kern, hist, material, damage_table, table = held

    def exchange(a, stride):
        return lax.ppermute(a, "long", [(i, i ^ stride) for i in range(n)])

    steps = strides(n)
    gathered = jnp.concatenate([block, exchange(block, steps[0])], 0)

    halo = pltpu.VMEM((HALO_PLANES, nz, ny), f32)
    even, odd = pl.pallas_call(
        halo_kernel,
        out_shape=(halo, halo),
        in_specs=[vmem] * 4,
        out_specs=[vmem] * 2,
        compiler_params=params,
        cost_estimate=pl.CostEstimate(flops=20_000_000, bytes_accessed=1_000_000, transcendentals=0),
    )(u, v, damage, material)
    pairs = [(i, i ^ 1) for i in range(n)]
    even = lax.ppermute(even, "long", pairs)
    odd = lax.ppermute(odd, "long", [((a + 1) % n, (b + 1) % n) for a, b in pairs])

    placed = lambda *shape: pltpu.VMEM(shape, f32)
    parts = (
        placed(4, SLOTS, nz, ny), placed(2, SLOTS, nz, ny), placed(4, SLOTS, nz, ny),
        placed(2, cells, nz, ny), placed(2, cells, nz, ny),
        placed(4, cells, nz, ny), placed(4, cells, nz, ny), placed(2, cells, nz, ny),
    )
    inner = pl.pallas_call(
        inner_kernel,
        out_shape=parts,
        in_specs=[vmem] * 5,
        out_specs=[vmem] * 8,
        compiler_params=params,
        cost_estimate=pl.CostEstimate(flops=20_000_000_000, bytes_accessed=6_000_000, transcendentals=400_000),
    )(u, v, damage, material, damage_table)
    gathered = jnp.concatenate([gathered, exchange(gathered, steps[1])], 0)
    gathered, inner = lax.optimization_barrier((gathered, inner))
    for stride in steps[2:-2]:
        gathered = jnp.concatenate([gathered, exchange(gathered, stride)], 0)
    other = exchange(gathered, steps[-2])
    *_, u_far, v_far, d_far, packed, near = pl.pallas_call(
        edge_kernel,
        out_shape=(*parts, placed(PK_COUNT, nz, LANES), placed(LANES, length)),
        in_specs=[vmem] * 17,
        out_specs=[vmem] * 10,
        input_output_aliases={9 + i: i for i in range(8)},
        compiler_params=params,
        cost_estimate=pl.CostEstimate(flops=20_000_000, bytes_accessed=6_000_000, transcendentals=400_000),
    )(u, v, damage, material, damage_table, fault_rows, table, even, odd, *inner)
    gathered, packed = lax.optimization_barrier((gathered, packed))
    gathered = jnp.concatenate([gathered, other], 0)
    gathered = jnp.concatenate([gathered, exchange(gathered, steps[-1])], 0)

    u_new, v_new, d_new, hist_new = pl.pallas_call(
        functools.partial(final_kernel, n),
        out_shape=(shaped(*u.shape), shaped(*v.shape), shaped(*damage.shape), shaped(*hist.shape)),
        in_specs=[vmem] * 8,
        out_specs=[hbm] * 4,
        scratch_shapes=[
            pltpu.VMEM((16 * nz, length), f32),
            near_rows(4, cells), near_rows(4, cells), near_rows(2, cells),
            pltpu.VMEM((2, 2 * GROUP, nz), f32), pltpu.SemaphoreType.DMA((8,)),
        ],
        compiler_params=params,
    )(gathered, u_far, v_far, d_far, packed, near, table, hist)
    return (
        u_new.reshape(displacement.shape),
        v_new.reshape(velocity.shape),
        d_new,
        hist_new.reshape(history.shape),
    )


def solution(mesh):
    placed = (
        P("groups", None, "long", None, None),
        P("groups", None, "long", None, None),
        P("groups", "long", None, None),
        P("groups", "long", None, None),
        P(),
        P("groups", "long", None),
        P(None, "long", None, None),
        P("groups", "long", None, None, None),
    )
    return jax.shard_map(
        functools.partial(per_device, mesh.shape["long"]),
        mesh=mesh,
        in_specs=placed,
        out_specs=(placed[0], placed[1], placed[2], placed[7]),
        check_vma=False,
    )
```

```python
import functools
import math

import jax
import jax.numpy as jnp
import numpy as np
from jax import lax
from jax.experimental import pallas as pl
from jax.experimental.pallas import tpu as pltpu
from jax.sharding import PartitionSpec as P

DT = 0.5
EXACT = lax.Precision.HIGHEST
LANES = 128
GROUP = 8
OWNED = GROUP // 2
HALO_PLANES = 16
SLOTS = GROUP + 2


def table_of(length):
    lane = np.arange(length)
    wave = (lane // GROUP) * OWNED + lane % OWNED
    imag = (lane % GROUP) // OWNED
    phase = (np.arange(length)[:, None] * wave[None]) % length * (2.0 * np.pi / length)
    table = np.where(imag[None] == 1, -np.sin(phase), np.cos(phase)) / math.sqrt(length)
    return table.astype(np.float32)


def iota(shape, axis):
    return lax.broadcasted_iota(jnp.int32, shape, axis)


def up_z(a, fill):
    n = a.shape[0]
    return jnp.where(iota(a.shape, 0) == n - 1, fill, pltpu.roll(a, n - 1, 0))


def down_z(a, fill):
    return jnp.where(iota(a.shape, 0) == 0, fill, pltpu.roll(a, 1, 0))


def up_r(a, fill):
    n = a.shape[1]
    return jnp.where(iota(a.shape, 1) == n - 1, fill, pltpu.roll(a, n - 1, 1))


def down_r(a, fill):
    return jnp.where(iota(a.shape, 1) == 0, fill, pltpu.roll(a, 1, 1))


def fault_columns(rows_ref):
    rows = rows_ref[...].astype(jnp.float32).reshape(2 * GROUP, -1)
    nz = rows.shape[1]
    eye = (iota((nz, nz), 0) == iota((nz, nz), 1)).astype(jnp.float32)
    return lax.dot_general(eye, rows, (((1,), (1,)), ((), ())), preferred_element_type=jnp.float32)


def on_fault_plane(columns, s, x):
    nz = columns.shape[0]
    column = columns[:, s * GROUP + x : s * GROUP + x + 1]
    return jnp.broadcast_to(column, (nz, LANES)) == iota((nz, LANES), 1).astype(jnp.float32)


def k_row(lag, comp, form):
    return comp * 4 + form * 2 + lag


class Copies:
    def __init__(self, sems):
        self.sems, self.made = sems, []

    def start(self, src, dst):
        one = pltpu.make_async_copy(src, dst, self.sems.at[len(self.made)])
        one.start()
        self.made.append(one)
        return one

    def wait(self):
        for one in self.made:
            one.wait()


def pack_kernel(count, *refs):
    sources, held = refs[:count], refs[count + 1 : 2 * count + 1]
    mat_hbm, edges_ref, out_ref, sems = refs[count], *refs[2 * count + 1 :]
    loads = Copies(sems)
    rows_ref, kern_ref, hist_ref, ut, vt, dt = held
    for src, dst in zip(sources, held):
        loads.start(src, dst)
    for side, x in ((0, 0), (1, GROUP - 1)):
        loads.start(mat_hbm.at[:, x], edges_ref.at[side])
    nz = ut.shape[2]
    near = slice(0, LANES)
    for one in loads.made[:3]:
        one.wait()

    kern = kern_ref[...]
    count = kern.shape[0]
    real_row = (iota(kern.shape, 0) // 2) % 2 == 0
    from_next = pltpu.roll(kern, count - 2, 0)
    a_rows = jnp.where(real_row, kern, pltpu.roll(kern, 2, 0))
    b_rows = jnp.where(real_row, -from_next, kern)
    b_source = jnp.where(real_row, from_next, -kern)
    parts = []
    lags = hist_ref.shape[0] + 1
    for skip in (1, 2):
        straight = jnp.zeros((count, nz), jnp.float32)
        crossed = jnp.zeros((count, nz), jnp.float32)
        for l in range(skip, lags):
            straight += a_rows[:, l : l + 1] * hist_ref[l - skip]
            crossed += b_source[:, l : l + 1] * hist_ref[l - skip]
        real_here = (iota((count, nz), 0) // 2) % 2 == 0
        swapped = jnp.where(real_here, pltpu.roll(crossed, count - 2, 0), pltpu.roll(crossed, 2, 0))
        parts.append(straight + swapped)
    square = (count, nz)
    coefficients = jnp.zeros(square, jnp.float32)
    for c in range(2):
        for form, rows in enumerate((a_rows, b_rows)):
            for l in (0, 1):
                here = (iota(square, 0) % 2 == c) & (iota(square, 1) == k_row(l, c, form))
                coefficients = jnp.where(here, rows[:, l : l + 1], coefficients)
    parts.append(coefficients)
    stacked = jnp.concatenate(parts, 0)
    total = stacked.shape[0]
    row = iota((total, LANES), 0)
    start = jnp.where(row < 32, 32 + (row // 16) * 16 + (row % 2) * GROUP, LANES - GROUP)
    target = start + ((row // 2) % 2) * OWNED + (row // 4) % OWNED
    place = (target == iota((total, LANES), 1)).astype(jnp.float32)
    out = lax.dot_general(
        stacked, place, (((0,), (0,)), ((), ())), precision=EXACT, preferred_element_type=jnp.float32
    )

    lane = iota((nz, LANES), 1)
    columns = fault_columns(rows_ref)
    faults = [[on_fault_plane(columns, s, x) for x in range(GROUP)] for s in range(2)]
    zero = jnp.zeros((nz, LANES), jnp.float32)
    for one in loads.made[3:]:
        one.wait()
    for x in range(GROUP):
        slip = [zero, zero]
        ahead = [zero, zero]
        for s in range(2):
            fault = faults[s][x]
            c0 = 1.0 - dt[s, x, :, near]
            bars = []
            if x > 0:
                bars.append((x - 1, 0.5 * (c0 + (1.0 - dt[s, x - 1, :, near]))))
            if x < GROUP - 1:
                bars.append((x + 1, 0.5 * (c0 + (1.0 - dt[s, x + 1, :, near]))))
            bar_zu = 0.5 * (c0 + up_z(c0, c0))
            bar_zd = 0.5 * (c0 + down_z(c0, c0))
            bar_ru = 0.5 * (c0 + up_r(c0, c0))
            bar_rd = 0.5 * (c0 + down_r(c0, c0))
            for c in range(2):
                u0 = ut[c * 2 + s, x, :, near]
                force = bar_zu * (up_z(u0, 0.0) - u0) + bar_zd * (down_z(u0, 0.0) - u0)
                force += bar_ru * (up_r(u0, 0.0) - u0) + bar_rd * (down_r(u0, 0.0) - u0)
                for other, bar in bars:
                    force += bar * (ut[c * 2 + s, other, :, near] - u0)
                later = u0 + DT * (vt[c * 2 + s, x, :, near] + DT * force)
                sign = 1.0 if s == 1 else -1.0
                slip[c] += jnp.where(fault, sign * u0, 0.0)
                ahead[c] += jnp.where(fault, sign * later, 0.0)
            if x in (0, GROUP - 1):
                side = 0 if x == 0 else 1
                moves = [(64 + side * 16 + s * 8 + c * 4, ut[c * 2 + s, x, :, near]) for c in range(2)]
                moves.append((96 + side * 8 + s * 4, c0))
                for at, plane in moves:
                    out = jnp.where((lane >= at) & (lane < at + 4), pltpu.roll(plane, at, 1), out)
                column = columns[:, s * GROUP + x : s * GROUP + x + 1]
                out = jnp.where(lane == 112 + side * 2 + s, column, out)
        for c in range(2):
            out = jnp.where(lane == c * GROUP + x, jnp.sum(slip[c], 1, keepdims=True), out)
            out = jnp.where(lane == 16 + c * GROUP + x, jnp.sum(ahead[c], 1, keepdims=True), out)
    out_ref[0] = out


TILE = 8


class Plane:
    def __init__(self, tiles):
        self.tiles = tiles

    @classmethod
    def load(cls, ref, *index):
        nz, ny = ref.shape[-2:]
        return cls([
            [ref[(*index, slice(i, i + TILE), slice(j, j + LANES))] for j in range(0, ny, LANES)]
            for i in range(0, nz, TILE)
        ])

    def store(self, ref, *index):
        for i, line in enumerate(self.tiles):
            for j, tile in enumerate(line):
                ref[(*index, slice(i * TILE, (i + 1) * TILE), slice(j * LANES, (j + 1) * LANES))] = tile

    def map(self, function, *others):
        return Plane([
            [function(tile, *(other.tiles[i][j] for other in others)) for j, tile in enumerate(line)]
            for i, line in enumerate(self.tiles)
        ])

    def __add__(self, other):
        return self.map(lambda a, b: a + b, other)

    def __sub__(self, other):
        return self.map(lambda a, b: a - b, other)

    def __mul__(self, other):
        if isinstance(other, Plane):
            return self.map(lambda a, b: a * b, other)
        return self.map(lambda a: a * other)

    def moved(self, axis, step, zero):
        lines = self.tiles if axis == 1 else [list(line) for line in zip(*self.tiles)]
        size = LANES if axis == 1 else TILE
        shape = lines[0][0].shape
        end = iota(shape, axis) == (size - 1 if step == 1 else 0)
        result = []
        for line in lines:
            turned = [pltpu.roll(tile, size - 1 if step == 1 else 1, axis) for tile in line]
            new = []
            for k, tile in enumerate(line):
                inside = 0 <= k + step < len(line)
                new.append(jnp.where(end, turned[k + step] if inside else (0.0 if zero else tile), turned[k]))
            result.append(new)
        return Plane(result if axis == 1 else [list(line) for line in zip(*result)])

    def beside(self, zero):
        return [self.moved(axis, step, zero) for axis in (0, 1) for step in (1, -1)]


def total(planes):
    result = planes[0]
    for one in planes[1:]:
        result = result + one
    return result


def squared(a):
    return a * a


def stencil(u, c):
    cm, c0, cp = c
    bars = [c0 + one for one in [cp, cm] + c0.beside(False)]
    forces, gradients = [], []
    for um, u0, up in u:
        near = [up, um] + u0.beside(True)
        forces.append(total([bar * (one - u0) for bar, one in zip(bars, near)]))
        gradients += [squared(near[k] - near[k + 1]) for k in range(0, 6, 2)]
    return forces, total(gradients) * 0.25


def classed(classes, table_ref):
    def entry(row, level):
        return jnp.broadcast_to(table_ref[row : row + 1, level : level + 1], classes.shape)

    rate, limit = entry(0, 0), entry(1, 0)
    for level in range(1, table_ref.shape[1]):
        here = classes == level
        rate = jnp.where(here, entry(0, level), rate)
        limit = jnp.where(here, entry(1, level), limit)
    return rate, limit


def decay(rate, limit, energy):
    over = energy - limit
    soft = jnp.maximum(over, 0.0) + jnp.log(1.0 + jnp.exp(-jnp.abs(over)))
    return jnp.exp(-rate * soft)


PK_U, PK_C, PK_V, PK_RATE, PK_LIMIT, PK_FAULT, PK_COUNT = 0, 4, 6, 10, 12, 14, 16


def strides(n):
    far = [(1 << i) | 1 for i in reversed(range(1, n.bit_length() - 1))]
    return far[-1:] + far[:-1] + [1]


def halo_kernel(u_ref, v_ref, d_ref, edges_ref, even_ref, odd_ref):
    parity = lax.rem(lax.axis_index("long"), 2)
    for ref, right in ((even_ref, 1 - parity), (odd_ref, parity)):
        edge, behind = right * (GROUP - 1), 1 + right * (GROUP - 3)
        for s in range(2):
            d0 = Plane.load(d_ref, s, edge)
            d0.store(ref, 8 + s)
            Plane.load(edges_ref, right, s).map(lambda a: a.astype(jnp.float32)).store(ref, 14 + s)
            c0, c1 = (a.map(lambda b: 1.0 - b) for a in (d0, Plane.load(d_ref, s, behind)))
            bars = [c0 + one for one in [c1] + c0.beside(False)]
            for comp in range(2):
                i = comp * 2 + s
                u0, u1 = Plane.load(u_ref, i, edge), Plane.load(u_ref, i, behind)
                u0.store(ref, i)
                u1.store(ref, 4 + i)
                force = total([bar * (one - u0) for bar, one in zip(bars, [u1] + u0.beside(True))])
                (u0 + (Plane.load(v_ref, i, edge) + force * (0.5 * DT)) * DT).store(ref, 10 + i)


def place_apart(apart, n):
    at, core = 0, apart & 1
    for i, stride in enumerate(strides(n)[:-1]):
        bit = (apart >> (stride.bit_length() - 1)) & 1
        at, core = at | (bit << i), core ^ bit
    return at | (core << (n.bit_length() - 2))


def second_step(x, u1, c1, v1, rates, limits, uo, vo, do):
    for s in range(2):
        c = [Plane.load(c1, s, x + k) for k in range(3)]
        u = [[Plane.load(u1, comp * 2 + s, x + k) for k in range(3)] for comp in range(2)]
        forces, energy = stencil(u, c)
        left = Plane.load(rates, s, x).map(decay, Plane.load(limits, s, x), energy)
        c[1].map(lambda a, b: 1.0 - a * b, left).store(do, s, x)
        for comp in range(2):
            i = comp * 2 + s
            v_new = Plane.load(v1, i, x) + forces[comp] * (0.5 * DT)
            v_new.store(vo, i, x)
            (u[comp][1] + v_new * DT).store(uo, i, x)


def inner_kernel(
    u_ref, v_ref, d_ref, rows_ref, mat_hbm, tab_hbm, table_hbm,
    u1, c1, v1, rates, limits, uo, vo, do, packed, mat, tab_ref, table, near, sems,
):
    loads = Copies(sems)
    for src, dst in ((mat_hbm, mat), (tab_hbm, tab_ref), (table_hbm, table)):
        loads.start(src, dst)
    pos = lax.axis_index("long")
    nz = u_ref.shape[2]
    lane = iota((nz, LANES), 1)
    columns = fault_columns(rows_ref)
    spread = iota((columns.shape[1], LANES), 0)
    wide = iota((columns.shape[1], LANES), 1)
    for s in range(2):
        pick = (spread == s * GROUP + wide // GROUP - 1) & (wide >= GROUP) & (wide < (GROUP + 1) * GROUP)
        rows = jnp.dot(columns, pick.astype(jnp.float32), preferred_element_type=jnp.float32)
        inside = (lane >= GROUP) & (lane < (GROUP + 1) * GROUP)
        hit = inside & (rows == (lane % GROUP).astype(jnp.float32))
        packed[PK_FAULT + s] = hit.astype(jnp.float32)
    loads.wait()
    length = table.shape[0]
    near[...] = jnp.zeros(near.shape, jnp.float32)
    for slot in range(SLOTS):
        x = lax.rem(pos * GROUP + (length - 1 + slot), length)
        near[slot * GROUP : (slot + 1) * GROUP, :] = jnp.broadcast_to(table[pl.ds(x, 1), :], (GROUP, length))

    def stiff(s, x):
        return Plane.load(d_ref, s, x).map(lambda a: 1.0 - a)

    def first_step(x):
        for s in range(2):
            c = [stiff(s, x + k) for k in (-1, 0, 1)]
            u = [[Plane.load(u_ref, comp * 2 + s, x + k) for k in (-1, 0, 1)] for comp in range(2)]
            finish_first(s, x, c, u, Plane.load(mat, s, x), v_ref, x, tab_ref, u1, c1, v1, rates, limits)

    @pl.loop(0, (GROUP - 2) // 2)
    def _(k):
        first_step(2 * k + 1)
        first_step(2 * k + 2)

    @pl.loop(0, (GROUP - 4) // 2)
    def _(k):
        second_step(2 * k + 2, u1, c1, v1, rates, limits, uo, vo, do)
        second_step(2 * k + 3, u1, c1, v1, rates, limits, uo, vo, do)

    pack_slots(packed, u1, c1, v1, rates, limits, range(2, GROUP), True)


def pack_slots(packed, u1, c1, v1, rates, limits, slots, fresh):
    nz = u1.shape[2]
    group = iota((nz, LANES), 1) // GROUP

    def pack(plane, ref, i, first_slot):
        result = jnp.zeros((nz, LANES), jnp.float32) if fresh else packed[plane]
        for slot in slots:
            if 0 <= slot - first_slot < ref.shape[1]:
                value = ref[i, slot - first_slot, :, 0:LANES]
                result = jnp.where(group == slot, pltpu.roll(value, slot * GROUP, 1) if slot else value, result)
        packed[plane] = result

    for i in range(4):
        pack(PK_U + i, u1, i, 0)
        pack(PK_V + i, v1, i, 1)
    for s in range(2):
        pack(PK_C + s, c1, s, 0)
        pack(PK_RATE + s, rates, s, 1)
        pack(PK_LIMIT + s, limits, s, 1)


def finish_first(s, x, c, u, classes, v_now, v_at, tab_ref, u1, c1, v1, rates, limits):
    slot = x + 1
    forces, energy = stencil(u, c)
    both = classes.map(lambda a: classed(a, tab_ref))
    rate, limit = both.map(lambda a: a[0]), both.map(lambda a: a[1])
    (c[1] * rate.map(decay, limit, energy)).store(c1, s, slot)
    rate.store(rates, s, x)
    limit.store(limits, s, x)
    for comp in range(2):
        i = comp * 2 + s
        v_new = Plane.load(v_now, i, v_at) + forces[comp] * (0.5 * DT)
        v_new.store(v1, i, x)
        (u[comp][1] + v_new * DT).store(u1, i, slot)


def edge_kernel(
    u_ref, v_ref, d_ref, mat, tab_ref, even_ref, odd_ref, *refs,
):
    u1, c1, v1, rates, limits, uo, vo, do, packed = refs[9:]
    pos = lax.axis_index("long")
    even_pos = lax.rem(pos, 2) == 0

    def halo(side, plane):
        pick = even_pos == (side == 1)
        return Plane.load(even_ref, plane).map(lambda a, b: jnp.where(pick, a, b), Plane.load(odd_ref, plane))

    def of_damage(plane):
        return plane.map(lambda a: 1.0 - a)

    for side, x in ((0, 0), (1, GROUP - 1)):
        inner_x = 1 if x == 0 else x - 1
        for s in range(2):
            c = [of_damage(Plane.load(d_ref, s, inner_x)), of_damage(Plane.load(d_ref, s, x)), of_damage(halo(side, 8 + s))]
            u = [[Plane.load(u_ref, i, inner_x), Plane.load(u_ref, i, x), halo(side, i)] for i in (s, 2 + s)]
            finish_first(s, x, c, u, Plane.load(mat, s, x), v_ref, x, tab_ref, u1, c1, v1, rates, limits)
            slot = (GROUP + 1) * side
            both = halo(side, 14 + s).map(lambda a: classed(a.astype(jnp.int32), tab_ref))
            rate, limit = both.map(lambda a: a[0]), both.map(lambda a: a[1])
            gradients = []
            for comp, (_, own, other) in enumerate(u):
                i = comp * 2 + s
                near_u = [halo(side, 4 + i), own] + other.beside(True)
                gradients += [squared(near_u[k] - near_u[k + 1]) for k in range(0, 6, 2)]
                force = (c[1] + c[2]) * (own - other)
                (halo(side, 10 + i) + force * (0.5 * DT * DT)).store(u1, i, slot)
            (c[2] * rate.map(decay, limit, total(gradients) * 0.25)).store(c1, s, slot)
    for x in (0, 1, GROUP - 2, GROUP - 1):
        second_step(x, u1, c1, v1, rates, limits, uo, vo, do)

    pack_slots(packed, u1, c1, v1, rates, limits, (0, 1, GROUP, GROUP + 1), False)


def split_dot(a, b, contract):
    halves = []
    for one in (a, b):
        high = one.astype(jnp.bfloat16)
        halves.append((high, (one - high.astype(jnp.float32)).astype(jnp.bfloat16)))
    (ah, al), (bh, bl) = halves
    dims = (((1,), (contract,)), ((), ()))
    products = [
        lax.dot_general(x, y, dims, preferred_element_type=jnp.float32) for x, y in ((ah, bl), (al, bh), (ah, bh))
    ]
    return products[0] + products[1] + products[2]


def regroup(blocks):
    lane = iota(blocks[0].shape, 1) // GROUP
    for bit in (1, 2, 4, 8):
        low = (lane & bit) == 0
        new = list(blocks)
        for i in range(16):
            if i & bit == 0:
                a, b = blocks[i], blocks[i | bit]
                new[i] = jnp.where(low, a, pltpu.roll(b, bit * GROUP, 1))
                new[i | bit] = jnp.where(low, pltpu.roll(a, LANES - bit * GROUP, 1), b)
        blocks = new
    return blocks


def swap_parts(a):
    n = a.shape[1]
    return jnp.where(
        iota(a.shape, 1) % GROUP < OWNED, pltpu.roll(a, n - OWNED, 1), pltpu.roll(a, OWNED, 1)
    )


def final_kernel(
    n, gathered, uo, vo, do, packed, near, table, hist_ref,
    u_out, v_out, d_out, hist_out,
    spread, ut, vt, dt, hist_new, sems,
):
    out = Copies(sems)
    first, far = pl.ds(0, LANES), pl.ds(LANES, uo.shape[3] - LANES)
    for ref, dst in ((uo, u_out), (vo, v_out), (do, d_out)):
        out.start(ref.at[:, :, :, far], dst.at[:, :, :, far])
    kept = hist_ref.shape[0] - 2
    out.start(hist_ref.at[pl.ds(0, kept)], hist_out.at[pl.ds(2, kept)])
    pos = lax.axis_index("long")
    nz = gathered.shape[1]
    length = n * GROUP
    lane = iota((nz, LANES), 1)

    here = place_apart(pos, n)

    def block_of(device):
        return gathered[jnp.bitwise_xor(here, place_apart(device, n))]

    for t in range(length // LANES):
        at = slice(t * LANES, (t + 1) * LANES)
        for g, block in enumerate(regroup([block_of(t * 16 + d) for d in range(16)])):
            spread[g * nz : (g + 1) * nz, at] = block

    def group(g):
        return spread[g * nz : (g + 1) * nz, :]

    full = iota((nz, length), 1)

    def stiff(side, s):
        plane = group(12 + side)
        first_half = full % GROUP < 4
        if s == 0:
            return jnp.where(first_half, plane, pltpu.roll(plane, 4, 1))
        return jnp.where(first_half, pltpu.roll(plane, length - 4, 1), plane)

    def on_edge(side, s):
        j = side * 2 + s
        row = pltpu.roll(group(14), length - j, 1) if j else group(14)
        row = jnp.where(full % GROUP == 0, row, 0.0)
        for step in (1, 2, 4):
            row += pltpu.roll(row, step, 1)
        return row == (full % 4).astype(jnp.float32)

    adds = []
    for s in range(2):
        next_u = pltpu.roll(group(8 + s), length - GROUP, 1)
        next_c = pltpu.roll(stiff(0, s), length - GROUP, 1)
        flux = (0.5 * (stiff(1, s) + next_c)) * (next_u - group(10 + s))
        flux = (DT * DT if s == 1 else -DT * DT) * flux
        adds.append((
            jnp.where(on_edge(1, s), flux, 0.0), jnp.where(on_edge(0, s), pltpu.roll(-flux, GROUP, 1), 0.0)
        ))
    for side, x in ((0, GROUP - 1), (1, 0)):
        total = adds[0][side] + adds[1][side]
        total += pltpu.roll(total, length - 1, 1)
        total += pltpu.roll(total, length - 2, 1)
        for c in range(2):
            moved = pltpu.roll(total, (x - c * 4) % length, 1)
            spread[(2 + c) * nz : (3 + c) * nz, :] += jnp.where(full % GROUP == x, moved, 0.0)

    both = 2 * nz
    spectra = split_dot(spread[0 : 2 * both, :], table[...], 0)
    first_now = spectra[0:both]
    hist1, hist2 = (spread[i * both : (i + 1) * both, :] for i in (2, 3))

    def factor(lag, form):
        rows = [15 * nz + k_row(lag, c, form) for c in range(2)]
        return jnp.concatenate(
            [jnp.broadcast_to(spread[row : row + 1, :], (nz, length)) for row in rows], 0
        )

    k0r, k0i, k1r, k1i = factor(0, 0), factor(0, 1), factor(1, 0), factor(1, 1)
    swapped = swap_parts(first_now)
    traction1 = hist1 + k0r * first_now + k0i * swapped
    wide = iota((both, length), 1)
    kept = jnp.where(wide == OWNED, 0.0, traction1)
    second_now = spectra[both : 2 * both] - (2.0 * DT * DT) * kept
    traction2 = hist2 + k1r * first_now + k1i * swapped + k0r * second_now + k0i * swap_parts(second_now)
    weight = jnp.where((wide // GROUP == 0) & (wide % OWNED == 0), 1.0, 2.0)
    weighted = jnp.concatenate([weight * traction1, weight * traction2], 0)
    tractions = split_dot(weighted, near[...], 1)

    u_now, v_now, c_now, faults = [], [], [], []
    for s in range(2):
        before = block_of(lax.rem(pos + n - 1, n))[:, 114 + s : 115 + s]
        after = block_of(lax.rem(pos + 1, n))[:, 112 + s : 113 + s]
        row = (lane % GROUP).astype(jnp.float32)
        fault = packed[PK_FAULT + s]
        fault = jnp.where(lane // GROUP == 0, (row == before).astype(jnp.float32), fault)
        fault = jnp.where(lane // GROUP == GROUP + 1, (row == after).astype(jnp.float32), fault)
        faults.append(fault if s == 0 else -fault)
        c_now.append(packed[PK_C + s])
    for i in range(4):
        c, s = i // 2, i % 2
        push = DT * tractions[c * nz : (c + 1) * nz] * faults[s]
        v_now.append(packed[PK_V + i] + push)
        u_now.append(packed[PK_U + i] + DT * push)

    low_row = lane % GROUP == 0

    def around(a, fill):
        return (
            pltpu.roll(a, LANES - GROUP, 1), pltpu.roll(a, GROUP, 1),
            up_z(a, fill), down_z(a, fill),
            pltpu.roll(a, LANES - 1, 1), jnp.where(low_row, fill, pltpu.roll(a, 1, 1)),
        )

    results = {}
    for s in range(2):
        c0 = c_now[s]
        bars = [0.5 * (c0 + one) for one in around(c0, c0)]
        quarter = jnp.zeros((nz, LANES), jnp.float32)
        for c in range(2):
            i = c * 2 + s
            u0 = u_now[i]
            steps = [one - u0 for one in around(u0, 0.0)]
            force = bars[0] * steps[0]
            for bar, step in zip(bars[1:], steps[1:]):
                force += bar * step
            for k in range(3):
                gradient = steps[2 * k] - steps[2 * k + 1]
                quarter += gradient * gradient
            at = (2 + c) * nz
            v_new = v_now[i] + DT * (force + tractions[at : at + nz] * faults[s])
            results["v", i] = v_new
            results["u", i] = u0 + DT * v_new
        results["d", s] = 1.0 - c0 * decay(packed[PK_RATE + s], packed[PK_LIMIT + s], 0.25 * quarter)

    changed = lane < 5
    for name, count, old, ref, dst in (
        ("u", 4, uo, ut, u_out), ("v", 4, vo, vt, v_out), ("d", 2, do, dt, d_out)
    ):
        for i in range(count):
            for x in range(GROUP):
                moved = pltpu.roll(results[name, i], LANES - (x + 1) * GROUP, 1)
                ref[i, x] = jnp.where(changed, moved, old[i, x, :, 0:LANES])
        out.start(ref, dst.at[:, :, :, first])

    rows = 2 * GROUP
    row = iota((rows, length), 0)
    target = pos * GROUP + ((row // 2) % 2) * OWNED + row // 4
    for step, now in ((1, first_now), (0, second_now)):
        total = jnp.zeros((rows, nz), jnp.float32)
        for c in range(2):
            pick = ((target == iota((rows, length), 1)) & (row % 2 == c)).astype(jnp.float32)
            total += lax.dot_general(
                pick, now[c * nz : (c + 1) * nz], (((1,), (1,)), ((), ())),
                precision=EXACT, preferred_element_type=jnp.float32,
            )
        hist_new[step] = total
    out.start(hist_new, hist_out.at[pl.ds(0, 2)])
    out.wait()


def per_device(n, displacement, velocity, damage, material, damage_table, fault_rows, kernel, history):
    comps, strips, cells, nz, ny = displacement.shape
    assert cells == GROUP and comps == 2 and strips == 2
    lags = kernel.shape[0]
    length = n * cells
    f32 = jnp.float32
    u = displacement.reshape(4, cells, nz, ny)
    v = velocity.reshape(4, cells, nz, ny)
    kern = jnp.transpose(kernel, (1, 2, 3, 0)).reshape(2 * GROUP, lags)
    hist = history.reshape(lags - 1, 2 * GROUP, nz)
    table = jnp.asarray(table_of(length))

    vmem = pl.BlockSpec(memory_space=pltpu.VMEM)
    hbm = pl.BlockSpec(memory_space=pltpu.HBM)
    shaped = lambda *shape: jax.ShapeDtypeStruct(shape, f32)
    scratch = lambda *lead: pltpu.VMEM((*lead, nz, ny), f32)
    near_rows = lambda *lead: pltpu.VMEM((*lead, nz, LANES), f32)
    params = pltpu.CompilerParams(vmem_limit_bytes=40 * 1024 * 1024)

    def at_rest(*arrays):
        return [pltpu.with_memory_space_constraint(a, pltpu.HBM) for a in arrays]

    sources = [fault_rows, kern, hist, u, v, damage]
    held = [pltpu.VMEM(a.shape, a.dtype) for a in sources]
    *held, edges, block = pl.pallas_call(
        functools.partial(pack_kernel, len(sources)),
        out_shape=(*held, pltpu.VMEM((2, 2, nz, ny), jnp.int32), pltpu.VMEM((1, nz, LANES), f32)),
        in_specs=[hbm] * (len(sources) + 1),
        out_specs=[vmem] * (len(sources) + 2),
        scratch_shapes=[pltpu.SemaphoreType.DMA((len(sources) + 2,))],
        compiler_params=params,
    )(*at_rest(*sources, material))
    fault_rows, kern, hist, u, v, damage = held

    def exchange(a, stride):
        return lax.ppermute(a, "long", [(i, i ^ stride) for i in range(n)])

    steps = strides(n)
    gathered = jnp.concatenate([block, exchange(block, steps[0])], 0)

    halo = pltpu.VMEM((HALO_PLANES, nz, ny), f32)
    even, odd = pl.pallas_call(
        halo_kernel,
        out_shape=(halo, halo),
        in_specs=[vmem] * 4,
        out_specs=[vmem] * 2,
        compiler_params=params,
        cost_estimate=pl.CostEstimate(flops=20_000_000, bytes_accessed=1_000_000, transcendentals=0),
    )(u, v, damage, edges)
    pairs = [(i, i ^ 1) for i in range(n)]
    even = lax.ppermute(even, "long", pairs)
    odd = lax.ppermute(odd, "long", [((a + 1) % n, (b + 1) % n) for a, b in pairs])

    placed = lambda *shape: pltpu.VMEM(shape, f32)
    parts = (
        placed(4, SLOTS, nz, ny), placed(2, SLOTS, nz, ny), placed(4, cells, nz, ny),
        placed(2, cells, nz, ny), placed(2, cells, nz, ny),
        placed(4, cells, nz, ny), placed(4, cells, nz, ny), placed(2, cells, nz, ny),
        placed(PK_COUNT, nz, LANES),
    )
    *inner, material, damage_table, table, near = pl.pallas_call(
        inner_kernel,
        out_shape=(
            *parts, pltpu.VMEM(material.shape, jnp.int32), placed(*damage_table.shape),
            placed(length, length), placed(LANES, length),
        ),
        in_specs=[vmem] * 4 + [hbm] * 3,
        out_specs=[vmem] * 13,
        scratch_shapes=[pltpu.SemaphoreType.DMA((3,))],
        compiler_params=params,
        cost_estimate=pl.CostEstimate(flops=20_000_000_000, bytes_accessed=6_000_000, transcendentals=400_000),
    )(u, v, damage, fault_rows, *at_rest(material, damage_table, table))
    gathered = jnp.concatenate([gathered, exchange(gathered, steps[1])], 0)
    gathered, inner = lax.optimization_barrier((gathered, inner))
    for stride in steps[2:-2]:
        gathered = jnp.concatenate([gathered, exchange(gathered, stride)], 0)
    other = exchange(gathered, steps[-2])
    *_, u_far, v_far, d_far, packed = pl.pallas_call(
        edge_kernel,
        out_shape=parts,
        in_specs=[vmem] * 16,
        out_specs=[vmem] * 9,
        input_output_aliases={7 + i: i for i in range(9)},
        compiler_params=params,
        cost_estimate=pl.CostEstimate(flops=20_000_000, bytes_accessed=6_000_000, transcendentals=400_000),
    )(u, v, damage, material, damage_table, even, odd, *inner)
    gathered, packed = lax.optimization_barrier((gathered, packed))
    gathered = jnp.concatenate([gathered, other], 0)
    gathered = jnp.concatenate([gathered, exchange(gathered, steps[-1])], 0)

    u_new, v_new, d_new, hist_new = pl.pallas_call(
        functools.partial(final_kernel, n),
        out_shape=(shaped(*u.shape), shaped(*v.shape), shaped(*damage.shape), shaped(*hist.shape)),
        in_specs=[vmem] * 8,
        out_specs=[hbm] * 4,
        scratch_shapes=[
            pltpu.VMEM((16 * nz, length), f32),
            near_rows(4, cells), near_rows(4, cells), near_rows(2, cells),
            pltpu.VMEM((2, 2 * GROUP, nz), f32), pltpu.SemaphoreType.DMA((8,)),
        ],
        compiler_params=params,
    )(gathered, u_far, v_far, d_far, packed, near, table, hist)
    return (
        u_new.reshape(displacement.shape),
        v_new.reshape(velocity.shape),
        d_new,
        hist_new.reshape(history.shape),
    )


def solution(mesh):
    placed = (
        P("groups", None, "long", None, None),
        P("groups", None, "long", None, None),
        P("groups", "long", None, None),
        P("groups", "long", None, None),
        P(),
        P("groups", "long", None),
        P(None, "long", None, None),
        P("groups", "long", None, None, None),
    )
    return jax.shard_map(
        functools.partial(per_device, mesh.shape["long"]),
        mesh=mesh,
        in_specs=placed,
        out_specs=(placed[0], placed[1], placed[2], placed[7]),
        check_vma=False,
    )
```

```python
import functools
import math

import jax
import jax.numpy as jnp
import numpy as np
from jax import lax
from jax.experimental import pallas as pl
from jax.experimental.pallas import tpu as pltpu
from jax.sharding import PartitionSpec as P

DT = 0.5
EXACT = lax.Precision.HIGHEST
LANES = 128
GROUP = 8
OWNED = GROUP // 2
HALO_PLANES = 16
SLOTS = GROUP + 2


def table_of(length):
    lane = np.arange(length)
    wave = (lane // GROUP) * OWNED + lane % OWNED
    imag = (lane % GROUP) // OWNED
    phase = (np.arange(length)[:, None] * wave[None]) % length * (2.0 * np.pi / length)
    table = np.where(imag[None] == 1, -np.sin(phase), np.cos(phase)) / math.sqrt(length)
    return table.astype(np.float32)


def iota(shape, axis):
    return lax.broadcasted_iota(jnp.int32, shape, axis)


def up_z(a, fill):
    n = a.shape[0]
    return jnp.where(iota(a.shape, 0) == n - 1, fill, pltpu.roll(a, n - 1, 0))


def down_z(a, fill):
    return jnp.where(iota(a.shape, 0) == 0, fill, pltpu.roll(a, 1, 0))


def up_r(a, fill):
    n = a.shape[1]
    return jnp.where(iota(a.shape, 1) == n - 1, fill, pltpu.roll(a, n - 1, 1))


def down_r(a, fill):
    return jnp.where(iota(a.shape, 1) == 0, fill, pltpu.roll(a, 1, 1))


def fault_columns(rows_ref):
    rows = rows_ref[...].astype(jnp.float32).reshape(2 * GROUP, -1)
    nz = rows.shape[1]
    eye = (iota((nz, nz), 0) == iota((nz, nz), 1)).astype(jnp.float32)
    return lax.dot_general(eye, rows, (((1,), (1,)), ((), ())), preferred_element_type=jnp.float32)


def on_fault_plane(columns, s, x):
    nz = columns.shape[0]
    column = columns[:, s * GROUP + x : s * GROUP + x + 1]
    return jnp.broadcast_to(column, (nz, LANES)) == iota((nz, LANES), 1).astype(jnp.float32)


def k_row(lag, comp, form):
    return comp * 4 + form * 2 + lag


class Copies:
    def __init__(self, sems):
        self.sems, self.made = sems, []

    def start(self, src, dst):
        one = pltpu.make_async_copy(src, dst, self.sems.at[len(self.made)])
        one.start()
        self.made.append(one)
        return one

    def wait(self):
        for one in self.made:
            one.wait()


def pack_kernel(count, *refs):
    sources, held = refs[:count], refs[count + 1 : 2 * count + 1]
    mat_hbm, edges_ref, out_ref, sems = refs[count], *refs[2 * count + 1 :]
    loads = Copies(sems)
    rows_ref, kern_ref, hist_ref, ut, vt, dt = held
    for src, dst in zip(sources, held):
        loads.start(src, dst)
    for side, x in ((0, 0), (1, GROUP - 1)):
        loads.start(mat_hbm.at[:, x], edges_ref.at[side])
    nz = ut.shape[2]
    near = slice(0, LANES)
    for one in loads.made[:3]:
        one.wait()

    kern = kern_ref[...]
    count = kern.shape[0]
    real_row = (iota(kern.shape, 0) // 2) % 2 == 0
    from_next = pltpu.roll(kern, count - 2, 0)
    a_rows = jnp.where(real_row, kern, pltpu.roll(kern, 2, 0))
    b_rows = jnp.where(real_row, -from_next, kern)
    b_source = jnp.where(real_row, from_next, -kern)
    parts = []
    lags = hist_ref.shape[0] + 1
    for skip in (1, 2):
        straight = jnp.zeros((count, nz), jnp.float32)
        crossed = jnp.zeros((count, nz), jnp.float32)
        for l in range(skip, lags):
            straight += a_rows[:, l : l + 1] * hist_ref[l - skip]
            crossed += b_source[:, l : l + 1] * hist_ref[l - skip]
        real_here = (iota((count, nz), 0) // 2) % 2 == 0
        swapped = jnp.where(real_here, pltpu.roll(crossed, count - 2, 0), pltpu.roll(crossed, 2, 0))
        parts.append(straight + swapped)
    square = (count, nz)
    coefficients = jnp.zeros(square, jnp.float32)
    for c in range(2):
        for form, rows in enumerate((a_rows, b_rows)):
            for l in (0, 1):
                here = (iota(square, 0) % 2 == c) & (iota(square, 1) == k_row(l, c, form))
                coefficients = jnp.where(here, rows[:, l : l + 1], coefficients)
    parts.append(coefficients)
    stacked = jnp.concatenate(parts, 0)
    total = stacked.shape[0]
    row = iota((total, LANES), 0)
    start = jnp.where(row < 32, 32 + (row // 16) * 16 + (row % 2) * GROUP, LANES - GROUP)
    target = start + ((row // 2) % 2) * OWNED + (row // 4) % OWNED
    place = (target == iota((total, LANES), 1)).astype(jnp.float32)
    out = lax.dot_general(
        stacked, place, (((0,), (0,)), ((), ())), precision=EXACT, preferred_element_type=jnp.float32
    )

    lane = iota((nz, LANES), 1)
    columns = fault_columns(rows_ref)
    faults = [[on_fault_plane(columns, s, x) for x in range(GROUP)] for s in range(2)]
    zero = jnp.zeros((nz, LANES), jnp.float32)
    for one in loads.made[3:]:
        one.wait()
    for x in range(GROUP):
        slip = [zero, zero]
        ahead = [zero, zero]
        for s in range(2):
            fault = faults[s][x]
            c0 = 1.0 - dt[s, x, :, near]
            bars = []
            if x > 0:
                bars.append((x - 1, 0.5 * (c0 + (1.0 - dt[s, x - 1, :, near]))))
            if x < GROUP - 1:
                bars.append((x + 1, 0.5 * (c0 + (1.0 - dt[s, x + 1, :, near]))))
            bar_zu = 0.5 * (c0 + up_z(c0, c0))
            bar_zd = 0.5 * (c0 + down_z(c0, c0))
            bar_ru = 0.5 * (c0 + up_r(c0, c0))
            bar_rd = 0.5 * (c0 + down_r(c0, c0))
            for c in range(2):
                u0 = ut[c * 2 + s, x, :, near]
                force = bar_zu * (up_z(u0, 0.0) - u0) + bar_zd * (down_z(u0, 0.0) - u0)
                force += bar_ru * (up_r(u0, 0.0) - u0) + bar_rd * (down_r(u0, 0.0) - u0)
                for other, bar in bars:
                    force += bar * (ut[c * 2 + s, other, :, near] - u0)
                later = u0 + DT * (vt[c * 2 + s, x, :, near] + DT * force)
                sign = 1.0 if s == 1 else -1.0
                slip[c] += jnp.where(fault, sign * u0, 0.0)
                ahead[c] += jnp.where(fault, sign * later, 0.0)
            if x in (0, GROUP - 1):
                side = 0 if x == 0 else 1
                moves = [(64 + side * 16 + s * 8 + c * 4, ut[c * 2 + s, x, :, near]) for c in range(2)]
                moves.append((96 + side * 8 + s * 4, c0))
                for at, plane in moves:
                    out = jnp.where((lane >= at) & (lane < at + 4), pltpu.roll(plane, at, 1), out)
                column = columns[:, s * GROUP + x : s * GROUP + x + 1]
                out = jnp.where(lane == 112 + side * 2 + s, column, out)
        for c in range(2):
            out = jnp.where(lane == c * GROUP + x, jnp.sum(slip[c], 1, keepdims=True), out)
            out = jnp.where(lane == 16 + c * GROUP + x, jnp.sum(ahead[c], 1, keepdims=True), out)
    out_ref[0] = out


TILE = 8


class Plane:
    def __init__(self, tiles):
        self.tiles = tiles

    @classmethod
    def load(cls, ref, *index):
        nz, ny = ref.shape[-2:]
        return cls([
            [ref[(*index, slice(i, i + TILE), slice(j, j + LANES))] for j in range(0, ny, LANES)]
            for i in range(0, nz, TILE)
        ])

    def store(self, ref, *index):
        for i, line in enumerate(self.tiles):
            for j, tile in enumerate(line):
                ref[(*index, slice(i * TILE, (i + 1) * TILE), slice(j * LANES, (j + 1) * LANES))] = tile

    def map(self, function, *others):
        return Plane([
            [function(tile, *(other.tiles[i][j] for other in others)) for j, tile in enumerate(line)]
            for i, line in enumerate(self.tiles)
        ])

    def __add__(self, other):
        return self.map(lambda a, b: a + b, other)

    def __sub__(self, other):
        return self.map(lambda a, b: a - b, other)

    def __mul__(self, other):
        if isinstance(other, Plane):
            return self.map(lambda a, b: a * b, other)
        return self.map(lambda a: a * other)

    def moved(self, axis, step, zero):
        lines = self.tiles if axis == 1 else [list(line) for line in zip(*self.tiles)]
        size = LANES if axis == 1 else TILE
        shape = lines[0][0].shape
        end = iota(shape, axis) == (size - 1 if step == 1 else 0)
        result = []
        for line in lines:
            turned = [pltpu.roll(tile, size - 1 if step == 1 else 1, axis) for tile in line]
            new = []
            for k, tile in enumerate(line):
                inside = 0 <= k + step < len(line)
                new.append(jnp.where(end, turned[k + step] if inside else (0.0 if zero else tile), turned[k]))
            result.append(new)
        return Plane(result if axis == 1 else [list(line) for line in zip(*result)])

    def beside(self, zero):
        return [self.moved(axis, step, zero) for axis in (0, 1) for step in (1, -1)]


def total(planes):
    result = planes[0]
    for one in planes[1:]:
        result = result + one
    return result


def squared(a):
    return a * a


def stencil(u, c):
    cm, c0, cp = c
    bars = [c0 + one for one in [cp, cm] + c0.beside(False)]
    forces, gradients = [], []
    for um, u0, up in u:
        near = [up, um] + u0.beside(True)
        forces.append(total([bar * (one - u0) for bar, one in zip(bars, near)]))
        gradients += [squared(near[k] - near[k + 1]) for k in range(0, 6, 2)]
    return forces, total(gradients) * 0.25


def classed(classes, table_ref):
    def entry(row, level):
        return jnp.broadcast_to(table_ref[row : row + 1, level : level + 1], classes.shape)

    rate, limit = entry(0, 0), entry(1, 0)
    for level in range(1, table_ref.shape[1]):
        here = classes == level
        rate = jnp.where(here, entry(0, level), rate)
        limit = jnp.where(here, entry(1, level), limit)
    return rate, limit


def decay(rate, limit, energy):
    over = energy - limit
    soft = jnp.maximum(over, 0.0) + jnp.log(1.0 + jnp.exp(-jnp.abs(over)))
    return jnp.exp(-rate * soft)


PK_U, PK_C, PK_V, PK_RATE, PK_LIMIT, PK_FAULT, PK_COUNT = 0, 4, 6, 10, 12, 14, 16


def strides(n):
    far = [(1 << i) | 1 for i in reversed(range(1, n.bit_length() - 1))]
    return far[-1:] + far[:-1] + [1]


def halo_kernel(u_ref, v_ref, d_ref, edges_ref, even_ref, odd_ref):
    parity = lax.rem(lax.axis_index("long"), 2)
    for ref, right in ((even_ref, 1 - parity), (odd_ref, parity)):
        edge, behind = right * (GROUP - 1), 1 + right * (GROUP - 3)
        for s in range(2):
            d0 = Plane.load(d_ref, s, edge)
            d0.store(ref, 8 + s)
            Plane.load(edges_ref, right, s).map(lambda a: a.astype(jnp.float32)).store(ref, 14 + s)
            c0, c1 = (a.map(lambda b: 1.0 - b) for a in (d0, Plane.load(d_ref, s, behind)))
            bars = [c0 + one for one in [c1] + c0.beside(False)]
            for comp in range(2):
                i = comp * 2 + s
                u0, u1 = Plane.load(u_ref, i, edge), Plane.load(u_ref, i, behind)
                u0.store(ref, i)
                u1.store(ref, 4 + i)
                force = total([bar * (one - u0) for bar, one in zip(bars, [u1] + u0.beside(True))])
                (u0 + (Plane.load(v_ref, i, edge) + force * (0.5 * DT)) * DT).store(ref, 10 + i)


def place_apart(apart, n):
    at, core = 0, apart & 1
    for i, stride in enumerate(strides(n)[:-1]):
        bit = (apart >> (stride.bit_length() - 1)) & 1
        at, core = at | (bit << i), core ^ bit
    return at | (core << (n.bit_length() - 2))


def second_step(x, u1, c1, v1, rates, limits, uo, vo, do):
    for s in range(2):
        c = [Plane.load(c1, s, x + k) for k in range(3)]
        u = [[Plane.load(u1, comp * 2 + s, x + k) for k in range(3)] for comp in range(2)]
        forces, energy = stencil(u, c)
        left = Plane.load(rates, s, x).map(decay, Plane.load(limits, s, x), energy)
        c[1].map(lambda a, b: 1.0 - a * b, left).store(do, s, x)
        for comp in range(2):
            i = comp * 2 + s
            v_new = Plane.load(v1, i, x) + forces[comp] * (0.5 * DT)
            v_new.store(vo, i, x)
            (u[comp][1] + v_new * DT).store(uo, i, x)


def inner_kernel(
    u_ref, v_ref, d_ref, rows_ref, hist_ref, mat_hbm, tab_hbm, table_hbm,
    u1, c1, v1, rates, limits, uo, vo, do, packed, mat, tab_ref, table, near, hist_out, sems,
):
    loads = Copies(sems)
    for src, dst in ((mat_hbm, mat), (tab_hbm, tab_ref), (table_hbm, table)):
        loads.start(src, dst)
    kept = hist_ref.shape[0] - 2
    loads.start(hist_ref.at[pl.ds(0, kept)], hist_out.at[pl.ds(2, kept)])
    pos = lax.axis_index("long")
    nz = u_ref.shape[2]
    lane = iota((nz, LANES), 1)
    columns = fault_columns(rows_ref)
    spread = iota((columns.shape[1], LANES), 0)
    wide = iota((columns.shape[1], LANES), 1)
    for s in range(2):
        pick = (spread == s * GROUP + wide // GROUP - 1) & (wide >= GROUP) & (wide < (GROUP + 1) * GROUP)
        rows = jnp.dot(columns, pick.astype(jnp.float32), preferred_element_type=jnp.float32)
        inside = (lane >= GROUP) & (lane < (GROUP + 1) * GROUP)
        hit = inside & (rows == (lane % GROUP).astype(jnp.float32))
        packed[PK_FAULT + s] = hit.astype(jnp.float32)
    for one in loads.made[:3]:
        one.wait()
    length = table.shape[0]
    near[...] = jnp.zeros(near.shape, jnp.float32)
    for slot in range(SLOTS):
        x = lax.rem(pos * GROUP + (length - 1 + slot), length)
        near[slot * GROUP : (slot + 1) * GROUP, :] = jnp.broadcast_to(table[pl.ds(x, 1), :], (GROUP, length))

    def stiff(s, x):
        return Plane.load(d_ref, s, x).map(lambda a: 1.0 - a)

    def first_step(x):
        for s in range(2):
            c = [stiff(s, x + k) for k in (-1, 0, 1)]
            u = [[Plane.load(u_ref, comp * 2 + s, x + k) for k in (-1, 0, 1)] for comp in range(2)]
            finish_first(s, x, c, u, Plane.load(mat, s, x), v_ref, x, tab_ref, u1, c1, v1, rates, limits)

    @pl.loop(0, (GROUP - 2) // 2)
    def _(k):
        first_step(2 * k + 1)
        first_step(2 * k + 2)

    loads.made[3].wait()

    @pl.loop(0, (GROUP - 4) // 2)
    def _(k):
        second_step(2 * k + 2, u1, c1, v1, rates, limits, uo, vo, do)
        second_step(2 * k + 3, u1, c1, v1, rates, limits, uo, vo, do)

    pack_slots(packed, u1, c1, v1, rates, limits, range(2, GROUP), True)


def pack_slots(packed, u1, c1, v1, rates, limits, slots, fresh):
    nz = u1.shape[2]
    group = iota((nz, LANES), 1) // GROUP

    def pack(plane, ref, i, first_slot):
        result = jnp.zeros((nz, LANES), jnp.float32) if fresh else packed[plane]
        for slot in slots:
            if 0 <= slot - first_slot < ref.shape[1]:
                value = ref[i, slot - first_slot, :, 0:LANES]
                result = jnp.where(group == slot, pltpu.roll(value, slot * GROUP, 1) if slot else value, result)
        packed[plane] = result

    for i in range(4):
        pack(PK_U + i, u1, i, 0)
        pack(PK_V + i, v1, i, 1)
    for s in range(2):
        pack(PK_C + s, c1, s, 0)
        pack(PK_RATE + s, rates, s, 1)
        pack(PK_LIMIT + s, limits, s, 1)


def finish_first(s, x, c, u, classes, v_now, v_at, tab_ref, u1, c1, v1, rates, limits):
    slot = x + 1
    forces, energy = stencil(u, c)
    both = classes.map(lambda a: classed(a, tab_ref))
    rate, limit = both.map(lambda a: a[0]), both.map(lambda a: a[1])
    (c[1] * rate.map(decay, limit, energy)).store(c1, s, slot)
    rate.store(rates, s, x)
    limit.store(limits, s, x)
    for comp in range(2):
        i = comp * 2 + s
        v_new = Plane.load(v_now, i, v_at) + forces[comp] * (0.5 * DT)
        v_new.store(v1, i, x)
        (u[comp][1] + v_new * DT).store(u1, i, slot)


def edge_kernel(
    u_ref, v_ref, d_ref, mat, tab_ref, even_ref, odd_ref, *refs,
):
    u1, c1, v1, rates, limits, uo, vo, do, packed = refs[9:]
    pos = lax.axis_index("long")
    even_pos = lax.rem(pos, 2) == 0

    def halo(side, plane):
        pick = even_pos == (side == 1)
        return Plane.load(even_ref, plane).map(lambda a, b: jnp.where(pick, a, b), Plane.load(odd_ref, plane))

    def of_damage(plane):
        return plane.map(lambda a: 1.0 - a)

    for side, x in ((0, 0), (1, GROUP - 1)):
        inner_x = 1 if x == 0 else x - 1
        for s in range(2):
            c = [of_damage(Plane.load(d_ref, s, inner_x)), of_damage(Plane.load(d_ref, s, x)), of_damage(halo(side, 8 + s))]
            u = [[Plane.load(u_ref, i, inner_x), Plane.load(u_ref, i, x), halo(side, i)] for i in (s, 2 + s)]
            finish_first(s, x, c, u, Plane.load(mat, s, x), v_ref, x, tab_ref, u1, c1, v1, rates, limits)
            slot = (GROUP + 1) * side
            both = halo(side, 14 + s).map(lambda a: classed(a.astype(jnp.int32), tab_ref))
            rate, limit = both.map(lambda a: a[0]), both.map(lambda a: a[1])
            gradients = []
            for comp, (_, own, other) in enumerate(u):
                i = comp * 2 + s
                near_u = [halo(side, 4 + i), own] + other.beside(True)
                gradients += [squared(near_u[k] - near_u[k + 1]) for k in range(0, 6, 2)]
                force = (c[1] + c[2]) * (own - other)
                (halo(side, 10 + i) + force * (0.5 * DT * DT)).store(u1, i, slot)
            (c[2] * rate.map(decay, limit, total(gradients) * 0.25)).store(c1, s, slot)
    for x in (0, 1, GROUP - 2, GROUP - 1):
        second_step(x, u1, c1, v1, rates, limits, uo, vo, do)

    pack_slots(packed, u1, c1, v1, rates, limits, (0, 1, GROUP, GROUP + 1), False)


def split_dot(a, b, contract):
    halves = []
    for one in (a, b):
        high = one.astype(jnp.bfloat16)
        halves.append((high, (one - high.astype(jnp.float32)).astype(jnp.bfloat16)))
    (ah, al), (bh, bl) = halves
    dims = (((1,), (contract,)), ((), ()))
    products = [
        lax.dot_general(x, y, dims, preferred_element_type=jnp.float32) for x, y in ((ah, bl), (al, bh), (ah, bh))
    ]
    return products[0] + products[1] + products[2]


def regroup(blocks):
    lane = iota(blocks[0].shape, 1) // GROUP
    for unit in (1, 4):
        digit = (lane // unit) % 4
        new = list(blocks)
        for i in range(16):
            own = (i // unit) % 4
            for other in range(4):
                shift = (other - own) * unit * GROUP
                source = blocks[i + (other - own) * unit]
                moved = source if shift == 0 else pltpu.roll(source, shift % LANES, 1)
                new[i] = moved if other == 0 else jnp.where(digit == other, moved, new[i])
        blocks = new
    return blocks


def swap_parts(a):
    n = a.shape[1]
    return jnp.where(
        iota(a.shape, 1) % GROUP < OWNED, pltpu.roll(a, n - OWNED, 1), pltpu.roll(a, OWNED, 1)
    )


def final_kernel(
    n, gathered, uo, vo, do, packed, near, table, hist_in,
    u_out, v_out, d_out, hist_out,
    spread, ut, vt, dt, hist_new, sems,
):
    out = Copies(sems)
    first, far = pl.ds(0, LANES), pl.ds(LANES, uo.shape[3] - LANES)
    for ref, dst in ((uo, u_out), (vo, v_out), (do, d_out)):
        out.start(ref.at[:, :, :, far], dst.at[:, :, :, far])
    pos = lax.axis_index("long")
    nz = gathered.shape[1]
    length = n * GROUP
    lane = iota((nz, LANES), 1)

    here = place_apart(pos, n)

    def block_of(device):
        return gathered[jnp.bitwise_xor(here, place_apart(device, n))]

    for t in range(length // LANES):
        at = slice(t * LANES, (t + 1) * LANES)
        for g, block in enumerate(regroup([block_of(t * 16 + d) for d in range(16)])):
            spread[g * nz : (g + 1) * nz, at] = block

    def group(g):
        return spread[g * nz : (g + 1) * nz, :]

    full = iota((nz, length), 1)

    def picked(plane, lanes):
        tiles = [
            jnp.take_along_axis(plane[:, t : t + LANES], lane - lane % GROUP + lanes, axis=1)
            for t in range(0, length, LANES)
        ]
        return tiles[0] if len(tiles) == 1 else jnp.concatenate(tiles, 1)

    def stiff(side, s):
        return picked(group(12 + side), s * 4 + lane % 4)

    def on_edge(side, s):
        return picked(group(14), jnp.full(lane.shape, side * 2 + s)) == (full % 4).astype(jnp.float32)

    adds = []
    for s in range(2):
        next_u = pltpu.roll(group(8 + s), length - GROUP, 1)
        next_c = pltpu.roll(stiff(0, s), length - GROUP, 1)
        flux = (0.5 * (stiff(1, s) + next_c)) * (next_u - group(10 + s))
        flux = (DT * DT if s == 1 else -DT * DT) * flux
        adds.append((
            jnp.where(on_edge(1, s), flux, 0.0), jnp.where(on_edge(0, s), pltpu.roll(-flux, GROUP, 1), 0.0)
        ))
    for side, x in ((0, GROUP - 1), (1, 0)):
        total = adds[0][side] + adds[1][side]
        total += pltpu.roll(total, length - 1, 1)
        total += pltpu.roll(total, length - 2, 1)
        for c in range(2):
            moved = pltpu.roll(total, (x - c * 4) % length, 1)
            spread[(2 + c) * nz : (3 + c) * nz, :] += jnp.where(full % GROUP == x, moved, 0.0)

    both = 2 * nz
    spectra = split_dot(spread[0 : 2 * both, :], table[...], 0)
    first_now = spectra[0:both]
    hist1, hist2 = (spread[i * both : (i + 1) * both, :] for i in (2, 3))

    def factor(lag, form):
        rows = [15 * nz + k_row(lag, c, form) for c in range(2)]
        return jnp.concatenate(
            [jnp.broadcast_to(spread[row : row + 1, :], (nz, length)) for row in rows], 0
        )

    k0r, k0i, k1r, k1i = factor(0, 0), factor(0, 1), factor(1, 0), factor(1, 1)
    swapped = swap_parts(first_now)
    traction1 = hist1 + k0r * first_now + k0i * swapped
    wide = iota((both, length), 1)
    kept = jnp.where(wide == OWNED, 0.0, traction1)
    second_now = spectra[both : 2 * both] - (2.0 * DT * DT) * kept
    traction2 = hist2 + k1r * first_now + k1i * swapped + k0r * second_now + k0i * swap_parts(second_now)
    weight = jnp.where((wide // GROUP == 0) & (wide % OWNED == 0), 1.0, 2.0)
    weighted = jnp.concatenate([weight * traction1, weight * traction2], 0)
    tractions = split_dot(weighted, near[...], 1)

    u_now, v_now, c_now, faults = [], [], [], []
    for s in range(2):
        before = block_of(lax.rem(pos + n - 1, n))[:, 114 + s : 115 + s]
        after = block_of(lax.rem(pos + 1, n))[:, 112 + s : 113 + s]
        row = (lane % GROUP).astype(jnp.float32)
        fault = packed[PK_FAULT + s]
        fault = jnp.where(lane // GROUP == 0, (row == before).astype(jnp.float32), fault)
        fault = jnp.where(lane // GROUP == GROUP + 1, (row == after).astype(jnp.float32), fault)
        faults.append(fault if s == 0 else -fault)
        c_now.append(packed[PK_C + s])
    for i in range(4):
        c, s = i // 2, i % 2
        push = DT * tractions[c * nz : (c + 1) * nz] * faults[s]
        v_now.append(packed[PK_V + i] + push)
        u_now.append(packed[PK_U + i] + DT * push)

    low_row = lane % GROUP == 0

    def around(a, fill):
        return (
            pltpu.roll(a, LANES - GROUP, 1), pltpu.roll(a, GROUP, 1),
            up_z(a, fill), down_z(a, fill),
            pltpu.roll(a, LANES - 1, 1), jnp.where(low_row, fill, pltpu.roll(a, 1, 1)),
        )

    results = {}
    for s in range(2):
        c0 = c_now[s]
        bars = [0.5 * (c0 + one) for one in around(c0, c0)]
        quarter = jnp.zeros((nz, LANES), jnp.float32)
        for c in range(2):
            i = c * 2 + s
            u0 = u_now[i]
            steps = [one - u0 for one in around(u0, 0.0)]
            force = bars[0] * steps[0]
            for bar, step in zip(bars[1:], steps[1:]):
                force += bar * step
            for k in range(3):
                gradient = steps[2 * k] - steps[2 * k + 1]
                quarter += gradient * gradient
            at = (2 + c) * nz
            v_new = v_now[i] + DT * (force + tractions[at : at + nz] * faults[s])
            results["v", i] = v_new
            results["u", i] = u0 + DT * v_new
        results["d", s] = 1.0 - c0 * decay(packed[PK_RATE + s], packed[PK_LIMIT + s], 0.25 * quarter)

    changed = lane < 5
    for name, count, old, ref, dst in (
        ("u", 4, uo, ut, u_out), ("v", 4, vo, vt, v_out), ("d", 2, do, dt, d_out)
    ):
        for i in range(count):
            for x in range(GROUP):
                moved = pltpu.roll(results[name, i], LANES - (x + 1) * GROUP, 1)
                ref[i, x] = jnp.where(changed, moved, old[i, x, :, 0:LANES])
        out.start(ref, dst.at[:, :, :, first])

    rows = 2 * GROUP
    row = iota((rows, length), 0)
    target = pos * GROUP + ((row // 2) % 2) * OWNED + row // 4
    for step, now in ((1, first_now), (0, second_now)):
        total = jnp.zeros((rows, nz), jnp.float32)
        for c in range(2):
            pick = ((target == iota((rows, length), 1)) & (row % 2 == c)).astype(jnp.float32)
            total += lax.dot_general(
                pick, now[c * nz : (c + 1) * nz], (((1,), (1,)), ((), ())),
                precision=EXACT, preferred_element_type=jnp.float32,
            )
        hist_new[step] = total
    out.start(hist_new, hist_out.at[pl.ds(0, 2)])
    out.wait()


def per_device(n, displacement, velocity, damage, material, damage_table, fault_rows, kernel, history):
    comps, strips, cells, nz, ny = displacement.shape
    assert cells == GROUP and comps == 2 and strips == 2
    lags = kernel.shape[0]
    length = n * cells
    f32 = jnp.float32
    u = displacement.reshape(4, cells, nz, ny)
    v = velocity.reshape(4, cells, nz, ny)
    kern = jnp.transpose(kernel, (1, 2, 3, 0)).reshape(2 * GROUP, lags)
    hist = history.reshape(lags - 1, 2 * GROUP, nz)
    table = jnp.asarray(table_of(length))

    vmem = pl.BlockSpec(memory_space=pltpu.VMEM)
    hbm = pl.BlockSpec(memory_space=pltpu.HBM)
    shaped = lambda *shape: jax.ShapeDtypeStruct(shape, f32)
    scratch = lambda *lead: pltpu.VMEM((*lead, nz, ny), f32)
    near_rows = lambda *lead: pltpu.VMEM((*lead, nz, LANES), f32)
    params = pltpu.CompilerParams(vmem_limit_bytes=40 * 1024 * 1024)

    def at_rest(*arrays):
        return [pltpu.with_memory_space_constraint(a, pltpu.HBM) for a in arrays]

    sources = [fault_rows, kern, hist, u, v, damage]
    held = [pltpu.VMEM(a.shape, a.dtype) for a in sources]
    *held, edges, block = pl.pallas_call(
        functools.partial(pack_kernel, len(sources)),
        out_shape=(*held, pltpu.VMEM((2, 2, nz, ny), jnp.int32), pltpu.VMEM((1, nz, LANES), f32)),
        in_specs=[hbm] * (len(sources) + 1),
        out_specs=[vmem] * (len(sources) + 2),
        scratch_shapes=[pltpu.SemaphoreType.DMA((len(sources) + 2,))],
        compiler_params=params,
    )(*at_rest(*sources, material))
    fault_rows, kern, hist, u, v, damage = held

    def exchange(a, stride):
        return lax.ppermute(a, "long", [(i, i ^ stride) for i in range(n)])

    steps = strides(n)
    gathered = jnp.concatenate([block, exchange(block, steps[0])], 0)

    halo = pltpu.VMEM((HALO_PLANES, nz, ny), f32)
    even, odd = pl.pallas_call(
        halo_kernel,
        out_shape=(halo, halo),
        in_specs=[vmem] * 4,
        out_specs=[vmem] * 2,
        compiler_params=params,
        cost_estimate=pl.CostEstimate(flops=20_000_000, bytes_accessed=1_000_000, transcendentals=0),
    )(u, v, damage, edges)
    pairs = [(i, i ^ 1) for i in range(n)]
    odd = lax.ppermute(odd, "long", [((a + 1) % n, (b + 1) % n) for a, b in pairs])
    gathered, even = lax.optimization_barrier((gathered, even))
    even = lax.ppermute(even, "long", pairs)

    placed = lambda *shape: pltpu.VMEM(shape, f32)
    parts = (
        placed(4, SLOTS, nz, ny), placed(2, SLOTS, nz, ny), placed(4, cells, nz, ny),
        placed(2, cells, nz, ny), placed(2, cells, nz, ny),
        placed(4, cells, nz, ny), placed(4, cells, nz, ny), placed(2, cells, nz, ny),
        placed(PK_COUNT, nz, LANES),
    )
    *inner, material, damage_table, table, near, hist = pl.pallas_call(
        inner_kernel,
        out_shape=(
            *parts, pltpu.VMEM(material.shape, jnp.int32), placed(*damage_table.shape),
            placed(length, length), placed(LANES, length), shaped(*hist.shape),
        ),
        in_specs=[vmem] * 5 + [hbm] * 3,
        out_specs=[vmem] * 13 + [hbm],
        scratch_shapes=[pltpu.SemaphoreType.DMA((4,))],
        compiler_params=params,
        cost_estimate=pl.CostEstimate(flops=20_000_000_000, bytes_accessed=6_000_000, transcendentals=400_000),
    )(u, v, damage, fault_rows, hist, *at_rest(material, damage_table, table))
    gathered = jnp.concatenate([gathered, exchange(gathered, steps[1])], 0)
    gathered, inner = lax.optimization_barrier((gathered, inner))
    for stride in steps[2:-2]:
        gathered = jnp.concatenate([gathered, exchange(gathered, stride)], 0)
    other = exchange(gathered, steps[-2])
    *_, u_far, v_far, d_far, packed = pl.pallas_call(
        edge_kernel,
        out_shape=parts,
        in_specs=[vmem] * 16,
        out_specs=[vmem] * 9,
        input_output_aliases={7 + i: i for i in range(9)},
        compiler_params=params,
        cost_estimate=pl.CostEstimate(flops=20_000_000, bytes_accessed=6_000_000, transcendentals=400_000),
    )(u, v, damage, material, damage_table, even, odd, *inner)
    gathered, packed = lax.optimization_barrier((gathered, packed))
    gathered = jnp.concatenate([gathered, other], 0)
    gathered = jnp.concatenate([gathered, exchange(gathered, steps[-1])], 0)

    u_new, v_new, d_new, hist_new = pl.pallas_call(
        functools.partial(final_kernel, n),
        out_shape=(shaped(*u.shape), shaped(*v.shape), shaped(*damage.shape), shaped(*hist.shape)),
        in_specs=[vmem] * 7 + [hbm],
        out_specs=[hbm] * 4,
        input_output_aliases={7: 3},
        scratch_shapes=[
            pltpu.VMEM((16 * nz, length), f32),
            near_rows(4, cells), near_rows(4, cells), near_rows(2, cells),
            pltpu.VMEM((2, 2 * GROUP, nz), f32), pltpu.SemaphoreType.DMA((8,)),
        ],
        compiler_params=params,
    )(gathered, u_far, v_far, d_far, packed, near, table, hist)
    return (
        u_new.reshape(displacement.shape),
        v_new.reshape(velocity.shape),
        d_new,
        hist_new.reshape(history.shape),
    )


def solution(mesh):
    placed = (
        P("groups", None, "long", None, None),
        P("groups", None, "long", None, None),
        P("groups", "long", None, None),
        P("groups", "long", None, None),
        P(),
        P("groups", "long", None),
        P(None, "long", None, None),
        P("groups", "long", None, None, None),
    )
    return jax.shard_map(
        functools.partial(per_device, mesh.shape["long"]),
        mesh=mesh,
        in_specs=placed,
        out_specs=(placed[0], placed[1], placed[2], placed[7]),
        check_vma=False,
    )
```

```python
import functools
import math

import jax
import jax.numpy as jnp
import numpy as np
from jax import lax
from jax.experimental import pallas as pl
from jax.experimental.pallas import tpu as pltpu
from jax.sharding import PartitionSpec as P

DT = 0.5
EXACT = lax.Precision.HIGHEST
LANES = 128
GROUP = 8
OWNED = GROUP // 2
HALO_PLANES = 16
SLOTS = GROUP + 2


def table_of(length):
    lane = np.arange(length)
    wave = (lane // GROUP) * OWNED + lane % OWNED
    imag = (lane % GROUP) // OWNED
    phase = (np.arange(length)[:, None] * wave[None]) % length * (2.0 * np.pi / length)
    table = np.where(imag[None] == 1, -np.sin(phase), np.cos(phase)) / math.sqrt(length)
    return table.astype(np.float32)


def iota(shape, axis):
    return lax.broadcasted_iota(jnp.int32, shape, axis)


def up_z(a, fill):
    n = a.shape[0]
    return jnp.where(iota(a.shape, 0) == n - 1, fill, pltpu.roll(a, n - 1, 0))


def down_z(a, fill):
    return jnp.where(iota(a.shape, 0) == 0, fill, pltpu.roll(a, 1, 0))


def up_r(a, fill):
    n = a.shape[1]
    return jnp.where(iota(a.shape, 1) == n - 1, fill, pltpu.roll(a, n - 1, 1))


def down_r(a, fill):
    return jnp.where(iota(a.shape, 1) == 0, fill, pltpu.roll(a, 1, 1))


def fault_columns(rows_ref):
    rows = rows_ref[...].astype(jnp.float32).reshape(2 * GROUP, -1)
    nz = rows.shape[1]
    eye = (iota((nz, nz), 0) == iota((nz, nz), 1)).astype(jnp.float32)
    return lax.dot_general(eye, rows, (((1,), (1,)), ((), ())), preferred_element_type=jnp.float32)


def on_fault_plane(columns, s, x):
    nz = columns.shape[0]
    column = columns[:, s * GROUP + x : s * GROUP + x + 1]
    return jnp.broadcast_to(column, (nz, LANES)) == iota((nz, LANES), 1).astype(jnp.float32)


def k_row(lag, comp, form):
    return comp * 4 + form * 2 + lag


class Copies:
    def __init__(self, sems):
        self.sems, self.made = sems, []

    def start(self, src, dst):
        one = pltpu.make_async_copy(src, dst, self.sems.at[len(self.made)])
        one.start()
        self.made.append(one)
        return one

    def wait(self):
        for one in self.made:
            one.wait()


def pack_kernel(count, *refs):
    sources, held = refs[:count], refs[count + 1 : 2 * count + 1]
    mat_hbm, edges_ref, out_ref, sems = refs[count], *refs[2 * count + 1 :]
    loads = Copies(sems)
    rows_ref, kern_ref, hist_ref, ut, vt, dt = held
    for src, dst in zip(sources, held):
        loads.start(src, dst)
    for side, x in ((0, 0), (1, GROUP - 1)):
        loads.start(mat_hbm.at[:, x], edges_ref.at[side])
    nz = ut.shape[2]
    near = slice(0, LANES)
    for one in loads.made[:3]:
        one.wait()

    kern = kern_ref[...]
    count = kern.shape[0]
    real_row = (iota(kern.shape, 0) // 2) % 2 == 0
    from_next = pltpu.roll(kern, count - 2, 0)
    a_rows = jnp.where(real_row, kern, pltpu.roll(kern, 2, 0))
    b_rows = jnp.where(real_row, -from_next, kern)
    b_source = jnp.where(real_row, from_next, -kern)
    parts = []
    lags = hist_ref.shape[0] + 1
    for skip in (1, 2):
        straight = jnp.zeros((count, nz), jnp.float32)
        crossed = jnp.zeros((count, nz), jnp.float32)
        for l in range(skip, lags):
            straight += a_rows[:, l : l + 1] * hist_ref[l - skip]
            crossed += b_source[:, l : l + 1] * hist_ref[l - skip]
        real_here = (iota((count, nz), 0) // 2) % 2 == 0
        swapped = jnp.where(real_here, pltpu.roll(crossed, count - 2, 0), pltpu.roll(crossed, 2, 0))
        parts.append(straight + swapped)
    square = (count, nz)
    coefficients = jnp.zeros(square, jnp.float32)
    for c in range(2):
        for form, rows in enumerate((a_rows, b_rows)):
            for l in (0, 1):
                here = (iota(square, 0) % 2 == c) & (iota(square, 1) == k_row(l, c, form))
                coefficients = jnp.where(here, rows[:, l : l + 1], coefficients)
    parts.append(coefficients)
    stacked = jnp.concatenate(parts, 0)
    total = stacked.shape[0]
    row = iota((total, LANES), 0)
    start = jnp.where(row < 32, 32 + (row // 16) * 16 + (row % 2) * GROUP, LANES - GROUP)
    target = start + ((row // 2) % 2) * OWNED + (row // 4) % OWNED
    place = (target == iota((total, LANES), 1)).astype(jnp.float32)
    out = lax.dot_general(
        stacked, place, (((0,), (0,)), ((), ())), precision=EXACT, preferred_element_type=jnp.float32
    )

    lane = iota((nz, LANES), 1)
    columns = fault_columns(rows_ref)
    faults = [[on_fault_plane(columns, s, x) for x in range(GROUP)] for s in range(2)]
    zero = jnp.zeros((nz, LANES), jnp.float32)
    for one in loads.made[3:]:
        one.wait()
    for x in range(GROUP):
        slip = [zero, zero]
        ahead = [zero, zero]
        for s in range(2):
            fault = faults[s][x]
            c0 = 1.0 - dt[s, x, :, near]
            bars = []
            if x > 0:
                bars.append((x - 1, 0.5 * (c0 + (1.0 - dt[s, x - 1, :, near]))))
            if x < GROUP - 1:
                bars.append((x + 1, 0.5 * (c0 + (1.0 - dt[s, x + 1, :, near]))))
            bar_zu = 0.5 * (c0 + up_z(c0, c0))
            bar_zd = 0.5 * (c0 + down_z(c0, c0))
            bar_ru = 0.5 * (c0 + up_r(c0, c0))
            bar_rd = 0.5 * (c0 + down_r(c0, c0))
            for c in range(2):
                u0 = ut[c * 2 + s, x, :, near]
                force = bar_zu * (up_z(u0, 0.0) - u0) + bar_zd * (down_z(u0, 0.0) - u0)
                force += bar_ru * (up_r(u0, 0.0) - u0) + bar_rd * (down_r(u0, 0.0) - u0)
                for other, bar in bars:
                    force += bar * (ut[c * 2 + s, other, :, near] - u0)
                later = u0 + DT * (vt[c * 2 + s, x, :, near] + DT * force)
                sign = 1.0 if s == 1 else -1.0
                slip[c] += jnp.where(fault, sign * u0, 0.0)
                ahead[c] += jnp.where(fault, sign * later, 0.0)
            if x in (0, GROUP - 1):
                side = 0 if x == 0 else 1
                moves = [(64 + side * 16 + s * 8 + c * 4, ut[c * 2 + s, x, :, near]) for c in range(2)]
                moves.append((96 + side * 8 + s * 4, c0))
                for at, plane in moves:
                    out = jnp.where((lane >= at) & (lane < at + 4), pltpu.roll(plane, at, 1), out)
                column = columns[:, s * GROUP + x : s * GROUP + x + 1]
                out = jnp.where(lane == 112 + side * 2 + s, column, out)
        for c in range(2):
            out = jnp.where(lane == c * GROUP + x, jnp.sum(slip[c], 1, keepdims=True), out)
            out = jnp.where(lane == 16 + c * GROUP + x, jnp.sum(ahead[c], 1, keepdims=True), out)
    out_ref[0] = out


TILE = 8


class Plane:
    def __init__(self, tiles):
        self.tiles = tiles

    @classmethod
    def load(cls, ref, *index):
        nz, ny = ref.shape[-2:]
        return cls([
            [ref[(*index, slice(i, i + TILE), slice(j, j + LANES))] for j in range(0, ny, LANES)]
            for i in range(0, nz, TILE)
        ])

    def store(self, ref, *index):
        for i, line in enumerate(self.tiles):
            for j, tile in enumerate(line):
                ref[(*index, slice(i * TILE, (i + 1) * TILE), slice(j * LANES, (j + 1) * LANES))] = tile

    def map(self, function, *others):
        return Plane([
            [function(tile, *(other.tiles[i][j] for other in others)) for j, tile in enumerate(line)]
            for i, line in enumerate(self.tiles)
        ])

    def __add__(self, other):
        return self.map(lambda a, b: a + b, other)

    def __sub__(self, other):
        return self.map(lambda a, b: a - b, other)

    def __mul__(self, other):
        if isinstance(other, Plane):
            return self.map(lambda a, b: a * b, other)
        return self.map(lambda a: a * other)

    def moved(self, axis, step, zero):
        lines = self.tiles if axis == 1 else [list(line) for line in zip(*self.tiles)]
        size = LANES if axis == 1 else TILE
        shape = lines[0][0].shape
        end = iota(shape, axis) == (size - 1 if step == 1 else 0)
        result = []
        for line in lines:
            turned = [pltpu.roll(tile, size - 1 if step == 1 else 1, axis) for tile in line]
            new = []
            for k, tile in enumerate(line):
                inside = 0 <= k + step < len(line)
                new.append(jnp.where(end, turned[k + step] if inside else (0.0 if zero else tile), turned[k]))
            result.append(new)
        return Plane(result if axis == 1 else [list(line) for line in zip(*result)])

    def beside(self, zero):
        return [self.moved(axis, step, zero) for axis in (0, 1) for step in (1, -1)]


def total(planes):
    result = planes[0]
    for one in planes[1:]:
        result = result + one
    return result


def squared(a):
    return a * a


def stencil(u, c):
    cm, c0, cp = c
    bars = [c0 + one for one in [cp, cm] + c0.beside(False)]
    forces, gradients = [], []
    for um, u0, up in u:
        near = [up, um] + u0.beside(True)
        forces.append(total([bar * (one - u0) for bar, one in zip(bars, near)]))
        gradients += [squared(near[k] - near[k + 1]) for k in range(0, 6, 2)]
    return forces, total(gradients) * 0.25


def classed(classes, table_ref):
    def entry(row, level):
        return jnp.broadcast_to(table_ref[row : row + 1, level : level + 1], classes.shape)

    rate, limit = entry(0, 0), entry(1, 0)
    for level in range(1, table_ref.shape[1]):
        here = classes == level
        rate = jnp.where(here, entry(0, level), rate)
        limit = jnp.where(here, entry(1, level), limit)
    return rate, limit


def decay(rate, limit, energy):
    over = energy - limit
    soft = jnp.maximum(over, 0.0) + jnp.log(1.0 + jnp.exp(-jnp.abs(over)))
    return jnp.exp(-rate * soft)


PK_U, PK_C, PK_V, PK_RATE, PK_LIMIT, PK_FAULT, PK_COUNT = 0, 4, 6, 10, 12, 14, 16


def strides(n):
    far = [(1 << i) | 1 for i in reversed(range(1, n.bit_length() - 1))]
    return far[-1:] + far[:-1] + [1]


def halo_kernel(u_ref, v_ref, d_ref, edges_ref, even_ref, odd_ref):
    parity = lax.rem(lax.axis_index("long"), 2)
    for ref, right in ((even_ref, 1 - parity), (odd_ref, parity)):
        edge, behind = right * (GROUP - 1), 1 + right * (GROUP - 3)
        for s in range(2):
            d0 = Plane.load(d_ref, s, edge)
            d0.store(ref, 8 + s)
            Plane.load(edges_ref, right, s).map(lambda a: a.astype(jnp.float32)).store(ref, 14 + s)
            c0, c1 = (a.map(lambda b: 1.0 - b) for a in (d0, Plane.load(d_ref, s, behind)))
            bars = [c0 + one for one in [c1] + c0.beside(False)]
            for comp in range(2):
                i = comp * 2 + s
                u0, u1 = Plane.load(u_ref, i, edge), Plane.load(u_ref, i, behind)
                u0.store(ref, i)
                u1.store(ref, 4 + i)
                force = total([bar * (one - u0) for bar, one in zip(bars, [u1] + u0.beside(True))])
                (u0 + (Plane.load(v_ref, i, edge) + force * (0.5 * DT)) * DT).store(ref, 10 + i)


def place_apart(apart, n):
    at, core = 0, apart & 1
    for i, stride in enumerate(strides(n)[:-1]):
        bit = (apart >> (stride.bit_length() - 1)) & 1
        at, core = at | (bit << i), core ^ bit
    return at | (core << (n.bit_length() - 2))


def second_step(x, u1, c1, v1, rates, limits, uo, vo, do):
    for s in range(2):
        c = [Plane.load(c1, s, x + k) for k in range(3)]
        u = [[Plane.load(u1, comp * 2 + s, x + k) for k in range(3)] for comp in range(2)]
        forces, energy = stencil(u, c)
        left = Plane.load(rates, s, x).map(decay, Plane.load(limits, s, x), energy)
        c[1].map(lambda a, b: 1.0 - a * b, left).store(do, s, x)
        for comp in range(2):
            i = comp * 2 + s
            v_new = Plane.load(v1, i, x) + forces[comp] * (0.5 * DT)
            v_new.store(vo, i, x)
            (u[comp][1] + v_new * DT).store(uo, i, x)


def inner_kernel(
    u_ref, v_ref, d_ref, rows_ref, hist_ref, mat_hbm, tab_hbm, table_hbm,
    u1, c1, v1, rates, limits, uo, vo, do, packed, mat, tab_ref, table, near, hist_out, sems,
):
    loads = Copies(sems)
    for src, dst in ((mat_hbm, mat), (tab_hbm, tab_ref), (table_hbm, table)):
        loads.start(src, dst)
    kept = hist_ref.shape[0] - 2
    loads.start(hist_ref.at[pl.ds(0, kept)], hist_out.at[pl.ds(2, kept)])
    pos = lax.axis_index("long")
    nz = u_ref.shape[2]
    lane = iota((nz, LANES), 1)
    columns = fault_columns(rows_ref)
    spread = iota((columns.shape[1], LANES), 0)
    wide = iota((columns.shape[1], LANES), 1)
    for s in range(2):
        pick = (spread == s * GROUP + wide // GROUP - 1) & (wide >= GROUP) & (wide < (GROUP + 1) * GROUP)
        rows = jnp.dot(columns, pick.astype(jnp.float32), preferred_element_type=jnp.float32)
        inside = (lane >= GROUP) & (lane < (GROUP + 1) * GROUP)
        hit = inside & (rows == (lane % GROUP).astype(jnp.float32))
        packed[PK_FAULT + s] = hit.astype(jnp.float32)
    for one in loads.made[:3]:
        one.wait()
    length = table.shape[0]
    near[...] = jnp.zeros(near.shape, jnp.float32)
    for slot in range(SLOTS):
        x = lax.rem(pos * GROUP + (length - 1 + slot), length)
        near[slot * GROUP : (slot + 1) * GROUP, :] = jnp.broadcast_to(table[pl.ds(x, 1), :], (GROUP, length))

    def stiff(s, x):
        return Plane.load(d_ref, s, x).map(lambda a: 1.0 - a)

    def first_step(x):
        for s in range(2):
            c = [stiff(s, x + k) for k in (-1, 0, 1)]
            u = [[Plane.load(u_ref, comp * 2 + s, x + k) for k in (-1, 0, 1)] for comp in range(2)]
            finish_first(s, x, c, u, Plane.load(mat, s, x), v_ref, x, tab_ref, u1, c1, v1, rates, limits)

    @pl.loop(0, (GROUP - 2) // 2)
    def _(k):
        first_step(2 * k + 1)
        first_step(2 * k + 2)

    loads.made[3].wait()

    @pl.loop(0, (GROUP - 4) // 2)
    def _(k):
        second_step(2 * k + 2, u1, c1, v1, rates, limits, uo, vo, do)
        second_step(2 * k + 3, u1, c1, v1, rates, limits, uo, vo, do)

    pack_slots(packed, u1, c1, v1, rates, limits, range(2, GROUP), True)


def pack_slots(packed, u1, c1, v1, rates, limits, slots, fresh):
    nz = u1.shape[2]
    group = iota((nz, LANES), 1) // GROUP

    def pack(plane, ref, i, first_slot):
        result = jnp.zeros((nz, LANES), jnp.float32) if fresh else packed[plane]
        for slot in slots:
            if 0 <= slot - first_slot < ref.shape[1]:
                value = ref[i, slot - first_slot, :, 0:LANES]
                result = jnp.where(group == slot, pltpu.roll(value, slot * GROUP, 1) if slot else value, result)
        packed[plane] = result

    for i in range(4):
        pack(PK_U + i, u1, i, 0)
        pack(PK_V + i, v1, i, 1)
    for s in range(2):
        pack(PK_C + s, c1, s, 0)
        pack(PK_RATE + s, rates, s, 1)
        pack(PK_LIMIT + s, limits, s, 1)


def finish_first(s, x, c, u, classes, v_now, v_at, tab_ref, u1, c1, v1, rates, limits):
    slot = x + 1
    forces, energy = stencil(u, c)
    both = classes.map(lambda a: classed(a, tab_ref))
    rate, limit = both.map(lambda a: a[0]), both.map(lambda a: a[1])
    (c[1] * rate.map(decay, limit, energy)).store(c1, s, slot)
    rate.store(rates, s, x)
    limit.store(limits, s, x)
    for comp in range(2):
        i = comp * 2 + s
        v_new = Plane.load(v_now, i, v_at) + forces[comp] * (0.5 * DT)
        v_new.store(v1, i, x)
        (u[comp][1] + v_new * DT).store(u1, i, slot)


def edge_kernel(
    u_ref, v_ref, d_ref, mat, tab_ref, even_ref, odd_ref, *refs,
):
    u1, c1, v1, rates, limits, uo, vo, do, packed = refs[9:]
    pos = lax.axis_index("long")
    even_pos = lax.rem(pos, 2) == 0

    def halo(side, plane):
        pick = even_pos == (side == 1)
        return Plane.load(even_ref, plane).map(lambda a, b: jnp.where(pick, a, b), Plane.load(odd_ref, plane))

    def of_damage(plane):
        return plane.map(lambda a: 1.0 - a)

    for side, x in ((0, 0), (1, GROUP - 1)):
        inner_x = 1 if x == 0 else x - 1
        for s in range(2):
            c = [of_damage(Plane.load(d_ref, s, inner_x)), of_damage(Plane.load(d_ref, s, x)), of_damage(halo(side, 8 + s))]
            u = [[Plane.load(u_ref, i, inner_x), Plane.load(u_ref, i, x), halo(side, i)] for i in (s, 2 + s)]
            finish_first(s, x, c, u, Plane.load(mat, s, x), v_ref, x, tab_ref, u1, c1, v1, rates, limits)
            slot = (GROUP + 1) * side
            both = halo(side, 14 + s).map(lambda a: classed(a.astype(jnp.int32), tab_ref))
            rate, limit = both.map(lambda a: a[0]), both.map(lambda a: a[1])
            gradients = []
            for comp, (_, own, other) in enumerate(u):
                i = comp * 2 + s
                near_u = [halo(side, 4 + i), own] + other.beside(True)
                gradients += [squared(near_u[k] - near_u[k + 1]) for k in range(0, 6, 2)]
                force = (c[1] + c[2]) * (own - other)
                (halo(side, 10 + i) + force * (0.5 * DT * DT)).store(u1, i, slot)
            (c[2] * rate.map(decay, limit, total(gradients) * 0.25)).store(c1, s, slot)
    for x in (0, 1, GROUP - 2, GROUP - 1):
        second_step(x, u1, c1, v1, rates, limits, uo, vo, do)

    pack_slots(packed, u1, c1, v1, rates, limits, (0, 1, GROUP, GROUP + 1), False)


def far_kernel(uo, vo, do, u_out, v_out, d_out, sems):
    far = pl.ds(LANES, uo.shape[3] - LANES)
    out = Copies(sems)
    for ref, dst in ((uo, u_out), (vo, v_out), (do, d_out)):
        out.start(ref.at[:, :, :, far], dst.at[:, :, :, far])
    out.wait()


def split_dot(a, b, contract):
    halves = []
    for one in (a, b):
        high = one.astype(jnp.bfloat16)
        halves.append((high, (one - high.astype(jnp.float32)).astype(jnp.bfloat16)))
    (ah, al), (bh, bl) = halves
    dims = (((1,), (contract,)), ((), ()))
    rows = a.shape[0]
    upper = lax.dot_general(jnp.concatenate([ah, al], 0), bh, dims, preferred_element_type=jnp.float32)
    lower = lax.dot_general(ah, bl, dims, preferred_element_type=jnp.float32)
    return upper[:rows] + (upper[rows:] + lower)


def regroup(blocks):
    lane = iota(blocks[0].shape, 1) // GROUP
    for unit in (1, 4):
        digit = (lane // unit) % 4
        new = list(blocks)
        for i in range(16):
            own = (i // unit) % 4
            for other in range(4):
                shift = (other - own) * unit * GROUP
                source = blocks[i + (other - own) * unit]
                moved = source if shift == 0 else pltpu.roll(source, shift % LANES, 1)
                new[i] = moved if other == 0 else jnp.where(digit == other, moved, new[i])
        blocks = new
    return blocks


def swap_parts(a):
    n = a.shape[1]
    return jnp.where(
        iota(a.shape, 1) % GROUP < OWNED, pltpu.roll(a, n - OWNED, 1), pltpu.roll(a, OWNED, 1)
    )


def final_kernel(
    n, gathered, uo, vo, do, packed, near, table, u_in, v_in, d_in, hist_in,
    u_out, v_out, d_out, hist_out,
    spread, ut, vt, dt, hist_new, sems,
):
    out = Copies(sems)
    first = pl.ds(0, LANES)
    pos = lax.axis_index("long")
    nz = gathered.shape[1]
    length = n * GROUP
    lane = iota((nz, LANES), 1)

    here = place_apart(pos, n)

    def block_of(device):
        return gathered[jnp.bitwise_xor(here, place_apart(device, n))]

    for t in range(length // LANES):
        at = slice(t * LANES, (t + 1) * LANES)
        for g, block in enumerate(regroup([block_of(t * 16 + d) for d in range(16)])):
            spread[g * nz : (g + 1) * nz, at] = block

    def group(g):
        return spread[g * nz : (g + 1) * nz, :]

    full = iota((nz, length), 1)

    def picked(plane, lanes):
        tiles = [
            jnp.take_along_axis(plane[:, t : t + LANES], lane - lane % GROUP + lanes, axis=1)
            for t in range(0, length, LANES)
        ]
        return tiles[0] if len(tiles) == 1 else jnp.concatenate(tiles, 1)

    def stiff(side, s):
        return picked(group(12 + side), s * 4 + lane % 4)

    def on_edge(side, s):
        return picked(group(14), jnp.full(lane.shape, side * 2 + s)) == (full % 4).astype(jnp.float32)

    adds = []
    for s in range(2):
        next_u = pltpu.roll(group(8 + s), length - GROUP, 1)
        next_c = pltpu.roll(stiff(0, s), length - GROUP, 1)
        flux = (0.5 * (stiff(1, s) + next_c)) * (next_u - group(10 + s))
        flux = (DT * DT if s == 1 else -DT * DT) * flux
        adds.append((
            jnp.where(on_edge(1, s), flux, 0.0), jnp.where(on_edge(0, s), pltpu.roll(-flux, GROUP, 1), 0.0)
        ))
    for side, x in ((0, GROUP - 1), (1, 0)):
        total = adds[0][side] + adds[1][side]
        total += pltpu.roll(total, length - 1, 1)
        total += pltpu.roll(total, length - 2, 1)
        for c in range(2):
            moved = pltpu.roll(total, (x - c * 4) % length, 1)
            spread[(2 + c) * nz : (3 + c) * nz, :] += jnp.where(full % GROUP == x, moved, 0.0)

    both = 2 * nz
    spectra = split_dot(spread[0 : 2 * both, :], table[...], 0)
    first_now = spectra[0:both]
    hist1, hist2 = (spread[i * both : (i + 1) * both, :] for i in (2, 3))

    def factor(lag, form):
        rows = [15 * nz + k_row(lag, c, form) for c in range(2)]
        return jnp.concatenate(
            [jnp.broadcast_to(spread[row : row + 1, :], (nz, length)) for row in rows], 0
        )

    k0r, k0i, k1r, k1i = factor(0, 0), factor(0, 1), factor(1, 0), factor(1, 1)
    swapped = swap_parts(first_now)
    traction1 = hist1 + k0r * first_now + k0i * swapped
    wide = iota((both, length), 1)
    kept = jnp.where(wide == OWNED, 0.0, traction1)
    second_now = spectra[both : 2 * both] - (2.0 * DT * DT) * kept
    traction2 = hist2 + k1r * first_now + k1i * swapped + k0r * second_now + k0i * swap_parts(second_now)
    weight = jnp.where((wide // GROUP == 0) & (wide % OWNED == 0), 1.0, 2.0)
    weighted = jnp.concatenate([weight * traction1, weight * traction2], 0)
    tractions = split_dot(weighted, near[...], 1)

    u_now, v_now, c_now, faults = [], [], [], []
    for s in range(2):
        before = block_of(lax.rem(pos + n - 1, n))[:, 114 + s : 115 + s]
        after = block_of(lax.rem(pos + 1, n))[:, 112 + s : 113 + s]
        row = (lane % GROUP).astype(jnp.float32)
        fault = packed[PK_FAULT + s]
        fault = jnp.where(lane // GROUP == 0, (row == before).astype(jnp.float32), fault)
        fault = jnp.where(lane // GROUP == GROUP + 1, (row == after).astype(jnp.float32), fault)
        faults.append(fault if s == 0 else -fault)
        c_now.append(packed[PK_C + s])
    for i in range(4):
        c, s = i // 2, i % 2
        push = DT * tractions[c * nz : (c + 1) * nz] * faults[s]
        v_now.append(packed[PK_V + i] + push)
        u_now.append(packed[PK_U + i] + DT * push)

    low_row = lane % GROUP == 0

    def around(a, fill):
        return (
            pltpu.roll(a, LANES - GROUP, 1), pltpu.roll(a, GROUP, 1),
            up_z(a, fill), down_z(a, fill),
            pltpu.roll(a, LANES - 1, 1), jnp.where(low_row, fill, pltpu.roll(a, 1, 1)),
        )

    results = {}
    for s in range(2):
        c0 = c_now[s]
        bars = [0.5 * (c0 + one) for one in around(c0, c0)]
        quarter = jnp.zeros((nz, LANES), jnp.float32)
        for c in range(2):
            i = c * 2 + s
            u0 = u_now[i]
            steps = [one - u0 for one in around(u0, 0.0)]
            force = bars[0] * steps[0]
            for bar, step in zip(bars[1:], steps[1:]):
                force += bar * step
            for k in range(3):
                gradient = steps[2 * k] - steps[2 * k + 1]
                quarter += gradient * gradient
            at = (2 + c) * nz
            v_new = v_now[i] + DT * (force + tractions[at : at + nz] * faults[s])
            results["v", i] = v_new
            results["u", i] = u0 + DT * v_new
        results["d", s] = 1.0 - c0 * decay(packed[PK_RATE + s], packed[PK_LIMIT + s], 0.25 * quarter)

    changed = lane < 5
    for name, count, old, ref, dst in (
        ("u", 4, uo, ut, u_out), ("v", 4, vo, vt, v_out), ("d", 2, do, dt, d_out)
    ):
        for i in range(count):
            for x in range(GROUP):
                moved = pltpu.roll(results[name, i], LANES - (x + 1) * GROUP, 1)
                ref[i, x] = jnp.where(changed, moved, old[i, x, :, 0:LANES])
        out.start(ref, dst.at[:, :, :, first])

    rows = 2 * GROUP
    row = iota((rows, length), 0)
    target = pos * GROUP + ((row // 2) % 2) * OWNED + row // 4
    for step, now in ((1, first_now), (0, second_now)):
        total = jnp.zeros((rows, nz), jnp.float32)
        for c in range(2):
            pick = ((target == iota((rows, length), 1)) & (row % 2 == c)).astype(jnp.float32)
            total += lax.dot_general(
                pick, now[c * nz : (c + 1) * nz], (((1,), (1,)), ((), ())),
                precision=EXACT, preferred_element_type=jnp.float32,
            )
        hist_new[step] = total
    out.start(hist_new, hist_out.at[pl.ds(0, 2)])
    out.wait()


def per_device(n, displacement, velocity, damage, material, damage_table, fault_rows, kernel, history):
    comps, strips, cells, nz, ny = displacement.shape
    assert cells == GROUP and comps == 2 and strips == 2
    lags = kernel.shape[0]
    length = n * cells
    f32 = jnp.float32
    u = displacement.reshape(4, cells, nz, ny)
    v = velocity.reshape(4, cells, nz, ny)
    kern = jnp.transpose(kernel, (1, 2, 3, 0)).reshape(2 * GROUP, lags)
    hist = history.reshape(lags - 1, 2 * GROUP, nz)
    table = jnp.asarray(table_of(length))

    vmem = pl.BlockSpec(memory_space=pltpu.VMEM)
    hbm = pl.BlockSpec(memory_space=pltpu.HBM)
    shaped = lambda *shape: jax.ShapeDtypeStruct(shape, f32)
    scratch = lambda *lead: pltpu.VMEM((*lead, nz, ny), f32)
    near_rows = lambda *lead: pltpu.VMEM((*lead, nz, LANES), f32)
    params = pltpu.CompilerParams(vmem_limit_bytes=40 * 1024 * 1024)

    def at_rest(*arrays):
        return [pltpu.with_memory_space_constraint(a, pltpu.HBM) for a in arrays]

    sources = [fault_rows, kern, hist, u, v, damage]
    held = [pltpu.VMEM(a.shape, a.dtype) for a in sources]
    *held, edges, block = pl.pallas_call(
        functools.partial(pack_kernel, len(sources)),
        out_shape=(*held, pltpu.VMEM((2, 2, nz, ny), jnp.int32), pltpu.VMEM((1, nz, LANES), f32)),
        in_specs=[hbm] * (len(sources) + 1),
        out_specs=[vmem] * (len(sources) + 2),
        scratch_shapes=[pltpu.SemaphoreType.DMA((len(sources) + 2,))],
        compiler_params=params,
    )(*at_rest(*sources, material))
    fault_rows, kern, hist, u, v, damage = held

    def exchange(a, stride):
        return lax.ppermute(a, "long", [(i, i ^ stride) for i in range(n)])

    steps = strides(n)
    gathered = jnp.concatenate([block, exchange(block, steps[0])], 0)

    halo = pltpu.VMEM((HALO_PLANES, nz, ny), f32)
    even, odd = pl.pallas_call(
        halo_kernel,
        out_shape=(halo, halo),
        in_specs=[vmem] * 4,
        out_specs=[vmem] * 2,
        compiler_params=params,
        cost_estimate=pl.CostEstimate(flops=20_000_000, bytes_accessed=1_000_000, transcendentals=0),
    )(u, v, damage, edges)
    pairs = [(i, i ^ 1) for i in range(n)]
    odd = lax.ppermute(odd, "long", [((a + 1) % n, (b + 1) % n) for a, b in pairs])
    gathered, even = lax.optimization_barrier((gathered, even))
    even = lax.ppermute(even, "long", pairs)

    placed = lambda *shape: pltpu.VMEM(shape, f32)
    parts = (
        placed(4, SLOTS, nz, ny), placed(2, SLOTS, nz, ny), placed(4, cells, nz, ny),
        placed(2, cells, nz, ny), placed(2, cells, nz, ny),
        placed(4, cells, nz, ny), placed(4, cells, nz, ny), placed(2, cells, nz, ny),
        placed(PK_COUNT, nz, LANES),
    )
    *inner, material, damage_table, table, near, hist = pl.pallas_call(
        inner_kernel,
        out_shape=(
            *parts, pltpu.VMEM(material.shape, jnp.int32), placed(*damage_table.shape),
            placed(length, length), placed(LANES, length), shaped(*hist.shape),
        ),
        in_specs=[vmem] * 5 + [hbm] * 3,
        out_specs=[vmem] * 13 + [hbm],
        scratch_shapes=[pltpu.SemaphoreType.DMA((4,))],
        compiler_params=params,
        cost_estimate=pl.CostEstimate(flops=20_000_000_000, bytes_accessed=6_000_000, transcendentals=400_000),
    )(u, v, damage, fault_rows, hist, *at_rest(material, damage_table, table))
    gathered = jnp.concatenate([gathered, exchange(gathered, steps[1])], 0)
    gathered, inner = lax.optimization_barrier((gathered, inner))
    for stride in steps[2:-2]:
        gathered = jnp.concatenate([gathered, exchange(gathered, stride)], 0)
    other = exchange(gathered, steps[-2])
    *_, u_far, v_far, d_far, packed = pl.pallas_call(
        edge_kernel,
        out_shape=parts,
        in_specs=[vmem] * 16,
        out_specs=[vmem] * 9,
        input_output_aliases={7 + i: i for i in range(9)},
        compiler_params=params,
        cost_estimate=pl.CostEstimate(flops=20_000_000, bytes_accessed=6_000_000, transcendentals=400_000),
    )(u, v, damage, material, damage_table, even, odd, *inner)
    gathered, packed = lax.optimization_barrier((gathered, packed))
    gathered = jnp.concatenate([gathered, other], 0)
    gathered, d_ready = lax.optimization_barrier((gathered, d_far))
    other = exchange(gathered, steps[-1])
    finals = pl.pallas_call(
        far_kernel,
        out_shape=(shaped(*u.shape), shaped(*v.shape), shaped(*damage.shape)),
        in_specs=[vmem] * 3,
        out_specs=[hbm] * 3,
        scratch_shapes=[pltpu.SemaphoreType.DMA((3,))],
        compiler_params=params,
        cost_estimate=pl.CostEstimate(flops=20_000_000, bytes_accessed=1_000_000, transcendentals=0),
    )(u_far, v_far, d_ready)
    gathered, finals = lax.optimization_barrier((gathered, finals))
    gathered = jnp.concatenate([gathered, other], 0)
    u_new, v_new, d_new, hist_new = pl.pallas_call(
        functools.partial(final_kernel, n),
        out_shape=(shaped(*u.shape), shaped(*v.shape), shaped(*damage.shape), shaped(*hist.shape)),
        in_specs=[vmem] * 7 + [hbm] * 4,
        out_specs=[hbm] * 4,
        input_output_aliases={7 + i: i for i in range(4)},
        scratch_shapes=[
            pltpu.VMEM((16 * nz, length), f32),
            near_rows(4, cells), near_rows(4, cells), near_rows(2, cells),
            pltpu.VMEM((2, 2 * GROUP, nz), f32), pltpu.SemaphoreType.DMA((8,)),
        ],
        compiler_params=params,
    )(gathered, u_far, v_far, d_far, packed, near, table, *finals, hist)
    return (
        u_new.reshape(displacement.shape),
        v_new.reshape(velocity.shape),
        d_new,
        hist_new.reshape(history.shape),
    )


def solution(mesh):
    placed = (
        P("groups", None, "long", None, None),
        P("groups", None, "long", None, None),
        P("groups", "long", None, None),
        P("groups", "long", None, None),
        P(),
        P("groups", "long", None),
        P(None, "long", None, None),
        P("groups", "long", None, None, None),
    )
    return jax.shard_map(
        functools.partial(per_device, mesh.shape["long"]),
        mesh=mesh,
        in_specs=placed,
        out_specs=(placed[0], placed[1], placed[2], placed[7]),
        check_vma=False,
    )
```

```python
import functools
import math

import jax
import jax.numpy as jnp
import numpy as np
from jax import lax
from jax.experimental import pallas as pl
from jax.experimental.pallas import tpu as pltpu
from jax.sharding import PartitionSpec as P

DT = 0.5
EXACT = lax.Precision.HIGHEST
LANES = 128
GROUP = 8
OWNED = GROUP // 2
HALO_PLANES = 16
SLOTS = GROUP + 2


def table_of(length):
    lane = np.arange(length)
    wave = (lane // GROUP) * OWNED + lane % OWNED
    imag = (lane % GROUP) // OWNED
    phase = (np.arange(length)[:, None] * wave[None]) % length * (2.0 * np.pi / length)
    table = np.where(imag[None] == 1, -np.sin(phase), np.cos(phase)) / math.sqrt(length)
    return table.astype(np.float32)


def iota(shape, axis):
    return lax.broadcasted_iota(jnp.int32, shape, axis)


def up_z(a, fill):
    n = a.shape[0]
    return jnp.where(iota(a.shape, 0) == n - 1, fill, pltpu.roll(a, n - 1, 0))


def down_z(a, fill):
    return jnp.where(iota(a.shape, 0) == 0, fill, pltpu.roll(a, 1, 0))


def up_r(a, fill):
    n = a.shape[1]
    return jnp.where(iota(a.shape, 1) == n - 1, fill, pltpu.roll(a, n - 1, 1))


def down_r(a, fill):
    return jnp.where(iota(a.shape, 1) == 0, fill, pltpu.roll(a, 1, 1))


def fault_columns(rows_ref):
    rows = rows_ref[...].astype(jnp.float32).reshape(2 * GROUP, -1)
    nz = rows.shape[1]
    eye = (iota((nz, nz), 0) == iota((nz, nz), 1)).astype(jnp.float32)
    return lax.dot_general(eye, rows, (((1,), (1,)), ((), ())), preferred_element_type=jnp.float32)


def on_fault_plane(columns, s, x):
    nz = columns.shape[0]
    column = columns[:, s * GROUP + x : s * GROUP + x + 1]
    return jnp.broadcast_to(column, (nz, LANES)) == iota((nz, LANES), 1).astype(jnp.float32)


def k_row(lag, comp, form):
    return comp * 4 + form * 2 + lag


class Copies:
    def __init__(self, sems):
        self.sems, self.made = sems, []

    def start(self, src, dst):
        one = pltpu.make_async_copy(src, dst, self.sems.at[len(self.made)])
        one.start()
        self.made.append(one)
        return one

    def wait(self):
        for one in self.made:
            one.wait()


def pack_kernel(count, *refs):
    sources, held = refs[:count], refs[count + 1 : 2 * count + 1]
    mat_hbm, edges_ref, out_ref, sems = refs[count], *refs[2 * count + 1 :]
    loads = Copies(sems)
    rows_ref, kern_ref, hist_ref, ut, vt, dt = held
    for src, dst in zip(sources, held):
        loads.start(src, dst)
    for side, x in ((0, 0), (1, GROUP - 1)):
        loads.start(mat_hbm.at[:, x], edges_ref.at[side])
    nz = ut.shape[2]
    near = slice(0, LANES)
    for one in loads.made[:3]:
        one.wait()

    kern = kern_ref[...]
    count = kern.shape[0]
    real_row = (iota(kern.shape, 0) // 2) % 2 == 0
    from_next = pltpu.roll(kern, count - 2, 0)
    a_rows = jnp.where(real_row, kern, pltpu.roll(kern, 2, 0))
    b_rows = jnp.where(real_row, -from_next, kern)
    b_source = jnp.where(real_row, from_next, -kern)
    parts = []
    lags = hist_ref.shape[0] + 1
    for skip in (1, 2):
        straight = jnp.zeros((count, nz), jnp.float32)
        crossed = jnp.zeros((count, nz), jnp.float32)
        for l in range(skip, lags):
            straight += a_rows[:, l : l + 1] * hist_ref[l - skip]
            crossed += b_source[:, l : l + 1] * hist_ref[l - skip]
        real_here = (iota((count, nz), 0) // 2) % 2 == 0
        swapped = jnp.where(real_here, pltpu.roll(crossed, count - 2, 0), pltpu.roll(crossed, 2, 0))
        parts.append(straight + swapped)
    square = (count, nz)
    coefficients = jnp.zeros(square, jnp.float32)
    for c in range(2):
        for form, rows in enumerate((a_rows, b_rows)):
            for l in (0, 1):
                here = (iota(square, 0) % 2 == c) & (iota(square, 1) == k_row(l, c, form))
                coefficients = jnp.where(here, rows[:, l : l + 1], coefficients)
    parts.append(coefficients)
    stacked = jnp.concatenate(parts, 0)
    total = stacked.shape[0]
    row = iota((total, LANES), 0)
    start = jnp.where(row < 32, 32 + (row // 16) * 16 + (row % 2) * GROUP, LANES - GROUP)
    target = start + ((row // 2) % 2) * OWNED + (row // 4) % OWNED
    place = (target == iota((total, LANES), 1)).astype(jnp.float32)
    out = lax.dot_general(
        stacked, place, (((0,), (0,)), ((), ())), precision=EXACT, preferred_element_type=jnp.float32
    )

    lane = iota((nz, LANES), 1)
    columns = fault_columns(rows_ref)
    faults = [[on_fault_plane(columns, s, x) for x in range(GROUP)] for s in range(2)]
    zero = jnp.zeros((nz, LANES), jnp.float32)
    for one in loads.made[3:]:
        one.wait()
    for x in range(GROUP):
        slip = [zero, zero]
        ahead = [zero, zero]
        for s in range(2):
            fault = faults[s][x]
            c0 = 1.0 - dt[s, x, :, near]
            bars = []
            if x > 0:
                bars.append((x - 1, 0.5 * (c0 + (1.0 - dt[s, x - 1, :, near]))))
            if x < GROUP - 1:
                bars.append((x + 1, 0.5 * (c0 + (1.0 - dt[s, x + 1, :, near]))))
            bar_zu = 0.5 * (c0 + up_z(c0, c0))
            bar_zd = 0.5 * (c0 + down_z(c0, c0))
            bar_ru = 0.5 * (c0 + up_r(c0, c0))
            bar_rd = 0.5 * (c0 + down_r(c0, c0))
            for c in range(2):
                u0 = ut[c * 2 + s, x, :, near]
                force = bar_zu * (up_z(u0, 0.0) - u0) + bar_zd * (down_z(u0, 0.0) - u0)
                force += bar_ru * (up_r(u0, 0.0) - u0) + bar_rd * (down_r(u0, 0.0) - u0)
                for other, bar in bars:
                    force += bar * (ut[c * 2 + s, other, :, near] - u0)
                later = u0 + DT * (vt[c * 2 + s, x, :, near] + DT * force)
                sign = 1.0 if s == 1 else -1.0
                slip[c] += jnp.where(fault, sign * u0, 0.0)
                ahead[c] += jnp.where(fault, sign * later, 0.0)
            if x in (0, GROUP - 1):
                side = 0 if x == 0 else 1
                moves = [(64 + side * 16 + s * 8 + c * 4, ut[c * 2 + s, x, :, near]) for c in range(2)]
                moves.append((96 + side * 8 + s * 4, c0))
                for at, plane in moves:
                    out = jnp.where((lane >= at) & (lane < at + 4), pltpu.roll(plane, at, 1), out)
                column = columns[:, s * GROUP + x : s * GROUP + x + 1]
                out = jnp.where(lane == 112 + side * 2 + s, column, out)
        for c in range(2):
            out = jnp.where(lane == c * GROUP + x, jnp.sum(slip[c], 1, keepdims=True), out)
            out = jnp.where(lane == 16 + c * GROUP + x, jnp.sum(ahead[c], 1, keepdims=True), out)
    out_ref[0] = out


TILE = 8


class Plane:
    def __init__(self, tiles):
        self.tiles = tiles

    @classmethod
    def load(cls, ref, *index):
        nz, ny = ref.shape[-2:]
        return cls([
            [ref[(*index, slice(i, i + TILE), slice(j, j + LANES))] for j in range(0, ny, LANES)]
            for i in range(0, nz, TILE)
        ])

    def store(self, ref, *index):
        for i, line in enumerate(self.tiles):
            for j, tile in enumerate(line):
                ref[(*index, slice(i * TILE, (i + 1) * TILE), slice(j * LANES, (j + 1) * LANES))] = tile

    def map(self, function, *others):
        return Plane([
            [function(tile, *(other.tiles[i][j] for other in others)) for j, tile in enumerate(line)]
            for i, line in enumerate(self.tiles)
        ])

    def __add__(self, other):
        return self.map(lambda a, b: a + b, other)

    def __sub__(self, other):
        return self.map(lambda a, b: a - b, other)

    def __mul__(self, other):
        if isinstance(other, Plane):
            return self.map(lambda a, b: a * b, other)
        return self.map(lambda a: a * other)

    def moved(self, axis, step, zero):
        lines = self.tiles if axis == 1 else [list(line) for line in zip(*self.tiles)]
        size = LANES if axis == 1 else TILE
        shape = lines[0][0].shape
        end = iota(shape, axis) == (size - 1 if step == 1 else 0)
        result = []
        for line in lines:
            turned = [pltpu.roll(tile, size - 1 if step == 1 else 1, axis) for tile in line]
            new = []
            for k, tile in enumerate(line):
                inside = 0 <= k + step < len(line)
                new.append(jnp.where(end, turned[k + step] if inside else (0.0 if zero else tile), turned[k]))
            result.append(new)
        return Plane(result if axis == 1 else [list(line) for line in zip(*result)])

    def beside(self, zero):
        return [self.moved(axis, step, zero) for axis in (0, 1) for step in (1, -1)]


def total(planes):
    result = planes[0]
    for one in planes[1:]:
        result = result + one
    return result


def squared(a):
    return a * a


def stencil(u, c):
    cm, c0, cp = c
    bars = [c0 + one for one in [cp, cm] + c0.beside(False)]
    forces, gradients = [], []
    for um, u0, up in u:
        near = [up, um] + u0.beside(True)
        forces.append(total([bar * (one - u0) for bar, one in zip(bars, near)]))
        gradients += [squared(near[k] - near[k + 1]) for k in range(0, 6, 2)]
    return forces, total(gradients) * 0.25


def classed(classes, table_ref):
    def entry(row, level):
        return jnp.broadcast_to(table_ref[row : row + 1, level : level + 1], classes.shape)

    rate, limit = entry(0, 0), entry(1, 0)
    for level in range(1, table_ref.shape[1]):
        here = classes == level
        rate = jnp.where(here, entry(0, level), rate)
        limit = jnp.where(here, entry(1, level), limit)
    return rate, limit


def decay(rate, limit, energy):
    over = energy - limit
    soft = jnp.maximum(over, 0.0) + jnp.log(1.0 + jnp.exp(-jnp.abs(over)))
    return jnp.exp(-rate * soft)


PK_U, PK_C, PK_V, PK_RATE, PK_LIMIT, PK_FAULT, PK_COUNT = 0, 4, 6, 10, 12, 14, 16


def strides(n):
    far = [(1 << i) | 1 for i in reversed(range(1, n.bit_length() - 1))]
    return far[-1:] + far[:-1] + [1]


def halo_kernel(u_ref, v_ref, d_ref, edges_ref, even_ref, odd_ref):
    parity = lax.rem(lax.axis_index("long"), 2)
    for ref, right in ((even_ref, 1 - parity), (odd_ref, parity)):
        edge, behind = right * (GROUP - 1), 1 + right * (GROUP - 3)
        for s in range(2):
            d0 = Plane.load(d_ref, s, edge)
            d0.store(ref, 8 + s)
            Plane.load(edges_ref, right, s).map(lambda a: a.astype(jnp.float32)).store(ref, 14 + s)
            c0, c1 = (a.map(lambda b: 1.0 - b) for a in (d0, Plane.load(d_ref, s, behind)))
            bars = [c0 + one for one in [c1] + c0.beside(False)]
            for comp in range(2):
                i = comp * 2 + s
                u0, u1 = Plane.load(u_ref, i, edge), Plane.load(u_ref, i, behind)
                u0.store(ref, i)
                u1.store(ref, 4 + i)
                force = total([bar * (one - u0) for bar, one in zip(bars, [u1] + u0.beside(True))])
                (u0 + (Plane.load(v_ref, i, edge) + force * (0.5 * DT)) * DT).store(ref, 10 + i)


def place_apart(apart, n):
    at, core = 0, apart & 1
    for i, stride in enumerate(strides(n)[:-1]):
        bit = (apart >> (stride.bit_length() - 1)) & 1
        at, core = at | (bit << i), core ^ bit
    return at | (core << (n.bit_length() - 2))


def second_step(x, u1, c1, v1, rates, limits, uo, vo, do):
    for s in range(2):
        c = [Plane.load(c1, s, x + k) for k in range(3)]
        u = [[Plane.load(u1, comp * 2 + s, x + k) for k in range(3)] for comp in range(2)]
        forces, energy = stencil(u, c)
        left = Plane.load(rates, s, x).map(decay, Plane.load(limits, s, x), energy)
        c[1].map(lambda a, b: 1.0 - a * b, left).store(do, s, x)
        for comp in range(2):
            i = comp * 2 + s
            v_new = Plane.load(v1, i, x) + forces[comp] * (0.5 * DT)
            v_new.store(vo, i, x)
            (u[comp][1] + v_new * DT).store(uo, i, x)


def inner_kernel(
    u_ref, v_ref, d_ref, rows_ref, hist_ref, mat_hbm, tab_hbm, table_hbm,
    u1, c1, v1, rates, limits, uo, vo, do, packed, mat, tab_ref, table, near, hist_out, sems,
):
    loads = Copies(sems)
    for src, dst in ((mat_hbm, mat), (tab_hbm, tab_ref), (table_hbm, table)):
        loads.start(src, dst)
    kept = hist_ref.shape[0] - 2
    loads.start(hist_ref.at[pl.ds(0, kept)], hist_out.at[pl.ds(2, kept)])
    pos = lax.axis_index("long")
    nz = u_ref.shape[2]
    lane = iota((nz, LANES), 1)
    columns = fault_columns(rows_ref)
    spread = iota((columns.shape[1], LANES), 0)
    wide = iota((columns.shape[1], LANES), 1)
    for s in range(2):
        pick = (spread == s * GROUP + wide // GROUP - 1) & (wide >= GROUP) & (wide < (GROUP + 1) * GROUP)
        rows = jnp.dot(columns, pick.astype(jnp.float32), preferred_element_type=jnp.float32)
        inside = (lane >= GROUP) & (lane < (GROUP + 1) * GROUP)
        hit = inside & (rows == (lane % GROUP).astype(jnp.float32))
        packed[PK_FAULT + s] = hit.astype(jnp.float32)
    for one in loads.made[:3]:
        one.wait()
    length = table.shape[0]
    near[...] = jnp.zeros(near.shape, jnp.float32)
    for slot in range(SLOTS):
        x = lax.rem(pos * GROUP + (length - 1 + slot), length)
        near[slot * GROUP : (slot + 1) * GROUP, :] = jnp.broadcast_to(table[pl.ds(x, 1), :], (GROUP, length))

    def stiff(s, x):
        return Plane.load(d_ref, s, x).map(lambda a: 1.0 - a)

    def first_step(x):
        for s in range(2):
            c = [stiff(s, x + k) for k in (-1, 0, 1)]
            u = [[Plane.load(u_ref, comp * 2 + s, x + k) for k in (-1, 0, 1)] for comp in range(2)]
            finish_first(s, x, c, u, Plane.load(mat, s, x), v_ref, x, tab_ref, u1, c1, v1, rates, limits)

    @pl.loop(0, (GROUP - 2) // 2)
    def _(k):
        first_step(2 * k + 1)
        first_step(2 * k + 2)

    loads.made[3].wait()

    @pl.loop(0, (GROUP - 4) // 2)
    def _(k):
        second_step(2 * k + 2, u1, c1, v1, rates, limits, uo, vo, do)
        second_step(2 * k + 3, u1, c1, v1, rates, limits, uo, vo, do)

    pack_slots(packed, u1, c1, v1, rates, limits, range(2, GROUP), True)


def pack_slots(packed, u1, c1, v1, rates, limits, slots, fresh):
    nz = u1.shape[2]
    group = iota((nz, LANES), 1) // GROUP

    def pack(plane, ref, i, first_slot):
        result = jnp.zeros((nz, LANES), jnp.float32) if fresh else packed[plane]
        for slot in slots:
            if 0 <= slot - first_slot < ref.shape[1]:
                value = ref[i, slot - first_slot, :, 0:LANES]
                result = jnp.where(group == slot, pltpu.roll(value, slot * GROUP, 1) if slot else value, result)
        packed[plane] = result

    for i in range(4):
        pack(PK_U + i, u1, i, 0)
        pack(PK_V + i, v1, i, 1)
    for s in range(2):
        pack(PK_C + s, c1, s, 0)
        pack(PK_RATE + s, rates, s, 1)
        pack(PK_LIMIT + s, limits, s, 1)


def finish_first(s, x, c, u, classes, v_now, v_at, tab_ref, u1, c1, v1, rates, limits):
    slot = x + 1
    forces, energy = stencil(u, c)
    both = classes.map(lambda a: classed(a, tab_ref))
    rate, limit = both.map(lambda a: a[0]), both.map(lambda a: a[1])
    (c[1] * rate.map(decay, limit, energy)).store(c1, s, slot)
    rate.store(rates, s, x)
    limit.store(limits, s, x)
    for comp in range(2):
        i = comp * 2 + s
        v_new = Plane.load(v_now, i, v_at) + forces[comp] * (0.5 * DT)
        v_new.store(v1, i, x)
        (u[comp][1] + v_new * DT).store(u1, i, slot)


def edge_kernel(
    u_ref, v_ref, d_ref, mat, tab_ref, even_ref, odd_ref, *refs,
):
    u1, c1, v1, rates, limits, uo, vo, do, packed = refs[9:]
    pos = lax.axis_index("long")
    even_pos = lax.rem(pos, 2) == 0

    def halo(side, plane):
        pick = even_pos == (side == 1)
        return Plane.load(even_ref, plane).map(lambda a, b: jnp.where(pick, a, b), Plane.load(odd_ref, plane))

    def of_damage(plane):
        return plane.map(lambda a: 1.0 - a)

    for side, x in ((0, 0), (1, GROUP - 1)):
        inner_x = 1 if x == 0 else x - 1
        for s in range(2):
            c = [of_damage(Plane.load(d_ref, s, inner_x)), of_damage(Plane.load(d_ref, s, x)), of_damage(halo(side, 8 + s))]
            u = [[Plane.load(u_ref, i, inner_x), Plane.load(u_ref, i, x), halo(side, i)] for i in (s, 2 + s)]
            finish_first(s, x, c, u, Plane.load(mat, s, x), v_ref, x, tab_ref, u1, c1, v1, rates, limits)
            slot = (GROUP + 1) * side
            both = halo(side, 14 + s).map(lambda a: classed(a.astype(jnp.int32), tab_ref))
            rate, limit = both.map(lambda a: a[0]), both.map(lambda a: a[1])
            gradients = []
            for comp, (_, own, other) in enumerate(u):
                i = comp * 2 + s
                near_u = [halo(side, 4 + i), own] + other.beside(True)
                gradients += [squared(near_u[k] - near_u[k + 1]) for k in range(0, 6, 2)]
                force = (c[1] + c[2]) * (own - other)
                (halo(side, 10 + i) + force * (0.5 * DT * DT)).store(u1, i, slot)
            (c[2] * rate.map(decay, limit, total(gradients) * 0.25)).store(c1, s, slot)
    for x in (0, 1, GROUP - 2, GROUP - 1):
        second_step(x, u1, c1, v1, rates, limits, uo, vo, do)

    pack_slots(packed, u1, c1, v1, rates, limits, (0, 1, GROUP, GROUP + 1), False)


def far_kernel(uo, vo, do, u_out, v_out, d_out, sems):
    far = pl.ds(LANES, uo.shape[3] - LANES)
    out = Copies(sems)
    for ref, dst in ((uo, u_out), (vo, v_out), (do, d_out)):
        out.start(ref.at[:, :, :, far], dst.at[:, :, :, far])
    out.wait()


def split(a):
    high = a.astype(jnp.bfloat16)
    return high, (a - high.astype(jnp.float32)).astype(jnp.bfloat16)


def split_dot(a, b, contract):
    ah, al = split(a)
    bh, bl = b
    dims = (((1,), (contract,)), ((), ()))
    rows = a.shape[0]
    upper = lax.dot_general(jnp.concatenate([ah, al], 0), bh, dims, preferred_element_type=jnp.float32)
    lower = lax.dot_general(ah, bl, dims, preferred_element_type=jnp.float32)
    return upper[:rows] + (upper[rows:] + lower)


def regroup(blocks):
    lane = iota(blocks[0].shape, 1) // GROUP
    for unit in (1, 4):
        digit = (lane // unit) % 4
        new = list(blocks)
        for i in range(16):
            own = (i // unit) % 4
            for other in range(4):
                shift = (other - own) * unit * GROUP
                source = blocks[i + (other - own) * unit]
                moved = source if shift == 0 else pltpu.roll(source, shift % LANES, 1)
                new[i] = moved if other == 0 else jnp.where(digit == other, moved, new[i])
        blocks = new
    return blocks


def swap_parts(a):
    n = a.shape[1]
    return jnp.where(
        iota(a.shape, 1) % GROUP < OWNED, pltpu.roll(a, n - OWNED, 1), pltpu.roll(a, OWNED, 1)
    )


def final_kernel(
    n, gathered, uo, vo, do, packed, near, table, u_in, v_in, d_in, hist_in,
    u_out, v_out, d_out, hist_out,
    spread, ut, vt, dt, hist_new, sems,
):
    out = Copies(sems)
    first = pl.ds(0, LANES)
    pos = lax.axis_index("long")
    nz = gathered.shape[1]
    length = n * GROUP
    lane = iota((nz, LANES), 1)

    here = place_apart(pos, n)

    def block_of(device):
        return gathered[jnp.bitwise_xor(here, place_apart(device, n))]

    for t in range(length // LANES):
        at = slice(t * LANES, (t + 1) * LANES)
        for g, block in enumerate(regroup([block_of(t * 16 + d) for d in range(16)])):
            spread[g * nz : (g + 1) * nz, at] = block

    both = 2 * nz
    forward, inverse = split(table[...]), split(near[...])
    first_now = split_dot(spread[0:both, :], forward, 0)
    hist1, hist2 = (spread[i * both : (i + 1) * both, :] for i in (2, 3))

    def factor(lag, form):
        rows = [15 * nz + k_row(lag, c, form) for c in range(2)]
        return jnp.concatenate(
            [jnp.broadcast_to(spread[row : row + 1, :], (nz, length)) for row in rows], 0
        )

    k0r, k0i, k1r, k1i = factor(0, 0), factor(0, 1), factor(1, 0), factor(1, 1)
    swapped = swap_parts(first_now)
    traction1 = hist1 + k0r * first_now + k0i * swapped
    wide = iota((both, length), 1)
    weight = jnp.where((wide // GROUP == 0) & (wide % OWNED == 0), 1.0, 2.0)
    pulls1 = split_dot(weight * traction1, inverse, 1)

    def group(g):
        return spread[g * nz : (g + 1) * nz, :]

    full = iota((nz, length), 1)

    def picked(plane, lanes):
        tiles = [
            jnp.take_along_axis(plane[:, t : t + LANES], lane - lane % GROUP + lanes, axis=1)
            for t in range(0, length, LANES)
        ]
        return tiles[0] if len(tiles) == 1 else jnp.concatenate(tiles, 1)

    def stiff(side, s):
        return picked(group(12 + side), s * 4 + lane % 4)

    def on_edge(side, s):
        return picked(group(14), jnp.full(lane.shape, side * 2 + s)) == (full % 4).astype(jnp.float32)

    adds = []
    for s in range(2):
        next_u = pltpu.roll(group(8 + s), length - GROUP, 1)
        next_c = pltpu.roll(stiff(0, s), length - GROUP, 1)
        flux = (0.5 * (stiff(1, s) + next_c)) * (next_u - group(10 + s))
        flux = (DT * DT if s == 1 else -DT * DT) * flux
        adds.append((
            jnp.where(on_edge(1, s), flux, 0.0), jnp.where(on_edge(0, s), pltpu.roll(-flux, GROUP, 1), 0.0)
        ))
    ahead = [spread[(2 + c) * nz : (3 + c) * nz, :] for c in range(2)]
    for side, x in ((0, GROUP - 1), (1, 0)):
        total = adds[0][side] + adds[1][side]
        total += pltpu.roll(total, length - 1, 1)
        total += pltpu.roll(total, length - 2, 1)
        for c in range(2):
            moved = pltpu.roll(total, (x - c * 4) % length, 1)
            ahead[c] += jnp.where(full % GROUP == x, moved, 0.0)

    kept = jnp.where(wide == OWNED, 0.0, traction1)
    second_now = split_dot(jnp.concatenate(ahead, 0), forward, 0) - (2.0 * DT * DT) * kept
    traction2 = hist2 + k1r * first_now + k1i * swapped + k0r * second_now + k0i * swap_parts(second_now)
    pulls2 = split_dot(weight * traction2, inverse, 1)

    u_now, v_now, c_now, faults = [], [], [], []
    for s in range(2):
        before = block_of(lax.rem(pos + n - 1, n))[:, 114 + s : 115 + s]
        after = block_of(lax.rem(pos + 1, n))[:, 112 + s : 113 + s]
        row = (lane % GROUP).astype(jnp.float32)
        fault = packed[PK_FAULT + s]
        fault = jnp.where(lane // GROUP == 0, (row == before).astype(jnp.float32), fault)
        fault = jnp.where(lane // GROUP == GROUP + 1, (row == after).astype(jnp.float32), fault)
        faults.append(fault if s == 0 else -fault)
        c_now.append(packed[PK_C + s])
    for i in range(4):
        c, s = i // 2, i % 2
        push = DT * pulls1[c * nz : (c + 1) * nz] * faults[s]
        v_now.append(packed[PK_V + i] + push)
        u_now.append(packed[PK_U + i] + DT * push)

    low_row = lane % GROUP == 0

    def around(a, fill):
        return (
            pltpu.roll(a, LANES - GROUP, 1), pltpu.roll(a, GROUP, 1),
            up_z(a, fill), down_z(a, fill),
            pltpu.roll(a, LANES - 1, 1), jnp.where(low_row, fill, pltpu.roll(a, 1, 1)),
        )

    results = {}
    for s in range(2):
        c0 = c_now[s]
        bars = [0.5 * (c0 + one) for one in around(c0, c0)]
        quarter = jnp.zeros((nz, LANES), jnp.float32)
        for c in range(2):
            i = c * 2 + s
            u0 = u_now[i]
            steps = [one - u0 for one in around(u0, 0.0)]
            force = bars[0] * steps[0]
            for bar, step in zip(bars[1:], steps[1:]):
                force += bar * step
            for k in range(3):
                gradient = steps[2 * k] - steps[2 * k + 1]
                quarter += gradient * gradient
            at = c * nz
            v_new = v_now[i] + DT * (force + pulls2[at : at + nz] * faults[s])
            results["v", i] = v_new
            results["u", i] = u0 + DT * v_new
        results["d", s] = 1.0 - c0 * decay(packed[PK_RATE + s], packed[PK_LIMIT + s], 0.25 * quarter)

    changed = lane < 5
    for name, count, old, ref, dst in (
        ("d", 2, do, dt, d_out), ("v", 4, vo, vt, v_out), ("u", 4, uo, ut, u_out)
    ):
        for i in range(count):
            for x in range(GROUP):
                moved = pltpu.roll(results[name, i], LANES - (x + 1) * GROUP, 1)
                ref[i, x] = jnp.where(changed, moved, old[i, x, :, 0:LANES])
        out.start(ref, dst.at[:, :, :, first])

    rows = 2 * GROUP
    row = iota((rows, length), 0)
    target = pos * GROUP + ((row // 2) % 2) * OWNED + row // 4
    for step, now in ((1, first_now), (0, second_now)):
        total = jnp.zeros((rows, nz), jnp.float32)
        for c in range(2):
            pick = ((target == iota((rows, length), 1)) & (row % 2 == c)).astype(jnp.float32)
            total += lax.dot_general(
                pick, now[c * nz : (c + 1) * nz], (((1,), (1,)), ((), ())),
                precision=EXACT, preferred_element_type=jnp.float32,
            )
        hist_new[step] = total
    out.start(hist_new, hist_out.at[pl.ds(0, 2)])
    out.wait()


def per_device(n, displacement, velocity, damage, material, damage_table, fault_rows, kernel, history):
    comps, strips, cells, nz, ny = displacement.shape
    assert cells == GROUP and comps == 2 and strips == 2
    lags = kernel.shape[0]
    length = n * cells
    f32 = jnp.float32
    u = displacement.reshape(4, cells, nz, ny)
    v = velocity.reshape(4, cells, nz, ny)
    kern = jnp.transpose(kernel, (1, 2, 3, 0)).reshape(2 * GROUP, lags)
    hist = history.reshape(lags - 1, 2 * GROUP, nz)
    table = jnp.asarray(table_of(length))

    vmem = pl.BlockSpec(memory_space=pltpu.VMEM)
    hbm = pl.BlockSpec(memory_space=pltpu.HBM)
    shaped = lambda *shape: jax.ShapeDtypeStruct(shape, f32)
    scratch = lambda *lead: pltpu.VMEM((*lead, nz, ny), f32)
    near_rows = lambda *lead: pltpu.VMEM((*lead, nz, LANES), f32)
    params = pltpu.CompilerParams(vmem_limit_bytes=40 * 1024 * 1024)

    def at_rest(*arrays):
        return [pltpu.with_memory_space_constraint(a, pltpu.HBM) for a in arrays]

    sources = [fault_rows, kern, hist, u, v, damage]
    held = [pltpu.VMEM(a.shape, a.dtype) for a in sources]
    *held, edges, block = pl.pallas_call(
        functools.partial(pack_kernel, len(sources)),
        out_shape=(*held, pltpu.VMEM((2, 2, nz, ny), jnp.int32), pltpu.VMEM((1, nz, LANES), f32)),
        in_specs=[hbm] * (len(sources) + 1),
        out_specs=[vmem] * (len(sources) + 2),
        scratch_shapes=[pltpu.SemaphoreType.DMA((len(sources) + 2,))],
        compiler_params=params,
    )(*at_rest(*sources, material))
    fault_rows, kern, hist, u, v, damage = held

    def exchange(a, stride):
        return lax.ppermute(a, "long", [(i, i ^ stride) for i in range(n)])

    steps = strides(n)
    gathered = jnp.concatenate([block, exchange(block, steps[0])], 0)

    halo = pltpu.VMEM((HALO_PLANES, nz, ny), f32)
    even, odd = pl.pallas_call(
        halo_kernel,
        out_shape=(halo, halo),
        in_specs=[vmem] * 4,
        out_specs=[vmem] * 2,
        compiler_params=params,
        cost_estimate=pl.CostEstimate(flops=20_000_000, bytes_accessed=1_000_000, transcendentals=0),
    )(u, v, damage, edges)
    pairs = [(i, i ^ 1) for i in range(n)]
    odd = lax.ppermute(odd, "long", [((a + 1) % n, (b + 1) % n) for a, b in pairs])
    gathered, even = lax.optimization_barrier((gathered, even))
    even = lax.ppermute(even, "long", pairs)

    placed = lambda *shape: pltpu.VMEM(shape, f32)
    parts = (
        placed(4, SLOTS, nz, ny), placed(2, SLOTS, nz, ny), placed(4, cells, nz, ny),
        placed(2, cells, nz, ny), placed(2, cells, nz, ny),
        placed(4, cells, nz, ny), placed(4, cells, nz, ny), placed(2, cells, nz, ny),
        placed(PK_COUNT, nz, LANES),
    )
    *inner, material, damage_table, table, near, hist = pl.pallas_call(
        inner_kernel,
        out_shape=(
            *parts, pltpu.VMEM(material.shape, jnp.int32), placed(*damage_table.shape),
            placed(length, length), placed(LANES, length), shaped(*hist.shape),
        ),
        in_specs=[vmem] * 5 + [hbm] * 3,
        out_specs=[vmem] * 13 + [hbm],
        scratch_shapes=[pltpu.SemaphoreType.DMA((4,))],
        compiler_params=params,
        cost_estimate=pl.CostEstimate(flops=20_000_000_000, bytes_accessed=6_000_000, transcendentals=400_000),
    )(u, v, damage, fault_rows, hist, *at_rest(material, damage_table, table))
    gathered = jnp.concatenate([gathered, exchange(gathered, steps[1])], 0)
    gathered, inner = lax.optimization_barrier((gathered, inner))
    for stride in steps[2:-2]:
        gathered = jnp.concatenate([gathered, exchange(gathered, stride)], 0)
    other = exchange(gathered, steps[-2])
    *_, u_far, v_far, d_far, packed = pl.pallas_call(
        edge_kernel,
        out_shape=parts,
        in_specs=[vmem] * 16,
        out_specs=[vmem] * 9,
        input_output_aliases={7 + i: i for i in range(9)},
        compiler_params=params,
        cost_estimate=pl.CostEstimate(flops=20_000_000, bytes_accessed=6_000_000, transcendentals=400_000),
    )(u, v, damage, material, damage_table, even, odd, *inner)
    gathered, packed = lax.optimization_barrier((gathered, packed))
    gathered = jnp.concatenate([gathered, other], 0)
    gathered, d_ready = lax.optimization_barrier((gathered, d_far))
    other = exchange(gathered, steps[-1])
    finals = pl.pallas_call(
        far_kernel,
        out_shape=(shaped(*u.shape), shaped(*v.shape), shaped(*damage.shape)),
        in_specs=[vmem] * 3,
        out_specs=[hbm] * 3,
        scratch_shapes=[pltpu.SemaphoreType.DMA((3,))],
        compiler_params=params,
        cost_estimate=pl.CostEstimate(flops=20_000_000, bytes_accessed=1_000_000, transcendentals=0),
    )(u_far, v_far, d_ready)
    gathered, finals = lax.optimization_barrier((gathered, finals))
    gathered = jnp.concatenate([gathered, other], 0)
    u_new, v_new, d_new, hist_new = pl.pallas_call(
        functools.partial(final_kernel, n),
        out_shape=(shaped(*u.shape), shaped(*v.shape), shaped(*damage.shape), shaped(*hist.shape)),
        in_specs=[vmem] * 7 + [hbm] * 4,
        out_specs=[hbm] * 4,
        input_output_aliases={7 + i: i for i in range(4)},
        scratch_shapes=[
            pltpu.VMEM((16 * nz, length), f32),
            near_rows(4, cells), near_rows(4, cells), near_rows(2, cells),
            pltpu.VMEM((2, 2 * GROUP, nz), f32), pltpu.SemaphoreType.DMA((8,)),
        ],
        compiler_params=params,
    )(gathered, u_far, v_far, d_far, packed, near, table, *finals, hist)
    return (
        u_new.reshape(displacement.shape),
        v_new.reshape(velocity.shape),
        d_new,
        hist_new.reshape(history.shape),
    )


def solution(mesh):
    placed = (
        P("groups", None, "long", None, None),
        P("groups", None, "long", None, None),
        P("groups", "long", None, None),
        P("groups", "long", None, None),
        P(),
        P("groups", "long", None),
        P(None, "long", None, None),
        P("groups", "long", None, None, None),
    )
    return jax.shard_map(
        functools.partial(per_device, mesh.shape["long"]),
        mesh=mesh,
        in_specs=placed,
        out_specs=(placed[0], placed[1], placed[2], placed[7]),
        check_vma=False,
    )
```

```python
import functools
import math

import jax
import jax.numpy as jnp
import numpy as np
from jax import lax
from jax.experimental import pallas as pl
from jax.experimental.pallas import tpu as pltpu
from jax.sharding import PartitionSpec as P

DT = 0.5
EXACT = lax.Precision.HIGHEST
LANES = 128
GROUP = 8
OWNED = GROUP // 2
HALO_PLANES = 16
SLOTS = GROUP + 2


def table_of(length):
    lane = np.arange(length)
    wave = (lane // GROUP) * OWNED + lane % OWNED
    imag = (lane % GROUP) // OWNED
    phase = (np.arange(length)[:, None] * wave[None]) % length * (2.0 * np.pi / length)
    table = np.where(imag[None] == 1, -np.sin(phase), np.cos(phase)) / math.sqrt(length)
    return table.astype(np.float32)


def iota(shape, axis):
    return lax.broadcasted_iota(jnp.int32, shape, axis)


def up_z(a, fill):
    n = a.shape[0]
    return jnp.where(iota(a.shape, 0) == n - 1, fill, pltpu.roll(a, n - 1, 0))


def down_z(a, fill):
    return jnp.where(iota(a.shape, 0) == 0, fill, pltpu.roll(a, 1, 0))


def up_r(a, fill):
    n = a.shape[1]
    return jnp.where(iota(a.shape, 1) == n - 1, fill, pltpu.roll(a, n - 1, 1))


def down_r(a, fill):
    return jnp.where(iota(a.shape, 1) == 0, fill, pltpu.roll(a, 1, 1))


def fault_columns(rows_ref):
    rows = rows_ref[...].astype(jnp.float32).reshape(2 * GROUP, -1)
    nz = rows.shape[1]
    eye = (iota((nz, nz), 0) == iota((nz, nz), 1)).astype(jnp.float32)
    return lax.dot_general(eye, rows, (((1,), (1,)), ((), ())), preferred_element_type=jnp.float32)


def on_fault_plane(columns, s, x):
    nz = columns.shape[0]
    column = columns[:, s * GROUP + x : s * GROUP + x + 1]
    return jnp.broadcast_to(column, (nz, LANES)) == iota((nz, LANES), 1).astype(jnp.float32)


def k_row(lag, comp, form):
    return comp * 4 + form * 2 + lag


class Copies:
    def __init__(self, sems):
        self.sems, self.made = sems, []

    def start(self, src, dst):
        one = pltpu.make_async_copy(src, dst, self.sems.at[len(self.made)])
        one.start()
        self.made.append(one)
        return one

    def wait(self):
        for one in self.made:
            one.wait()


def pack_kernel(count, *refs):
    sources, held = refs[:count], refs[count + 1 : 2 * count + 1]
    mat_hbm, edges_ref, out_ref, sems = refs[count], *refs[2 * count + 1 :]
    loads = Copies(sems)
    rows_ref, kern_ref, hist_ref, ut, vt, dt = held
    for src, dst in zip(sources, held):
        loads.start(src, dst)
    for side, x in ((0, 0), (1, GROUP - 1)):
        loads.start(mat_hbm.at[:, x], edges_ref.at[side])
    nz = ut.shape[2]
    near = slice(0, LANES)
    for one in loads.made[:3]:
        one.wait()

    kern = kern_ref[...]
    count = kern.shape[0]
    real_row = (iota(kern.shape, 0) // 2) % 2 == 0
    from_next = pltpu.roll(kern, count - 2, 0)
    a_rows = jnp.where(real_row, kern, pltpu.roll(kern, 2, 0))
    b_rows = jnp.where(real_row, -from_next, kern)
    b_source = jnp.where(real_row, from_next, -kern)
    parts = []
    lags = hist_ref.shape[0] + 1
    for skip in (1, 2):
        straight = jnp.zeros((count, nz), jnp.float32)
        crossed = jnp.zeros((count, nz), jnp.float32)
        for l in range(skip, lags):
            straight += a_rows[:, l : l + 1] * hist_ref[l - skip]
            crossed += b_source[:, l : l + 1] * hist_ref[l - skip]
        real_here = (iota((count, nz), 0) // 2) % 2 == 0
        swapped = jnp.where(real_here, pltpu.roll(crossed, count - 2, 0), pltpu.roll(crossed, 2, 0))
        parts.append(straight + swapped)
    square = (count, nz)
    coefficients = jnp.zeros(square, jnp.float32)
    for c in range(2):
        for form, rows in enumerate((a_rows, b_rows)):
            for l in (0, 1):
                here = (iota(square, 0) % 2 == c) & (iota(square, 1) == k_row(l, c, form))
                coefficients = jnp.where(here, rows[:, l : l + 1], coefficients)
    parts.append(coefficients)
    stacked = jnp.concatenate(parts, 0)
    total = stacked.shape[0]
    row = iota((total, LANES), 0)
    start = jnp.where(row < 32, 32 + (row // 16) * 16 + (row % 2) * GROUP, LANES - GROUP)
    target = start + ((row // 2) % 2) * OWNED + (row // 4) % OWNED
    place = (target == iota((total, LANES), 1)).astype(jnp.float32)
    out = lax.dot_general(
        stacked, place, (((0,), (0,)), ((), ())), precision=EXACT, preferred_element_type=jnp.float32
    )

    lane = iota((nz, LANES), 1)
    columns = fault_columns(rows_ref)
    faults = [[on_fault_plane(columns, s, x) for x in range(GROUP)] for s in range(2)]
    zero = jnp.zeros((nz, LANES), jnp.float32)
    for one in loads.made[3:]:
        one.wait()
    for x in range(GROUP):
        slip = [zero, zero]
        ahead = [zero, zero]
        for s in range(2):
            fault = faults[s][x]
            c0 = 1.0 - dt[s, x, :, near]
            bars = []
            if x > 0:
                bars.append((x - 1, 0.5 * (c0 + (1.0 - dt[s, x - 1, :, near]))))
            if x < GROUP - 1:
                bars.append((x + 1, 0.5 * (c0 + (1.0 - dt[s, x + 1, :, near]))))
            bar_zu = 0.5 * (c0 + up_z(c0, c0))
            bar_zd = 0.5 * (c0 + down_z(c0, c0))
            bar_ru = 0.5 * (c0 + up_r(c0, c0))
            bar_rd = 0.5 * (c0 + down_r(c0, c0))
            for c in range(2):
                u0 = ut[c * 2 + s, x, :, near]
                force = bar_zu * (up_z(u0, 0.0) - u0) + bar_zd * (down_z(u0, 0.0) - u0)
                force += bar_ru * (up_r(u0, 0.0) - u0) + bar_rd * (down_r(u0, 0.0) - u0)
                for other, bar in bars:
                    force += bar * (ut[c * 2 + s, other, :, near] - u0)
                later = u0 + DT * (vt[c * 2 + s, x, :, near] + DT * force)
                sign = 1.0 if s == 1 else -1.0
                slip[c] += jnp.where(fault, sign * u0, 0.0)
                ahead[c] += jnp.where(fault, sign * later, 0.0)
            if x in (0, GROUP - 1):
                side = 0 if x == 0 else 1
                moves = [(64 + side * 16 + s * 8 + c * 4, ut[c * 2 + s, x, :, near]) for c in range(2)]
                moves.append((96 + side * 8 + s * 4, c0))
                for at, plane in moves:
                    out = jnp.where((lane >= at) & (lane < at + 4), pltpu.roll(plane, at, 1), out)
                column = columns[:, s * GROUP + x : s * GROUP + x + 1]
                out = jnp.where(lane == 112 + side * 2 + s, column, out)
        for c in range(2):
            out = jnp.where(lane == c * GROUP + x, jnp.sum(slip[c], 1, keepdims=True), out)
            out = jnp.where(lane == 16 + c * GROUP + x, jnp.sum(ahead[c], 1, keepdims=True), out)
    out_ref[0] = out


TILE = 8


class Plane:
    def __init__(self, tiles):
        self.tiles = tiles

    @classmethod
    def load(cls, ref, *index):
        nz, ny = ref.shape[-2:]
        return cls([
            [ref[(*index, slice(i, i + TILE), slice(j, j + LANES))] for j in range(0, ny, LANES)]
            for i in range(0, nz, TILE)
        ])

    def store(self, ref, *index):
        for i, line in enumerate(self.tiles):
            for j, tile in enumerate(line):
                ref[(*index, slice(i * TILE, (i + 1) * TILE), slice(j * LANES, (j + 1) * LANES))] = tile

    def map(self, function, *others):
        return Plane([
            [function(tile, *(other.tiles[i][j] for other in others)) for j, tile in enumerate(line)]
            for i, line in enumerate(self.tiles)
        ])

    def __add__(self, other):
        return self.map(lambda a, b: a + b, other)

    def __sub__(self, other):
        return self.map(lambda a, b: a - b, other)

    def __mul__(self, other):
        if isinstance(other, Plane):
            return self.map(lambda a, b: a * b, other)
        return self.map(lambda a: a * other)

    def moved(self, axis, step, zero):
        lines = self.tiles if axis == 1 else [list(line) for line in zip(*self.tiles)]
        size = LANES if axis == 1 else TILE
        shape = lines[0][0].shape
        end = iota(shape, axis) == (size - 1 if step == 1 else 0)
        result = []
        for line in lines:
            turned = [pltpu.roll(tile, size - 1 if step == 1 else 1, axis) for tile in line]
            new = []
            for k, tile in enumerate(line):
                inside = 0 <= k + step < len(line)
                new.append(jnp.where(end, turned[k + step] if inside else (0.0 if zero else tile), turned[k]))
            result.append(new)
        return Plane(result if axis == 1 else [list(line) for line in zip(*result)])

    def beside(self, zero):
        return [self.moved(axis, step, zero) for axis in (0, 1) for step in (1, -1)]


def total(planes):
    result = planes[0]
    for one in planes[1:]:
        result = result + one
    return result


def squared(a):
    return a * a


def stencil(u, c):
    cm, c0, cp = c
    bars = [c0 + one for one in [cp, cm] + c0.beside(False)]
    forces, gradients = [], []
    for um, u0, up in u:
        near = [up, um] + u0.beside(True)
        forces.append(total([bar * (one - u0) for bar, one in zip(bars, near)]))
        gradients += [squared(near[k] - near[k + 1]) for k in range(0, 6, 2)]
    return forces, total(gradients) * 0.25


def classed(classes, table_ref):
    def entry(row, level):
        return jnp.broadcast_to(table_ref[row : row + 1, level : level + 1], classes.shape)

    rate, limit = entry(0, 0), entry(1, 0)
    for level in range(1, table_ref.shape[1]):
        here = classes == level
        rate = jnp.where(here, entry(0, level), rate)
        limit = jnp.where(here, entry(1, level), limit)
    return rate, limit


def decay(rate, limit, energy):
    over = energy - limit
    soft = jnp.maximum(over, 0.0) + jnp.log(1.0 + jnp.exp(-jnp.abs(over)))
    return jnp.exp(-rate * soft)


PK_U, PK_C, PK_V, PK_RATE, PK_LIMIT, PK_FAULT, PK_COUNT = 0, 4, 6, 10, 12, 14, 16


def strides(n):
    far = [(1 << i) | 1 for i in reversed(range(1, n.bit_length() - 1))]
    return far[-1:] + far[:-1] + [1]


def halo_kernel(u_ref, v_ref, d_ref, edges_ref, even_ref, odd_ref):
    parity = lax.rem(lax.axis_index("long"), 2)
    for ref, right in ((even_ref, 1 - parity), (odd_ref, parity)):
        edge, behind = right * (GROUP - 1), 1 + right * (GROUP - 3)
        for s in range(2):
            d0 = Plane.load(d_ref, s, edge)
            d0.store(ref, 8 + s)
            Plane.load(edges_ref, right, s).map(lambda a: a.astype(jnp.float32)).store(ref, 14 + s)
            c0, c1 = (a.map(lambda b: 1.0 - b) for a in (d0, Plane.load(d_ref, s, behind)))
            bars = [c0 + one for one in [c1] + c0.beside(False)]
            for comp in range(2):
                i = comp * 2 + s
                u0, u1 = Plane.load(u_ref, i, edge), Plane.load(u_ref, i, behind)
                u0.store(ref, i)
                u1.store(ref, 4 + i)
                force = total([bar * (one - u0) for bar, one in zip(bars, [u1] + u0.beside(True))])
                (u0 + (Plane.load(v_ref, i, edge) + force * (0.5 * DT)) * DT).store(ref, 10 + i)


def place_apart(apart, n):
    at, core = 0, apart & 1
    for i, stride in enumerate(strides(n)[:-1]):
        bit = (apart >> (stride.bit_length() - 1)) & 1
        at, core = at | (bit << i), core ^ bit
    return at | (core << (n.bit_length() - 2))


def second_step(x, u1, c1, v1, rates, limits, uo, vo, do):
    for s in range(2):
        c = [Plane.load(c1, s, x + k) for k in range(3)]
        u = [[Plane.load(u1, comp * 2 + s, x + k) for k in range(3)] for comp in range(2)]
        forces, energy = stencil(u, c)
        left = Plane.load(rates, s, x).map(decay, Plane.load(limits, s, x), energy)
        c[1].map(lambda a, b: 1.0 - a * b, left).store(do, s, x)
        for comp in range(2):
            i = comp * 2 + s
            v_new = Plane.load(v1, i, x) + forces[comp] * (0.5 * DT)
            v_new.store(vo, i, x)
            (u[comp][1] + v_new * DT).store(uo, i, x)


def inner_kernel(
    u_ref, v_ref, d_ref, rows_ref, hist_ref, mat_hbm, tab_hbm, table_hbm,
    u1, c1, v1, rates, limits, uo, vo, do, packed, mat, tab_ref, table_h, table_l, near_h, near_l, hist_out,
    table, near, sems,
):
    loads = Copies(sems)
    for src, dst in ((mat_hbm, mat), (tab_hbm, tab_ref), (table_hbm, table)):
        loads.start(src, dst)
    kept = hist_ref.shape[0] - 2
    loads.start(hist_ref.at[pl.ds(0, kept)], hist_out.at[pl.ds(2, kept)])
    pos = lax.axis_index("long")
    nz = u_ref.shape[2]
    lane = iota((nz, LANES), 1)
    columns = fault_columns(rows_ref)
    spread = iota((columns.shape[1], LANES), 0)
    wide = iota((columns.shape[1], LANES), 1)
    for s in range(2):
        pick = (spread == s * GROUP + wide // GROUP - 1) & (wide >= GROUP) & (wide < (GROUP + 1) * GROUP)
        rows = jnp.dot(columns, pick.astype(jnp.float32), preferred_element_type=jnp.float32)
        inside = (lane >= GROUP) & (lane < (GROUP + 1) * GROUP)
        hit = inside & (rows == (lane % GROUP).astype(jnp.float32))
        packed[PK_FAULT + s] = hit.astype(jnp.float32)
    for one in loads.made[:3]:
        one.wait()
    length = table.shape[0]
    near[...] = jnp.zeros(near.shape, jnp.float32)
    for slot in range(SLOTS):
        x = lax.rem(pos * GROUP + (length - 1 + slot), length)
        near[slot * GROUP : (slot + 1) * GROUP, :] = jnp.broadcast_to(table[pl.ds(x, 1), :], (GROUP, length))
    wave = iota(near.shape, 1)
    weight = jnp.where((wave // GROUP == 0) & (wave % OWNED == 0), 1.0, 2.0)
    table_h[...], table_l[...] = split(table[...])
    near_h[...], near_l[...] = split(near[...] * weight)

    def stiff(s, x):
        return Plane.load(d_ref, s, x).map(lambda a: 1.0 - a)

    def first_step(x):
        for s in range(2):
            c = [stiff(s, x + k) for k in (-1, 0, 1)]
            u = [[Plane.load(u_ref, comp * 2 + s, x + k) for k in (-1, 0, 1)] for comp in range(2)]
            finish_first(s, x, c, u, Plane.load(mat, s, x), v_ref, x, tab_ref, u1, c1, v1, rates, limits)

    @pl.loop(0, (GROUP - 2) // 2)
    def _(k):
        first_step(2 * k + 1)
        first_step(2 * k + 2)

    loads.made[3].wait()

    @pl.loop(0, (GROUP - 4) // 2)
    def _(k):
        second_step(2 * k + 2, u1, c1, v1, rates, limits, uo, vo, do)
        second_step(2 * k + 3, u1, c1, v1, rates, limits, uo, vo, do)

    pack_slots(packed, u1, c1, v1, rates, limits, range(2, GROUP), True)


def pack_slots(packed, u1, c1, v1, rates, limits, slots, fresh):
    nz = u1.shape[2]
    group = iota((nz, LANES), 1) // GROUP

    def pack(plane, ref, i, first_slot):
        result = jnp.zeros((nz, LANES), jnp.float32) if fresh else packed[plane]
        for slot in slots:
            if 0 <= slot - first_slot < ref.shape[1]:
                value = ref[i, slot - first_slot, :, 0:LANES]
                result = jnp.where(group == slot, pltpu.roll(value, slot * GROUP, 1) if slot else value, result)
        packed[plane] = result

    for i in range(4):
        pack(PK_U + i, u1, i, 0)
        pack(PK_V + i, v1, i, 1)
    for s in range(2):
        pack(PK_C + s, c1, s, 0)
        pack(PK_RATE + s, rates, s, 1)
        pack(PK_LIMIT + s, limits, s, 1)


def finish_first(s, x, c, u, classes, v_now, v_at, tab_ref, u1, c1, v1, rates, limits):
    slot = x + 1
    forces, energy = stencil(u, c)
    both = classes.map(lambda a: classed(a, tab_ref))
    rate, limit = both.map(lambda a: a[0]), both.map(lambda a: a[1])
    (c[1] * rate.map(decay, limit, energy)).store(c1, s, slot)
    rate.store(rates, s, x)
    limit.store(limits, s, x)
    for comp in range(2):
        i = comp * 2 + s
        v_new = Plane.load(v_now, i, v_at) + forces[comp] * (0.5 * DT)
        v_new.store(v1, i, x)
        (u[comp][1] + v_new * DT).store(u1, i, slot)


def edge_kernel(
    u_ref, v_ref, d_ref, mat, tab_ref, even_ref, odd_ref, *refs,
):
    u1, c1, v1, rates, limits, uo, vo, do, packed = refs[9:]
    pos = lax.axis_index("long")
    even_pos = lax.rem(pos, 2) == 0

    def halo(side, plane):
        pick = even_pos == (side == 1)
        return Plane.load(even_ref, plane).map(lambda a, b: jnp.where(pick, a, b), Plane.load(odd_ref, plane))

    def of_damage(plane):
        return plane.map(lambda a: 1.0 - a)

    for side, x in ((0, 0), (1, GROUP - 1)):
        inner_x = 1 if x == 0 else x - 1
        for s in range(2):
            c = [of_damage(Plane.load(d_ref, s, inner_x)), of_damage(Plane.load(d_ref, s, x)), of_damage(halo(side, 8 + s))]
            u = [[Plane.load(u_ref, i, inner_x), Plane.load(u_ref, i, x), halo(side, i)] for i in (s, 2 + s)]
            finish_first(s, x, c, u, Plane.load(mat, s, x), v_ref, x, tab_ref, u1, c1, v1, rates, limits)
            slot = (GROUP + 1) * side
            both = halo(side, 14 + s).map(lambda a: classed(a.astype(jnp.int32), tab_ref))
            rate, limit = both.map(lambda a: a[0]), both.map(lambda a: a[1])
            gradients = []
            for comp, (_, own, other) in enumerate(u):
                i = comp * 2 + s
                near_u = [halo(side, 4 + i), own] + other.beside(True)
                gradients += [squared(near_u[k] - near_u[k + 1]) for k in range(0, 6, 2)]
                force = (c[1] + c[2]) * (own - other)
                (halo(side, 10 + i) + force * (0.5 * DT * DT)).store(u1, i, slot)
            (c[2] * rate.map(decay, limit, total(gradients) * 0.25)).store(c1, s, slot)
    for x in (0, 1, GROUP - 2, GROUP - 1):
        second_step(x, u1, c1, v1, rates, limits, uo, vo, do)

    pack_slots(packed, u1, c1, v1, rates, limits, (0, 1, GROUP, GROUP + 1), False)


def far_kernel(uo, vo, do, u_out, v_out, d_out, sems):
    far = pl.ds(LANES, uo.shape[3] - LANES)
    out = Copies(sems)
    for ref, dst in ((uo, u_out), (vo, v_out), (do, d_out)):
        out.start(ref.at[:, :, :, far], dst.at[:, :, :, far])
    out.wait()


def split(a):
    high = a.astype(jnp.bfloat16)
    return high, (a - high.astype(jnp.float32)).astype(jnp.bfloat16)


def split_dot(a, b, contract):
    ah, al = split(a)
    bh, bl = b
    dims = (((1,), (contract,)), ((), ()))
    rows = a.shape[0]
    upper = lax.dot_general(jnp.concatenate([ah, al], 0), bh, dims, preferred_element_type=jnp.float32)
    lower = lax.dot_general(ah, bl, dims, preferred_element_type=jnp.float32)
    return upper[:rows] + (upper[rows:] + lower)


def regroup(blocks):
    lane = iota(blocks[0].shape, 1) // GROUP
    for unit in (1, 4):
        digit = (lane // unit) % 4
        new = list(blocks)
        for i in range(16):
            own = (i // unit) % 4
            for other in range(4):
                shift = (other - own) * unit * GROUP
                source = blocks[i + (other - own) * unit]
                moved = source if shift == 0 else pltpu.roll(source, shift % LANES, 1)
                new[i] = moved if other == 0 else jnp.where(digit == other, moved, new[i])
        blocks = new
    return blocks


def swap_parts(a):
    n = a.shape[1]
    return jnp.where(
        iota(a.shape, 1) % GROUP < OWNED, pltpu.roll(a, n - OWNED, 1), pltpu.roll(a, OWNED, 1)
    )


def final_kernel(
    n, gathered, uo, vo, do, packed, near_h, near_l, table_h, table_l, u_in, v_in, d_in, hist_in,
    u_out, v_out, d_out, hist_out,
    spread, ut, vt, dt, hist_new, sems,
):
    out = Copies(sems)
    first = pl.ds(0, LANES)
    pos = lax.axis_index("long")
    nz = gathered.shape[1]
    length = n * GROUP
    lane = iota((nz, LANES), 1)

    here = place_apart(pos, n)

    def block_of(device):
        return gathered[jnp.bitwise_xor(here, place_apart(device, n))]

    for t in range(length // LANES):
        at = slice(t * LANES, (t + 1) * LANES)
        for g, block in enumerate(regroup([block_of(t * 16 + d) for d in range(16)])):
            spread[g * nz : (g + 1) * nz, at] = block

    both = 2 * nz
    forward, inverse = (table_h[...], table_l[...]), (near_h[...], near_l[...])
    first_now = split_dot(spread[0:both, :], forward, 0)
    hist1, hist2 = (spread[i * both : (i + 1) * both, :] for i in (2, 3))

    def factor(lag, form):
        rows = [15 * nz + k_row(lag, c, form) for c in range(2)]
        return jnp.concatenate(
            [jnp.broadcast_to(spread[row : row + 1, :], (nz, length)) for row in rows], 0
        )

    k0r, k0i, k1r, k1i = factor(0, 0), factor(0, 1), factor(1, 0), factor(1, 1)
    swapped = swap_parts(first_now)
    traction1 = hist1 + k0r * first_now + k0i * swapped
    wide = iota((both, length), 1)
    pulls1 = split_dot(traction1, inverse, 1)

    def group(g):
        return spread[g * nz : (g + 1) * nz, :]

    full = iota((nz, length), 1)

    def picked(plane, lanes):
        tiles = [
            jnp.take_along_axis(plane[:, t : t + LANES], lane - lane % GROUP + lanes, axis=1)
            for t in range(0, length, LANES)
        ]
        return tiles[0] if len(tiles) == 1 else jnp.concatenate(tiles, 1)

    def stiff(side, s):
        return picked(group(12 + side), s * 4 + lane % 4)

    def on_edge(side, s):
        return picked(group(14), jnp.full(lane.shape, side * 2 + s)) == (full % 4).astype(jnp.float32)

    adds = []
    for s in range(2):
        next_u = pltpu.roll(group(8 + s), length - GROUP, 1)
        next_c = pltpu.roll(stiff(0, s), length - GROUP, 1)
        flux = (0.5 * (stiff(1, s) + next_c)) * (next_u - group(10 + s))
        flux = (DT * DT if s == 1 else -DT * DT) * flux
        adds.append((
            jnp.where(on_edge(1, s), flux, 0.0), jnp.where(on_edge(0, s), pltpu.roll(-flux, GROUP, 1), 0.0)
        ))
    ahead = [spread[(2 + c) * nz : (3 + c) * nz, :] for c in range(2)]
    for side, x in ((0, GROUP - 1), (1, 0)):
        total = adds[0][side] + adds[1][side]
        total += pltpu.roll(total, length - 1, 1)
        total += pltpu.roll(total, length - 2, 1)
        for c in range(2):
            moved = pltpu.roll(total, (x - c * 4) % length, 1)
            ahead[c] += jnp.where(full % GROUP == x, moved, 0.0)

    kept = jnp.where(wide == OWNED, 0.0, traction1)
    second_now = split_dot(jnp.concatenate(ahead, 0), forward, 0) - (2.0 * DT * DT) * kept
    traction2 = hist2 + k1r * first_now + k1i * swapped + k0r * second_now + k0i * swap_parts(second_now)
    pulls2 = split_dot(traction2, inverse, 1)

    u_now, v_now, c_now, faults = [], [], [], []
    for s in range(2):
        before = block_of(lax.rem(pos + n - 1, n))[:, 114 + s : 115 + s]
        after = block_of(lax.rem(pos + 1, n))[:, 112 + s : 113 + s]
        row = (lane % GROUP).astype(jnp.float32)
        fault = packed[PK_FAULT + s]
        fault = jnp.where(lane // GROUP == 0, (row == before).astype(jnp.float32), fault)
        fault = jnp.where(lane // GROUP == GROUP + 1, (row == after).astype(jnp.float32), fault)
        faults.append(fault if s == 0 else -fault)
        c_now.append(packed[PK_C + s])
    for i in range(4):
        c, s = i // 2, i % 2
        push = DT * pulls1[c * nz : (c + 1) * nz] * faults[s]
        v_now.append(packed[PK_V + i] + push)
        u_now.append(packed[PK_U + i] + DT * push)

    low_row = lane % GROUP == 0

    def around(a, fill):
        return (
            pltpu.roll(a, LANES - GROUP, 1), pltpu.roll(a, GROUP, 1),
            up_z(a, fill), down_z(a, fill),
            pltpu.roll(a, LANES - 1, 1), jnp.where(low_row, fill, pltpu.roll(a, 1, 1)),
        )

    results = {}
    for s in range(2):
        c0 = c_now[s]
        bars = [0.5 * (c0 + one) for one in around(c0, c0)]
        quarter = jnp.zeros((nz, LANES), jnp.float32)
        for c in range(2):
            i = c * 2 + s
            u0 = u_now[i]
            steps = [one - u0 for one in around(u0, 0.0)]
            force = bars[0] * steps[0]
            for bar, step in zip(bars[1:], steps[1:]):
                force += bar * step
            for k in range(3):
                gradient = steps[2 * k] - steps[2 * k + 1]
                quarter += gradient * gradient
            at = c * nz
            v_new = v_now[i] + DT * (force + pulls2[at : at + nz] * faults[s])
            results["v", i] = v_new
            results["u", i] = u0 + DT * v_new
        results["d", s] = 1.0 - c0 * decay(packed[PK_RATE + s], packed[PK_LIMIT + s], 0.25 * quarter)

    changed = lane < 5
    for name, count, old, ref, dst in (
        ("d", 2, do, dt, d_out), ("v", 4, vo, vt, v_out), ("u", 4, uo, ut, u_out)
    ):
        for i in range(count):
            for x in range(GROUP):
                moved = pltpu.roll(results[name, i], LANES - (x + 1) * GROUP, 1)
                ref[i, x] = jnp.where(changed, moved, old[i, x, :, 0:LANES])
        out.start(ref, dst.at[:, :, :, first])

    rows = 2 * GROUP
    row = iota((rows, length), 0)
    target = pos * GROUP + ((row // 2) % 2) * OWNED + row // 4
    for step, now in ((1, first_now), (0, second_now)):
        total = jnp.zeros((rows, nz), jnp.float32)
        for c in range(2):
            pick = ((target == iota((rows, length), 1)) & (row % 2 == c)).astype(jnp.float32)
            total += lax.dot_general(
                pick, now[c * nz : (c + 1) * nz], (((1,), (1,)), ((), ())),
                precision=EXACT, preferred_element_type=jnp.float32,
            )
        hist_new[step] = total
    out.start(hist_new, hist_out.at[pl.ds(0, 2)])
    out.wait()


def per_device(n, displacement, velocity, damage, material, damage_table, fault_rows, kernel, history):
    comps, strips, cells, nz, ny = displacement.shape
    assert cells == GROUP and comps == 2 and strips == 2
    lags = kernel.shape[0]
    length = n * cells
    f32 = jnp.float32
    u = displacement.reshape(4, cells, nz, ny)
    v = velocity.reshape(4, cells, nz, ny)
    kern = jnp.transpose(kernel, (1, 2, 3, 0)).reshape(2 * GROUP, lags)
    hist = history.reshape(lags - 1, 2 * GROUP, nz)
    table = jnp.asarray(table_of(length))

    vmem = pl.BlockSpec(memory_space=pltpu.VMEM)
    hbm = pl.BlockSpec(memory_space=pltpu.HBM)
    shaped = lambda *shape: jax.ShapeDtypeStruct(shape, f32)
    scratch = lambda *lead: pltpu.VMEM((*lead, nz, ny), f32)
    near_rows = lambda *lead: pltpu.VMEM((*lead, nz, LANES), f32)
    params = pltpu.CompilerParams(vmem_limit_bytes=40 * 1024 * 1024)

    def at_rest(*arrays):
        return [pltpu.with_memory_space_constraint(a, pltpu.HBM) for a in arrays]

    sources = [fault_rows, kern, hist, u, v, damage]
    held = [pltpu.VMEM(a.shape, a.dtype) for a in sources]
    *held, edges, block = pl.pallas_call(
        functools.partial(pack_kernel, len(sources)),
        out_shape=(*held, pltpu.VMEM((2, 2, nz, ny), jnp.int32), pltpu.VMEM((1, nz, LANES), f32)),
        in_specs=[hbm] * (len(sources) + 1),
        out_specs=[vmem] * (len(sources) + 2),
        scratch_shapes=[pltpu.SemaphoreType.DMA((len(sources) + 2,))],
        compiler_params=params,
    )(*at_rest(*sources, material))
    fault_rows, kern, hist, u, v, damage = held

    def exchange(a, stride):
        return lax.ppermute(a, "long", [(i, i ^ stride) for i in range(n)])

    steps = strides(n)
    gathered = jnp.concatenate([block, exchange(block, steps[0])], 0)

    halo = pltpu.VMEM((HALO_PLANES, nz, ny), f32)
    even, odd = pl.pallas_call(
        halo_kernel,
        out_shape=(halo, halo),
        in_specs=[vmem] * 4,
        out_specs=[vmem] * 2,
        compiler_params=params,
        cost_estimate=pl.CostEstimate(flops=20_000_000, bytes_accessed=1_000_000, transcendentals=0),
    )(u, v, damage, edges)
    pairs = [(i, i ^ 1) for i in range(n)]
    odd = lax.ppermute(odd, "long", [((a + 1) % n, (b + 1) % n) for a, b in pairs])
    gathered, even = lax.optimization_barrier((gathered, even))
    even = lax.ppermute(even, "long", pairs)

    placed = lambda *shape: pltpu.VMEM(shape, f32)
    parts = (
        placed(4, SLOTS, nz, ny), placed(2, SLOTS, nz, ny), placed(4, cells, nz, ny),
        placed(2, cells, nz, ny), placed(2, cells, nz, ny),
        placed(4, cells, nz, ny), placed(4, cells, nz, ny), placed(2, cells, nz, ny),
        placed(PK_COUNT, nz, LANES),
    )
    *inner, material, damage_table, table_h, table_l, near_h, near_l, hist = pl.pallas_call(
        inner_kernel,
        out_shape=(
            *parts, pltpu.VMEM(material.shape, jnp.int32), placed(*damage_table.shape),
            *[pltpu.VMEM((length, length), jnp.bfloat16)] * 2, *[pltpu.VMEM((LANES, length), jnp.bfloat16)] * 2,
            shaped(*hist.shape),
        ),
        in_specs=[vmem] * 5 + [hbm] * 3,
        out_specs=[vmem] * 15 + [hbm],
        scratch_shapes=[placed(length, length), placed(LANES, length), pltpu.SemaphoreType.DMA((4,))],
        compiler_params=params,
        cost_estimate=pl.CostEstimate(flops=20_000_000_000, bytes_accessed=6_000_000, transcendentals=400_000),
    )(u, v, damage, fault_rows, hist, *at_rest(material, damage_table, table))
    gathered = jnp.concatenate([gathered, exchange(gathered, steps[1])], 0)
    gathered, inner = lax.optimization_barrier((gathered, inner))
    for stride in steps[2:-2]:
        gathered = jnp.concatenate([gathered, exchange(gathered, stride)], 0)
    other = exchange(gathered, steps[-2])
    *_, u_far, v_far, d_far, packed = pl.pallas_call(
        edge_kernel,
        out_shape=parts,
        in_specs=[vmem] * 16,
        out_specs=[vmem] * 9,
        input_output_aliases={7 + i: i for i in range(9)},
        compiler_params=params,
        cost_estimate=pl.CostEstimate(flops=20_000_000, bytes_accessed=6_000_000, transcendentals=400_000),
    )(u, v, damage, material, damage_table, even, odd, *inner)
    gathered, packed = lax.optimization_barrier((gathered, packed))
    gathered = jnp.concatenate([gathered, other], 0)
    gathered, d_ready = lax.optimization_barrier((gathered, d_far))
    other = exchange(gathered, steps[-1])
    finals = pl.pallas_call(
        far_kernel,
        out_shape=(shaped(*u.shape), shaped(*v.shape), shaped(*damage.shape)),
        in_specs=[vmem] * 3,
        out_specs=[hbm] * 3,
        scratch_shapes=[pltpu.SemaphoreType.DMA((3,))],
        compiler_params=params,
        cost_estimate=pl.CostEstimate(flops=20_000_000, bytes_accessed=1_000_000, transcendentals=0),
    )(u_far, v_far, d_ready)
    gathered, finals = lax.optimization_barrier((gathered, finals))
    gathered = jnp.concatenate([gathered, other], 0)
    u_new, v_new, d_new, hist_new = pl.pallas_call(
        functools.partial(final_kernel, n),
        out_shape=(shaped(*u.shape), shaped(*v.shape), shaped(*damage.shape), shaped(*hist.shape)),
        in_specs=[vmem] * 9 + [hbm] * 4,
        out_specs=[hbm] * 4,
        input_output_aliases={9 + i: i for i in range(4)},
        scratch_shapes=[
            pltpu.VMEM((16 * nz, length), f32),
            near_rows(4, cells), near_rows(4, cells), near_rows(2, cells),
            pltpu.VMEM((2, 2 * GROUP, nz), f32), pltpu.SemaphoreType.DMA((8,)),
        ],
        compiler_params=params,
    )(gathered, u_far, v_far, d_far, packed, near_h, near_l, table_h, table_l, *finals, hist)
    return (
        u_new.reshape(displacement.shape),
        v_new.reshape(velocity.shape),
        d_new,
        hist_new.reshape(history.shape),
    )


def solution(mesh):
    placed = (
        P("groups", None, "long", None, None),
        P("groups", None, "long", None, None),
        P("groups", "long", None, None),
        P("groups", "long", None, None),
        P(),
        P("groups", "long", None),
        P(None, "long", None, None),
        P("groups", "long", None, None, None),
    )
    return jax.shard_map(
        functools.partial(per_device, mesh.shape["long"]),
        mesh=mesh,
        in_specs=placed,
        out_specs=(placed[0], placed[1], placed[2], placed[7]),
        check_vma=False,
    )
```
